32 devices in a mesh: quad: 4 (over z), slab: 8 (over y, x, core).
Axes of the slice: x: 2, y: 2, z: 4, core: 2. Of those that a mesh axis runs over, the one named last changes fastest.
Arguments:
- factors: bfloat16 [4, 8, 2, 512, 512], P('quad', 'slab'), may hold values from -0.1875 to 0.1875
- onsite: float32 [8, 512, 512], P('slab'), may hold values from -0.25 to 0.25, as said below
- coupling: float32 [8, 128, 128], P('slab'), may hold values from -1 to 1
- vectors: bfloat16 [8, 512, 128], P('slab'), may hold values from -1.5 to 1.5
- quad_weight: float32 [4, 2], P('quad'), may hold values from -0.6 to 0.6
Outputs:
- subspace: float32 [8, 512, 128], P('slab', 'quad')
- correlation: float32 [128, 128], replicated
- projected: float32 [128, 128], replicated
The draws below stay inside these ranges and needn't reach their ends.
Inputs may be any that keep to these rules, and one draw needn't show every extreme that they name: `onsite`: each diagonal block is symmetric, and its largest entry magnitude is exactly 8 / sqrt(1024).
All inputs are finite; a program needn't handle non-finite values.
Results may differ from the reference program's by a relative error of at most 0.0003.
Values sent between devices are 32-bit elements; how exact they have to be, the bound alone decides.
A program may use at most 64 MiB of HBM per device.

```python
import jax
import jax.numpy as jnp
from jax import lax

B = 512
M = 128
R = 128
NQ = 4
NSLABS = 8


def draw_onsite(key, part):
    normal_draw = jax.random.normal(key, (NSLABS, B, B), jnp.float32)
    clipped = jnp.clip(normal_draw, -4.0, 4.0)
    summed = clipped + jnp.swapaxes(clipped, 1, 2)
    largest = jnp.max(jnp.abs(summed), axis=(1, 2), keepdims=True)
    return summed / largest * (8.0 / jnp.sqrt(2.0 * B))


def shard_levels(rng, extent, split, least, high):
    loudness, own = 1.0, jax.random.fold_in(rng, 6)
    for axis_at, parts in split:
        steps = jnp.exp(jax.random.uniform(jax.random.fold_in(own, axis_at), (parts,), jnp.float32, least / len(split), high / len(split)))
        loudness = loudness * jnp.repeat(steps, extent[axis_at] // parts).reshape([-1 if axis == axis_at else 1 for axis in range(len(extent))])
    return loudness


def gaussian(stream_key, shape, scale, limit, cuts=(), held_as=jnp.bfloat16):
    loudness = shard_levels(stream_key, shape, cuts, -0.22, 0.18) if cuts else 1.0
    values = jax.random.normal(stream_key, shape, jnp.float32) * scale * loudness
    return jnp.minimum(jnp.maximum(values, -limit), limit).astype(held_as)


def setup_inputs(seed: int = 0) -> dict:
    keys = jax.random.split(jax.random.key(seed), 6)
    factors = gaussian(keys[0], (NQ, NSLABS, 2, B, B), (2 * B) ** -0.5, 0.1875, ((0, 4), (1, 8)))
    onsite = draw_onsite(jax.random.fold_in(keys[5], 71), 0)
    coupling = gaussian(keys[2], (NSLABS, R, R), (4 * R // 15) ** -0.5, 1.0, ((0, 8),), jnp.float32)
    vectors = gaussian(keys[3], (NSLABS, B, M), 0.25, 1.5, ((0, 8),))
    quad_weight = gaussian(keys[4], (NQ, 2), 0.1, 0.6, ((0, 4),), jnp.float32)
    return dict(factors=factors, onsite=onsite, coupling=coupling, vectors=vectors, quad_weight=quad_weight)


precise = lax.Precision.HIGHEST


def complex_times(left_cols, right_cols):
    real_part = jnp.dot(left_cols[0], right_cols[0], precision=precise, preferred_element_type=jnp.float32) - jnp.dot(left_cols[1], right_cols[1], precision=precise, preferred_element_type=jnp.float32)
    imag_part = jnp.dot(left_cols[0], right_cols[1], precision=precise, preferred_element_type=jnp.float32) + jnp.dot(left_cols[1], right_cols[0], precision=precise, preferred_element_type=jnp.float32)
    return jnp.stack([real_part, imag_part])


def real_times(real_left, right_cols):
    return jnp.stack([jnp.dot(real_left, right_cols[0], precision=precise, preferred_element_type=jnp.float32), jnp.dot(real_left, right_cols[1], precision=precise, preferred_element_type=jnp.float32)])


def reference(factors, onsite, coupling, vectors, quad_weight):
    zero_state = jnp.zeros((2, R, M), jnp.float32)

    def one_point(running, inputs):
        blocks, weight = inputs

        def forward_step(incoming, pieces):
            factor_block, vector_block, link_block = pieces
            source = jnp.dot(factor_block.reshape(2 * B, B), vector_block, preferred_element_type=jnp.float32).reshape(2, B, M)
            left_cols = factor_block[:, :, :R].astype(jnp.float32)
            solved = source + complex_times(left_cols, incoming)
            handed = real_times(link_block.T, solved[:, B - R:])
            return handed, solved

        unused, partial_rows = lax.scan(forward_step, zero_state, (blocks, vectors, coupling))

        def backward_step(incoming, pieces):
            factor_block, solved, link_block = pieces
            right_cols = factor_block[:, :, B - R:].astype(jnp.float32)
            result = solved + complex_times(right_cols, real_times(link_block, incoming))
            return result[:, :R], weight[0] * result[0] - weight[1] * result[1]

        unused, filtered = lax.scan(backward_step, zero_state, (blocks, partial_rows, coupling), reverse=True)
        return running + filtered, None

    subspace, unused = lax.scan(one_point, jnp.zeros((NSLABS, B, M), jnp.float32), (factors, quad_weight))
    diagonal_part = jnp.einsum("sbk,skm->sbm", onsite, subspace, precision=precise)
    next_planes = jnp.concatenate([subspace[1:, :R], jnp.zeros((1, R, M), jnp.float32)], axis=0)
    upper_part = jnp.einsum("sab,sbm->sam", coupling, next_planes, precision=precise)
    prev_planes = jnp.concatenate([jnp.zeros((1, R, M), jnp.float32), subspace[:-1, B - R:]], axis=0)
    prev_links = jnp.concatenate([jnp.zeros((1, R, R), jnp.float32), coupling[:-1]], axis=0)
    lower_part = jnp.einsum("sba,sbm->sam", prev_links, prev_planes, precision=precise)
    applied = jnp.concatenate([diagonal_part[:, :R] + lower_part, diagonal_part[:, R:B - R], diagonal_part[:, B - R:] + upper_part], axis=1)
    flattened = subspace.reshape(NSLABS * B, M)
    rows_all = NSLABS * B
    correlation = jnp.dot(flattened.T, flattened, precision=precise, preferred_element_type=jnp.float32) / rows_all
    projected = jnp.dot(flattened.T, applied.reshape(NSLABS * B, M), precision=precise, preferred_element_type=jnp.float32) / rows_all
    return (subspace, correlation, projected)
```

```python
import functools

import jax
import jax.numpy as jnp
from jax import lax
from jax.experimental import pallas as pl
from jax.experimental.pallas import tpu as pltpu
from jax.sharding import PartitionSpec as P

MESH = pl.DeviceIdType.MESH
f32, bf16 = jnp.float32, jnp.bfloat16


def split(x):
    high = x.astype(bf16)
    return high, (x - high.astype(f32)).astype(bf16)


def mm(a, b):
    return jnp.dot(a, b, preferred_element_type=f32)


def dot3(a, b):
    (ah, al), (bh, bl) = a, b
    return mm(ah, bh) + (mm(ah, bl) + mm(al, bh))


def nt(a, b):
    return lax.dot_general(a, b, (((1,), (1,)), ((), ())), preferred_element_type=f32)


def tn(a, b):
    return lax.dot_general(a, b, (((0,), (0,)), ((), ())), preferred_element_type=f32)


def tn3(a, b):
    (ah, al), (bh, bl) = a, b
    return tn(ah, bh) + (tn(ah, bl) + tn(al, bh))


def embed(w):
    n = w.shape[1] // 2
    return split(
        jnp.concatenate([w, jnp.concatenate([-w[:, n:], w[:, :n]], axis=1)], axis=0)
    )


def times(x, e):
    return dot3(split(x), e)


def body(nq, ns, f_hbm, on_hbm, v_hbm, y_hbm, w_ref, sub_ref, corr_ref, proj_ref,
         F, ON, V, Y, onh, onl, maps, vecs, uin, uout, tin, tout, ufull, tfull,
         seg_in, seg_out, z_buf, s_buf, g_buf, s_rs, g_rs, red, red_in, qbuf, full,
         lsem, ssem, rsem):
    B = F.shape[1]
    R = V.shape[0]
    M = Y.shape[1]
    hb = M // 2
    nc = ns // 2
    mid = nc // 2
    qrows = B // nq
    ch = M // ns
    q = lax.axis_index("quad")
    s = lax.axis_index("slab")
    chip = s // 2
    core = s % 2
    buddy = chip * 2 + (1 - core)

    loads = [
        pltpu.make_async_copy(src, dst, lsem.at[i])
        for i, (src, dst) in enumerate(
            [(y_hbm.at[0], Y), (f_hbm.at[0, 0], F), (v_hbm.at[0], V), (on_hbm.at[0], ON)]
        )
    ]
    for copy in loads:
        copy.start()

    barrier = pltpu.get_barrier_semaphore()
    for d in range(1, ns):
        pl.semaphore_signal(barrier, inc=1, device_id={"slab": lax.rem(s + d, ns)}, device_id_type=MESH)
    for d in range(1, nq):
        pl.semaphore_signal(barrier, inc=1, device_id={"quad": lax.rem(q + d, nq)}, device_id_type=MESH)

    def remote(src, dst, sem, **where):
        return pltpu.make_async_remote_copy(
            src_ref=src, dst_ref=dst, send_sem=ssem.at[sem], recv_sem=rsem.at[sem],
            device_id=where, device_id_type=MESH,
        )

    for copy in loads[:3]:
        copy.wait()
    y = Y[...]
    src_re = mm(F[0], y)
    src_im = mm(F[1], y)
    v = V[...]
    vs = split(v)
    vts = split(v.T)
    last = slice(B - R, B)
    f21 = jnp.concatenate([F[0, last, :R], F[1, last, :R]], axis=1)
    a_cols = mm(vts[0], f21) + mm(vts[1], f21)
    s_last = split(jnp.concatenate([src_re[last], src_im[last]], axis=1))
    b_cols = dot3(vts, s_last)
    f12 = jnp.concatenate([F[0, :R, last], F[1, :R, last]], axis=0)
    c_rows = mm(f12, vs[0]) + mm(f12, vs[1])
    vecs[core, 0] = jnp.concatenate([b_cols[:, :M].T, b_cols[:, M:].T], axis=1)
    vecs[core, 1] = jnp.concatenate([src_re[:R].T, src_im[:R].T], axis=1)
    maps[core, 0] = jnp.concatenate([a_cols[:, :R].T, a_cols[:, R:].T], axis=1)
    maps[core, 1] = jnp.concatenate([c_rows[:R].T, c_rows[R:].T], axis=1)
    maps[core, 2] = jnp.concatenate(
        [F[0, :R, :R].astype(f32).T, F[1, :R, :R].astype(f32).T], axis=1
    )

    pl.semaphore_wait(barrier, ns - 1 + nq - 1)
    pair_v = remote(vecs.at[core], vecs.at[core], 0, slab=buddy)
    pair_m = remote(maps.at[core], maps.at[core], 1, slab=buddy)
    pair_v.start()
    pair_m.start()

    wr, wi = w_ref[0, 0], w_ref[0, 1]
    s_buf[...] = wr * src_re - wi * src_im

    pltpu.make_async_remote_copy(
        src_ref=vecs.at[core], dst_ref=vecs.at[1 - core], send_sem=ssem.at[0],
        recv_sem=rsem.at[0], device_id={"slab": buddy}, device_id_type=MESH).wait_recv()
    pltpu.make_async_remote_copy(
        src_ref=maps.at[core], dst_ref=maps.at[1 - core], send_sem=ssem.at[1],
        recv_sem=rsem.at[1], device_id={"slab": buddy}, device_id_type=MESH).wait_recv()

    al, cl, dl = maps[0, 0], maps[0, 1], maps[0, 2]
    ar, cr, dr = maps[1, 0], maps[1, 1], maps[1, 2]
    bl, el = vecs[0, 0], vecs[0, 1]
    br, er = vecs[1, 0], vecs[1, 1]
    zero_map = jnp.zeros((R, 2 * R), f32)
    ab_l = split(jnp.concatenate([al, bl], axis=0))
    ab = dot3(ab_l, embed(ar)) + jnp.concatenate([zero_map, br], axis=0)
    rows = pl.ds(pl.multiple_of(core * hb, hb), hb)
    other_rows = pl.ds(pl.multiple_of((1 - core) * hb, hb), hb)

    def half(x):
        return jnp.where(core == 0, x[:hb], x[hb:])

    forward = remote(uout, uin, 2, slab=jnp.minimum(s + 2, ns - 2 + core))
    back = remote(tout, tin, 3, slab=jnp.maximum(s - 2, core))
    seg = remote(seg_out, seg_in, 4, slab=jnp.maximum(s - 2, core))

    @pl.when(chip == 0)
    def _():
        uin[...] = jnp.zeros_like(uin)
        uout[...] = half(ab[R:])
        forward.start()

    g = dot3(ab_l, embed(dr)) + jnp.concatenate([zero_map, er], axis=0)
    gc = times(jnp.concatenate([g, cr], axis=0), embed(cl))
    chip_d = gc[: R + M] + jnp.concatenate([dl, el], axis=0)
    chip_c = gc[R + M :]

    @pl.when(chip == nc - 1)
    def _():
        z_buf[...] = jnp.zeros_like(z_buf)
        seg_out[...] = chip_d

    @pl.when(jnp.logical_and(chip >= mid, chip < nc - 1))
    def _():
        seg.wait_recv()
        z = times(ab, embed(seg_in[:R])) + jnp.concatenate([zero_map, seg_in[R:]], axis=0)
        z_buf[...] = z
        seg_out[...] = times(z, embed(chip_c)) + chip_d

    @pl.when(chip > mid)
    def _():
        seg.start()

    e_out = embed(ab[:R])
    e_seg = embed(jnp.where(chip >= mid, seg_out[:R], chip_d[:R]))

    @pl.when(chip > 0)
    def _():
        forward.wait_recv()

    u_in = uin[...]
    us = split(u_in)

    @pl.when(chip == mid)
    def _():
        tout[...] = dot3(us, e_seg) + half(seg_out[R:])
        back.start()

    @pl.when(jnp.logical_and(chip > 0, chip < nc - 1))
    def _():
        uout[...] = dot3(us, e_out) + half(ab[R:])
        forward.start()

    ufull[rows, :] = u_in
    cross_u = remote(ufull.at[rows], ufull.at[rows], 5, slab=buddy)
    cross_u.start()

    @pl.when(chip >= mid)
    def _():
        tin[...] = dot3(us, embed(z_buf[:R])) + half(z_buf[R:])

    @pl.when(chip < mid)
    def _():
        const = dot3(us, e_seg) + half(chip_d[R:])
        e_c = embed(chip_c)
        back.wait_recv()

        @pl.when(chip > 0)
        def _():
            tout[...] = times(tin[...], e_c) + const
            back.start()

    tfull[rows, :] = tin[...]
    cross_t = remote(tfull.at[rows], tfull.at[rows], 6, slab=buddy)
    cross_t.start()

    remote(ufull.at[rows], ufull.at[other_rows], 5, slab=buddy).wait_recv()
    u_chip = ufull[...]
    u_left = times(u_chip, embed(al)) + bl
    t_const = times(u_left, embed(dr)) + er
    e_cr = embed(cr)
    u_own = jnp.where(core == 0, u_chip, u_left)

    def weighted(x):
        re, im = x[:, :R], x[:, R:]
        return wr * re - wi * im, -(wr * im + wi * re)

    wu = split(jnp.concatenate(weighted(u_own), axis=1))
    f_left = jnp.concatenate([F[0, :, :R], F[1, :, :R]], axis=1)
    f_right = jnp.concatenate([F[0, :, last], F[1, :, last]], axis=1)
    s_buf[...] += nt(f_left, wu[0]) + nt(f_left, wu[1])
    loads[3].wait()
    on = split(0.5 * ON[...])
    onh[...] = on[0]
    onl[...] = on[1]

    remote(tfull.at[rows], tfull.at[other_rows], 6, slab=buddy).wait_recv()
    t_chip = tfull[...]
    t_own = jnp.where(core == 0, times(t_chip, e_cr) + t_const, t_chip)
    wt = split(jnp.concatenate(weighted(t_own), axis=0))
    vt = nt(wt[0], vs[0]) + (nt(wt[0], vs[1]) + nt(wt[1], vs[0]))
    z = split(jnp.concatenate([vt[:M], vt[M:]], axis=1))
    s_buf[...] += nt(f_right, z[0]) + nt(f_right, z[1])

    base = 7
    quad_copies = []
    for part, (buf, landing) in enumerate([(s_buf, s_rs), (g_buf, g_rs)]):
        if part == 1:
            fs = split(s_buf[...])
            g_buf[...] = dot3((onh[...], onl[...]), fs)
            g_buf[last, :] += vt[:M].T
        for d in range(1, nq):
            to = lax.rem(q + d, nq)
            copy = remote(
                buf.at[pl.ds(pl.multiple_of(to * qrows, qrows), qrows)],
                landing.at[d - 1], base, quad=to)
            copy.start()
            quad_copies.append(copy)
            base += 1
    mine = pl.ds(pl.multiple_of(q * qrows, qrows), qrows)
    total_s = s_buf[mine, :]
    for d in range(1, nq):
        quad_copies[d - 1].wait_recv()
        total_s += s_rs[d - 1]
    sub_ref[0] = total_s
    ss = split(total_s)
    gram = tn3(ss, ss)
    total_g = g_buf[mine, :]
    for d in range(1, nq):
        quad_copies[nq - 2 + d].wait_recv()
        total_g += g_rs[d - 1]
    x = tn3(ss, split(total_g))
    proj = x + x.T

    at_row = lax.broadcasted_iota(jnp.int32, (M, M), 0)
    at_col = lax.broadcasted_iota(jnp.int32, (M, M), 1)
    tile = jnp.where(at_row <= at_col, gram, proj)
    diag = jnp.sum(jnp.where(at_row == at_col, proj, 0.0), axis=0, keepdims=True)
    diag = jnp.broadcast_to(diag, (8, M))
    for i in range(ns):
        red[i, :ch] = tile[i * ch : (i + 1) * ch]
        red[i, ch : ch + 8] = diag
    copies = []
    for d in range(1, ns):
        to = lax.rem(s + d, ns)
        copy = remote(red.at[to], red_in.at[d - 1], base, slab=to)
        copy.start()
        copies.append(copy)
        base += 1
    part = red[s]
    for d in range(1, ns):
        copies[d - 1].wait_recv()
        part += red_in[d - 1]
    qbuf[q] = part
    for d in range(1, nq):
        copy = remote(qbuf.at[q], qbuf.at[q], base, quad=lax.rem(q + d, nq))
        copy.start()
        copies.append(copy)
        base += 1
    for d in range(1, nq):
        remote(qbuf.at[q], qbuf.at[lax.rem(q - d + nq, nq)], base - nq + d, quad=lax.rem(q + d, nq)).wait_recv()
    part = qbuf[0]
    for k in range(1, nq):
        part += qbuf[k]
    full[s] = part
    for d in range(1, ns):
        copy = remote(full.at[s], full.at[s], base, slab=lax.rem(s + d, ns))
        copy.start()
        copies.append(copy)
        base += 1
    for d in range(1, ns):
        remote(full.at[s], full.at[lax.rem(s - d + ns, ns)], base - ns + d, slab=lax.rem(s + d, ns)).wait_recv()
    scale = 1.0 / (ns * B)
    tile = jnp.concatenate([full[i, :ch] for i in range(ns)], axis=0) * scale
    diag = full[0, ch : ch + 1] * scale
    flipped = tile.T
    corr_ref[...] = jnp.where(at_row <= at_col, tile, flipped)
    low = jnp.where(at_row > at_col, tile, flipped)
    proj_ref[...] = jnp.where(at_row == at_col, jnp.broadcast_to(diag, (M, M)), low)

    pair_v.wait_send()
    pair_m.wait_send()
    cross_u.wait_send()
    cross_t.wait_send()

    @pl.when(chip < nc - 1)
    def _():
        forward.wait_send()

    @pl.when(chip > mid)
    def _():
        seg.wait_send()

    @pl.when(jnp.logical_and(chip > 0, chip <= mid))
    def _():
        back.wait_send()

    for copy in quad_copies + copies:
        copy.wait_send()


def per_device(nq, ns, factors, onsite, coupling, vectors, quad_weight):
    B = factors.shape[3]
    R = coupling.shape[1]
    M = vectors.shape[2]
    hb, ch, qrows = M // 2, M // ns, B // nq
    sems = 7 + 2 * (nq - 1) + 2 * (ns - 1) + (nq - 1)
    vm = pltpu.VMEM
    anywhere = pl.BlockSpec(memory_space=pl.ANY)
    here = pl.BlockSpec(memory_space=pltpu.VMEM)
    return pl.pallas_call(
        functools.partial(body, nq, ns),
        out_shape=(
            jax.ShapeDtypeStruct((1, qrows, M), f32),
            jax.ShapeDtypeStruct((M, M), f32),
            jax.ShapeDtypeStruct((M, M), f32),
        ),
        in_specs=[anywhere] * 4 + [pl.BlockSpec(memory_space=pltpu.SMEM)],
        out_specs=(here, here, here),
        scratch_shapes=[
            vm((2, B, B), bf16), vm((B, B), f32), vm((R, R), f32), vm((B, M), bf16),
            vm((B, B), bf16), vm((B, B), bf16),
            vm((2, 3, R, 2 * R), f32), vm((2, 2, M, 2 * R), f32),
            vm((hb, 2 * R), f32), vm((hb, 2 * R), f32), vm((hb, 2 * R), f32), vm((hb, 2 * R), f32),
            vm((M, 2 * R), f32), vm((M, 2 * R), f32),
            vm((R + M, 2 * R), f32), vm((R + M, 2 * R), f32), vm((R + M, 2 * R), f32),
            vm((B, M), f32), vm((B, M), f32),
            vm((nq - 1, qrows, M), f32), vm((nq - 1, qrows, M), f32),
            vm((ns, ch + 8, M), f32), vm((ns - 1, ch + 8, M), f32),
            vm((nq, ch + 8, M), f32), vm((ns, ch + 8, M), f32),
            pltpu.SemaphoreType.DMA((4,)),
            pltpu.SemaphoreType.DMA((sems,)),
            pltpu.SemaphoreType.DMA((sems,)),
        ],
        compiler_params=pltpu.CompilerParams(
            collective_id=0, has_side_effects=True, vmem_limit_bytes=40 * 2**20
        ),
    )(factors, onsite, coupling, vectors, quad_weight)


def solution(mesh):
    placed = (
        P("quad", "slab", None, None, None),
        P("slab", None, None),
        P("slab", None, None),
        P("slab", None, None),
        P("quad", None),
    )
    return jax.shard_map(
        functools.partial(per_device, mesh.shape["quad"], mesh.shape["slab"]),
        mesh=mesh,
        in_specs=placed,
        out_specs=(P("slab", "quad", None), P(), P()),
        check_vma=False,
    )
```

```python
import functools

import jax
import jax.numpy as jnp
from jax import lax
from jax.experimental import pallas as pl
from jax.experimental.pallas import tpu as pltpu
from jax.sharding import PartitionSpec as P

MESH = pl.DeviceIdType.MESH
f32, bf16 = jnp.float32, jnp.bfloat16
VMEM_BYTES = 64 * 2**20 - 64 * 2**10


def split(x):
    high = x.astype(bf16)
    return high, (x - high.astype(f32)).astype(bf16)


def mm(a, b):
    return jnp.dot(a, b, preferred_element_type=f32)


def dot3(a, b):
    (ah, al), (bh, bl) = a, b
    return mm(ah, bh) + (mm(ah, bl) + mm(al, bh))


def nt(a, b):
    return lax.dot_general(a, b, (((1,), (1,)), ((), ())), preferred_element_type=f32)


def tn(a, b):
    return lax.dot_general(a, b, (((0,), (0,)), ((), ())), preferred_element_type=f32)


def tn3(a, b):
    (ah, al), (bh, bl) = a, b
    return tn(ah, bh) + (tn(ah, bl) + tn(al, bh))


def embed(w):
    n = w.shape[1] // 2
    return split(
        jnp.concatenate([w, jnp.concatenate([-w[:, n:], w[:, :n]], axis=1)], axis=0)
    )


def times(x, e):
    return dot3(split(x), e)


def body(nq, ns, f_hbm, on_hbm, v_hbm, y_hbm, w_ref, sub_ref, tile_ref,
         F, ON, V, Y, onh, onl, abs_, cde, uin, uout, tmid, tout, ufull, tfull,
         seg_in, seg_out, z_buf, c_in, c_out, e_in, e_out, s_buf, g_buf, low_in, high_in, nxt, land,
         red, red_in, full, lsem, ssem, rsem):
    B = F.shape[1]
    R = V.shape[0]
    M = Y.shape[1]
    hb = M // 2
    nc = ns // 2
    mid = nc // 2
    qrows = B // nq
    ch = M // ns
    blocks = B // R
    q = lax.axis_index("quad")
    s = lax.axis_index("slab")
    chip = s // 2
    core = s % 2
    buddy = chip * 2 + (1 - core)

    def home(slab):
        return nq // 2 - 1 + slab % 2

    target = home(s)

    loads = [
        pltpu.make_async_copy(src, dst, lsem.at[i])
        for i, (src, dst) in enumerate([
            (y_hbm.at[0], Y), (f_hbm.at[0, 0, 0], F.at[0]), (f_hbm.at[0, 0, 1], F.at[1]),
            (v_hbm.at[0], V), (on_hbm.at[0], ON)])
    ]
    for copy in loads:
        copy.start()

    barrier = pltpu.get_barrier_semaphore()
    for d in range(1, ns):
        pl.semaphore_signal(barrier, inc=1, device_id={"slab": lax.rem(s + d, ns)}, device_id_type=MESH)
    for d in range(1, nq):
        pl.semaphore_signal(barrier, inc=1, device_id={"quad": lax.rem(q + d, nq)}, device_id_type=MESH)

    @pl.when(q == target)
    def _():
        for d in range(1, ns, 2):
            to = lax.rem(s + d, ns)
            pl.semaphore_signal(barrier, inc=1, device_id={"quad": home(to), "slab": to}, device_id_type=MESH)

    counts = [0, 0]

    def fresh(which):
        counts[which] += 1
        return counts[which] - 1

    def remote(src, dst, recv, **where):
        return pltpu.make_async_remote_copy(
            src_ref=src, dst_ref=dst, send_sem=ssem.at[fresh(0)], recv_sem=rsem.at[recv],
            device_id=where, device_id_type=MESH,
        )

    def arrival(dst, recv):
        return pltpu.make_async_remote_copy(
            src_ref=dst, dst_ref=dst, send_sem=ssem.at[0], recv_sem=rsem.at[recv],
            device_id={"slab": buddy}, device_id_type=MESH,
        )

    for copy in loads[:4]:
        copy.wait()
    y = Y[...]
    src_re = mm(F[0], y)
    src_im = mm(F[1], y)
    v = V[...]
    vs = split(v)
    vts = split(v.T)
    last = slice(B - R, B)
    f21 = jnp.concatenate([F[0, last, :R], F[1, last, :R]], axis=1)
    a_cols = mm(vts[0], f21) + mm(vts[1], f21)
    s_last = split(jnp.concatenate([src_re[last], src_im[last]], axis=1))
    b_cols = dot3(vts, s_last)
    abs_[core, :R] = jnp.concatenate([a_cols[:, :R].T, a_cols[:, R:].T], axis=1)
    abs_[core, R:] = jnp.concatenate([b_cols[:, :M].T, b_cols[:, M:].T], axis=1)

    base_wait = ns - 1 + nq - 1

    @pl.when(q == target)
    def _():
        pl.semaphore_wait(barrier, base_wait + ns // 2)

    @pl.when(q != target)
    def _():
        pl.semaphore_wait(barrier, base_wait)

    r_ab, r_cde = fresh(1), fresh(1)
    pair_ab = remote(abs_.at[core], abs_.at[core], r_ab, slab=buddy)
    pair_cde = remote(cde.at[core], cde.at[core], r_cde, slab=buddy)
    pair_ab.start()

    f12 = jnp.concatenate([F[0, :R, last], F[1, :R, last]], axis=0)
    c_rows = mm(f12, vs[0]) + mm(f12, vs[1])
    cde[core, 0] = jnp.concatenate([c_rows[:R].T, c_rows[R:].T], axis=1)
    cde[core, 1] = jnp.concatenate(
        [F[0, :R, :R].astype(f32).T, F[1, :R, :R].astype(f32).T], axis=1
    )
    cde[core, 2] = jnp.concatenate([src_re[:R].T, src_im[:R].T], axis=1)
    pair_cde.start()

    rows = pl.ds(pl.multiple_of(core * hb, hb), hb)
    other_rows = pl.ds(pl.multiple_of((1 - core) * hb, hb), hb)

    def half(x):
        return jnp.where(core == 0, x[:hb], x[hb:])

    r_u, r_t, r_seg, r_relay, r_c, r_e = (fresh(1) for _ in range(6))
    left = jnp.maximum(s - 2, core)
    forward = remote(uout, uin, r_u, slab=jnp.minimum(s + 2, ns - 2 + core))
    back = [remote(tout, tmid, r_t, slab=2 * c + core) for c in range(mid)]
    seg = remote(seg_out.at[core], seg_in.at[core], r_seg, slab=left)
    relay = remote(seg_in.at[core], seg_in.at[core], r_relay, slab=buddy)
    send_c = remote(c_out, c_in, r_c, slab=left)
    send_e = remote(e_out, e_in, r_e, slab=left)
    inner_left = jnp.logical_and(chip > 0, chip < mid)

    arrival(abs_.at[1 - core], r_ab).wait_recv()
    ab_l = split(abs_[0])
    zero_map = jnp.zeros((R, 2 * R), f32)
    ab = dot3(ab_l, embed(abs_[1, :R])) + jnp.concatenate([zero_map, abs_[1, R:]], axis=0)

    @pl.when(chip == 0)
    def _():
        uin[...] = jnp.zeros_like(uin)
        uout[...] = half(ab[R:])
        forward.start()

    arrival(cde.at[1 - core], r_cde).wait_recv()
    cl, dl, el = cde[0, 0], cde[0, 1], cde[0, 2]
    cr, dr, er = cde[1, 0], cde[1, 1], cde[1, 2]
    e_dr = embed(dr)
    g = dot3(ab_l, e_dr) + jnp.concatenate([zero_map, er], axis=0)
    gc = times(jnp.concatenate([g, cr], axis=0), embed(cl))
    chip_d = gc[: R + M] + jnp.concatenate([dl, el], axis=0)
    chip_c = gc[R + M :]

    @pl.when(chip == nc - 1)
    def _():
        z_buf[...] = jnp.zeros_like(z_buf)
        seg_out[0] = chip_d[:R]
        seg_out[1] = chip_d[R:]

    @pl.when(jnp.logical_and(chip >= mid, chip < nc - 1))
    def _():
        seg.wait_recv()
        relay.start()
        arrival(seg_in.at[1 - core], r_relay).wait_recv()
        z = times(ab, embed(seg_in[0])) + jnp.concatenate([zero_map, seg_in[1]], axis=0)
        z_buf[...] = z
        out = times(z, embed(chip_c)) + chip_d
        seg_out[0] = out[:R]
        seg_out[1] = out[R:]

    @pl.when(chip > mid)
    def _():
        seg.start()

    @pl.when(chip == mid - 1)
    def _():
        c_out[...] = chip_c

    @pl.when(chip < mid - 1)
    def _():
        send_c.wait_recv()

        @pl.when(chip > 0)
        def _():
            c_out[...] = times(c_in[...], embed(chip_c))

    @pl.when(inner_left)
    def _():
        send_c.start()

    e_out_map = embed(ab[:R])
    e_seg = embed(jnp.where(chip >= mid, seg_out[0], chip_d[:R]))

    @pl.when(chip > 0)
    def _():
        forward.wait_recv()

    u_in = uin[...]
    us = split(u_in)

    @pl.when(chip == mid)
    def _():
        tout[...] = dot3(us, e_seg) + half(seg_out[1])
        for copy in back:
            copy.start()

    @pl.when(jnp.logical_and(chip > 0, chip < nc - 1))
    def _():
        uout[...] = dot3(us, e_out_map) + half(ab[R:])
        forward.start()

    r_cu, r_ct = fresh(1), fresh(1)
    ufull[rows, :] = u_in
    cross_u = remote(ufull.at[rows], ufull.at[rows], r_cu, slab=buddy)
    cross_u.start()
    cross_t = remote(tfull.at[rows], tfull.at[rows], r_ct, slab=buddy)

    @pl.when(inner_left)
    def _():
        const = dot3(us, e_seg) + half(chip_d[R:])

        @pl.when(chip == mid - 1)
        def _():
            e_out[...] = const

        @pl.when(chip < mid - 1)
        def _():
            send_e.wait_recv()
            e_out[...] = times(e_in[...], embed(chip_c)) + const

        send_e.start()

    @pl.when(chip == 0)
    def _():
        if mid > 1:
            send_e.wait_recv()

    @pl.when(chip >= mid)
    def _():
        tfull[rows, :] = dot3(us, embed(z_buf[:R])) + half(z_buf[R:])
        cross_t.start()

    wr, wi = w_ref[0, 0], w_ref[0, 1]

    def weighted(x):
        re, im = x[:, :R], x[:, R:]
        return wr * re - wi * im, -(wr * im + wi * re)

    arrival(ufull.at[other_rows], r_cu).wait_recv()
    u_chip = ufull[...]
    u_left = times(u_chip, embed(abs_[0, :R])) + abs_[0, R:]
    t_const = times(u_left, e_dr) + er
    e_cr = embed(cr)
    u_own = jnp.where(core == 0, u_chip, u_left)
    wu = split(jnp.concatenate(weighted(u_own), axis=1))
    f_left = jnp.concatenate([F[0, :, :R], F[1, :, :R]], axis=1)
    f_right = jnp.concatenate([F[0, :, last], F[1, :, last]], axis=1)
    s_buf[...] = wr * src_re - wi * src_im + (nt(f_left, wu[0]) + nt(f_left, wu[1]))
    loads[4].wait()

    @pl.when(q == target)
    def _():
        on = split(0.5 * ON[...])
        onh[...] = on[0]
        onl[...] = on[1]

    @pl.when(chip < mid)
    def _():
        back[0].wait_recv()

        @pl.when(chip == mid - 1)
        def _():
            tfull[rows, :] = tmid[...]

        @pl.when(chip < mid - 1)
        def _():
            tfull[rows, :] = times(tmid[...], embed(c_in[...])) + e_in[...]

        cross_t.start()

    arrival(tfull.at[other_rows], r_ct).wait_recv()
    t_chip = tfull[...]
    t_own = jnp.where(core == 0, times(t_chip, e_cr) + t_const, t_chip)
    wt = split(jnp.concatenate(weighted(t_own), axis=0))
    vt = nt(wt[0], vs[0]) + (nt(wt[0], vs[1]) + nt(wt[1], vs[0]))
    z = split(jnp.concatenate([vt[:M], vt[M:]], axis=1))

    ups, downs, r_low, r_high = [], [], [], []
    for i in range(blocks):
        part = slice(i * R, (i + 1) * R)
        r_low.append(fresh(1))
        r_high.append(fresh(1))
        ups.append(remote(s_buf.at[part], low_in.at[i], r_low[i], quad=jnp.minimum(q + 1, nq - 1)))
        downs.append(remote(s_buf.at[part], high_in.at[i], r_high[i], quad=jnp.maximum(q - 1, 0)))
    for i in range(blocks):
        part = slice(i * R, (i + 1) * R)
        s_buf[part, :] += nt(f_right[part], z[0]) + nt(f_right[part], z[1])

        @pl.when(q == 0)
        def _():
            ups[i].start()

        @pl.when(q == nq - 1)
        def _():
            downs[i].start()

    for i in range(blocks):
        part = slice(i * R, (i + 1) * R)

        @pl.when(jnp.logical_and(q > 0, q < target))
        def _():
            ups[i].wait_recv()
            s_buf[part, :] += low_in[i]
            ups[i].start()

        @pl.when(jnp.logical_and(q > target, q < nq - 1))
        def _():
            downs[i].wait_recv()
            s_buf[part, :] += high_in[i]
            downs[i].start()

    r_next, r_sub, r_line, r_full = (fresh(1) for _ in range(4))
    before = jnp.where(s > 0, s - 1, 1)
    to_prev = remote(s_buf.at[:R], nxt, r_next, quad=home(before), slab=before)
    shares = [
        remote(s_buf.at[slice(p * qrows, (p + 1) * qrows)], land, r_sub, quad=p)
        for p in range(nq)
    ]
    r_red = [fresh(1) for _ in range(1, ns)]
    scatter = []
    for d in range(1, ns):
        to = lax.rem(s + d, ns)
        scatter.append(remote(red.at[to], red_in.at[d - 1], r_red[d - 1], quad=home(to), slab=to))
    line = [remote(full.at[s], full.at[s], r_line, quad=lax.rem(q + d, nq)) for d in range(1, nq)]

    @pl.when(q == target)
    def _():
        gram = jnp.zeros((M, M), f32)
        for i in range(blocks):
            part = slice(i * R, (i + 1) * R)
            ups[i].wait_recv()
            downs[i].wait_recv()
            total = s_buf[part, :] + low_in[i] + high_in[i]
            s_buf[part, :] = total
            if i == 0:
                @pl.when(s > 0)
                def _():
                    to_prev.start()
            for p in range(nq):
                if i * R < (p + 1) * qrows <= (i + 1) * R:
                    @pl.when(q == p)
                    def _():
                        land[...] = s_buf[p * qrows : (p + 1) * qrows]

                    @pl.when(q != p)
                    def _():
                        shares[p].start()
            piece = split(total)
            gram += tn3(piece, piece)
            more = dot3((onh[:, part], onl[:, part]), piece)
            if i == 0:
                g_buf[...] = more
            else:
                g_buf[...] += more

        @pl.when(s < ns - 1)
        def _():
            to_prev.wait_recv()
            g_buf[last, :] += dot3(vs, split(nxt[...]))

        x = tn3(split(s_buf[...]), split(g_buf[...]))
        proj = x + x.T

        at_row = lax.broadcasted_iota(jnp.int32, (M, M), 0)
        at_col = lax.broadcasted_iota(jnp.int32, (M, M), 1)
        tile = jnp.where(at_row <= at_col, gram, proj)
        diag = jnp.sum(jnp.where(at_row == at_col, proj, 0.0), axis=0, keepdims=True)
        diag = jnp.broadcast_to(diag, (8, M))
        for i in range(ns):
            red[i, :ch] = tile[i * ch : (i + 1) * ch]
            red[i, ch : ch + 8] = diag
        for copy in scatter:
            copy.start()
        part = red[s]
        for d in range(1, ns):
            scatter[d - 1].wait_recv()
            part += red_in[d - 1]
        full[s] = part
        for copy in line:
            copy.start()

    @pl.when(q != target)
    def _():
        arrival(full.at[s], r_line).wait_recv()
        shares[0].wait_recv()

    spread, r_spread = [], []
    for d in range(1, ns):
        r_spread.append(fresh(1))
        copy = remote(full.at[s], full.at[s], r_spread[-1], slab=lax.rem(s + d, ns))
        copy.start()
        spread.append(copy)
    sub_ref[0] = land[...]
    for d in range(1, ns):
        arrival(full.at[lax.rem(s - d + ns, ns)], r_spread[d - 1]).wait_recv()
    scale = 1.0 / (ns * B)
    for i in range(ns):
        tile_ref[i * ch : (i + 1) * ch, :] = full[i, :ch] * scale
    tile_ref[M : M + 8, :] = full[0, ch : ch + 8] * scale

    for copy in [pair_ab, pair_cde, cross_u, cross_t] + spread:
        copy.wait_send()

    @pl.when(chip < nc - 1)
    def _():
        forward.wait_send()

    @pl.when(chip > mid)
    def _():
        seg.wait_send()

    @pl.when(jnp.logical_and(chip >= mid, chip < nc - 1))
    def _():
        relay.wait_send()

    @pl.when(inner_left)
    def _():
        send_c.wait_send()
        send_e.wait_send()

    @pl.when(chip == mid)
    def _():
        for copy in back:
            copy.wait_send()

    @pl.when(q < target)
    def _():
        for copy in ups:
            copy.wait_send()

    @pl.when(q > target)
    def _():
        for copy in downs:
            copy.wait_send()

    @pl.when(q == target)
    def _():
        for copy in scatter + line:
            copy.wait_send()

        @pl.when(s > 0)
        def _():
            to_prev.wait_send()

        for p in range(nq):
            @pl.when(q != p)
            def _():
                shares[p].wait_send()


def unpack(sub_ref, tile_ref, out_ref, corr_ref, proj_ref):
    M = corr_ref.shape[0]
    out_ref[...] = sub_ref[...]
    tile = tile_ref[:M]
    diag = tile_ref[M : M + 1]
    at_row = lax.broadcasted_iota(jnp.int32, (M, M), 0)
    at_col = lax.broadcasted_iota(jnp.int32, (M, M), 1)
    flipped = tile.T
    corr_ref[...] = jnp.where(at_row <= at_col, tile, flipped)
    low = jnp.where(at_row > at_col, tile, flipped)
    proj_ref[...] = jnp.where(at_row == at_col, jnp.broadcast_to(diag, (M, M)), low)


def per_device(nq, ns, factors, onsite, coupling, vectors, quad_weight):
    B = factors.shape[3]
    R = coupling.shape[1]
    M = vectors.shape[2]
    hb, ch, qrows, blocks = M // 2, M // ns, B // nq, B // R
    sends = 10 + ns // 4 + 2 * blocks + 1 + nq + (ns - 1) + (nq - 1) + (ns - 1)
    recvs = 10 + 2 * blocks + 4 + 2 * (ns - 1)
    vm = pltpu.VMEM
    in_hbm = pl.BlockSpec(memory_space=pltpu.HBM)
    here = pl.BlockSpec(memory_space=pltpu.VMEM)
    wide = vm((M, 2 * R), f32)
    thin = vm((hb, 2 * R), f32)
    sub, tile = pl.pallas_call(
        functools.partial(body, nq, ns),
        out_shape=(
            jax.ShapeDtypeStruct((1, qrows, M), f32),
            jax.ShapeDtypeStruct((M + 8, M), f32),
        ),
        in_specs=[in_hbm] * 4 + [pl.BlockSpec(memory_space=pltpu.SMEM)],
        out_specs=(here, here),
        scratch_shapes=[
            vm((2, B, B), bf16), vm((B, B), f32), vm((R, R), f32), vm((B, M), bf16),
            vm((B, B), bf16), vm((B, B), bf16),
            vm((2, R + M, 2 * R), f32), vm((2, 3, R, 2 * R), f32),
            thin, thin, thin, thin, wide, wide,
            vm((2, R, 2 * R), f32), vm((2, R, 2 * R), f32), vm((R + M, 2 * R), f32),
            vm((R, 2 * R), f32), vm((R, 2 * R), f32), thin, thin,
            vm((B, M), f32), vm((B, M), f32),
            vm((blocks, R, M), f32), vm((blocks, R, M), f32), vm((R, M), f32), vm((qrows, M), f32),
            vm((ns, ch + 8, M), f32), vm((ns - 1, ch + 8, M), f32), vm((ns, ch + 8, M), f32),
            pltpu.SemaphoreType.DMA((5,)),
            pltpu.SemaphoreType.DMA((sends,)),
            pltpu.SemaphoreType.DMA((recvs,)),
        ],
        compiler_params=pltpu.CompilerParams(
            collective_id=0, has_side_effects=True, vmem_limit_bytes=VMEM_BYTES
        ),
    )(factors, onsite, coupling, vectors, quad_weight)
    return pl.pallas_call(
        unpack,
        out_shape=(
            jax.ShapeDtypeStruct((1, qrows, M), f32),
            jax.ShapeDtypeStruct((M, M), f32),
            jax.ShapeDtypeStruct((M, M), f32),
        ),
        in_specs=[here, here],
        out_specs=(here, here, here),
        compiler_params=pltpu.CompilerParams(vmem_limit_bytes=VMEM_BYTES),
    )(sub, tile)


def solution(mesh):
    placed = (
        P("quad", "slab", None, None, None),
        P("slab", None, None),
        P("slab", None, None),
        P("slab", None, None),
        P("quad", None),
    )
    return jax.shard_map(
        functools.partial(per_device, mesh.shape["quad"], mesh.shape["slab"]),
        mesh=mesh,
        in_specs=placed,
        out_specs=(P("slab", "quad", None), P(), P()),
        check_vma=False,
    )
```

```python
import functools

import jax
import jax.numpy as jnp
from jax import lax
from jax.experimental import pallas as pl
from jax.experimental.pallas import tpu as pltpu
from jax.sharding import PartitionSpec as P

MESH = pl.DeviceIdType.MESH
f32, bf16 = jnp.float32, jnp.bfloat16
VMEM_BYTES = 64 * 2**20 - 64 * 2**10


def split(x):
    high = x.astype(bf16)
    return high, (x - high.astype(f32)).astype(bf16)


def mm(a, b):
    return jnp.dot(a, b, preferred_element_type=f32)


def dot3(a, b):
    (ah, al), (bh, bl) = a, b
    return mm(ah, bh) + (mm(ah, bl) + mm(al, bh))


def nt(a, b):
    return lax.dot_general(a, b, (((1,), (1,)), ((), ())), preferred_element_type=f32)


def tn(a, b):
    return lax.dot_general(a, b, (((0,), (0,)), ((), ())), preferred_element_type=f32)


def tn3(a, b):
    (ah, al), (bh, bl) = a, b
    return tn(ah, bh) + (tn(ah, bl) + tn(al, bh))


def embed(w):
    n = w.shape[1] // 2
    return split(
        jnp.concatenate([w, jnp.concatenate([-w[:, n:], w[:, :n]], axis=1)], axis=0)
    )


def times(x, e):
    return dot3(split(x), e)


def body(nq, ns, f_hbm, on_hbm, v_hbm, y_hbm, w_ref, sub_ref, tile_ref,
         F, ON, V, Y, onh, onl, abs_, cde, uin, uout, tmid, tout, ufull, t_buf,
         dm_in, dm_out, dv_in, dv_out, c_in, c_out, e_in, e_out, s_buf, b_in, p_out, p_in, ph, pl_,
         wt_out, wt_in, land, red, red_in, full, lsem, ssem, rsem):
    B = F.shape[1]
    R = V.shape[0]
    M = Y.shape[1]
    hb = M // 2
    nc = ns // 2
    mid = nc // 2
    qrows = B // nq
    ch = M // ns
    q = lax.axis_index("quad")
    s = lax.axis_index("slab")
    chip = s // 2
    core = s % 2
    buddy = chip * 2 + (1 - core)

    def home(slab):
        return nq // 2 - 1 + slab % 2

    target = home(s)

    top, last = slice(0, B - R), slice(B - R, B)
    loads = [
        pltpu.make_async_copy(src, dst, lsem.at[i])
        for i, (src, dst) in enumerate([
            (y_hbm.at[0], Y), (v_hbm.at[0], V),
            (f_hbm.at[0, 0, 0, last], F.at[0, last]), (f_hbm.at[0, 0, 1, last], F.at[1, last]),
            (f_hbm.at[0, 0, 0, top], F.at[0, top]), (f_hbm.at[0, 0, 1, top], F.at[1, top]),
            (on_hbm.at[0], ON)])
    ]
    for copy in loads:
        copy.start()

    barrier = pltpu.get_barrier_semaphore()
    for d in range(1, ns):
        pl.semaphore_signal(barrier, inc=1, device_id={"slab": lax.rem(s + d, ns)}, device_id_type=MESH)
    for d in range(1, nq):
        pl.semaphore_signal(barrier, inc=1, device_id={"quad": lax.rem(q + d, nq)}, device_id_type=MESH)
        pl.semaphore_signal(
            barrier, inc=1, device_id={"quad": lax.rem(q + d, nq), "slab": buddy}, device_id_type=MESH)

    @pl.when(q == target)
    def _():
        for d in range(2, ns, 2):
            to = lax.rem(buddy + d, ns)
            pl.semaphore_signal(barrier, inc=1, device_id={"quad": home(to), "slab": to}, device_id_type=MESH)

    counts = [0, 0]

    def fresh(which):
        counts[which] += 1
        return counts[which] - 1

    def remote(src, dst, recv, **where):
        return pltpu.make_async_remote_copy(
            src_ref=src, dst_ref=dst, send_sem=ssem.at[fresh(0)], recv_sem=rsem.at[recv],
            device_id=where, device_id_type=MESH,
        )

    def arrival(dst, recv):
        return pltpu.make_async_remote_copy(
            src_ref=dst, dst_ref=dst, send_sem=ssem.at[0], recv_sem=rsem.at[recv],
            device_id={"slab": buddy}, device_id_type=MESH,
        )

    for copy in loads[:4]:
        copy.wait()
    y = Y[...]
    last_re = mm(F[0, last], y)
    last_im = mm(F[1, last], y)
    vs = split(V[...])
    vts = split(V[...].T)
    f21 = jnp.concatenate([F[0, last, :R], F[1, last, :R]], axis=1)
    a_cols = mm(vts[0], f21) + mm(vts[1], f21)
    s_last = split(jnp.concatenate([last_re, last_im], axis=1))
    b_cols = dot3(vts, s_last)
    abs_[core, :R] = jnp.concatenate([a_cols[:, :R].T, a_cols[:, R:].T], axis=1)
    abs_[core, R:] = jnp.concatenate([b_cols[:, :M].T, b_cols[:, M:].T], axis=1)

    base_wait = ns - 1 + 2 * (nq - 1)

    @pl.when(q == target)
    def _():
        pl.semaphore_wait(barrier, base_wait + ns // 2 - 1)

    @pl.when(q != target)
    def _():
        pl.semaphore_wait(barrier, base_wait)

    r_ab, r_cde = fresh(1), fresh(1)
    pair_ab = remote(abs_.at[core], abs_.at[core], r_ab, slab=buddy)
    pair_cde = remote(cde.at[core], cde.at[core], r_cde, slab=buddy)
    pair_ab.start()

    for copy in loads[4:6]:
        copy.wait()
    src_re = jnp.concatenate([mm(F[0, top], y), last_re], axis=0)
    src_im = jnp.concatenate([mm(F[1, top], y), last_im], axis=0)
    f_right = jnp.concatenate([F[0, :, last], F[1, :, last]], axis=0)
    p_rows = mm(f_right, vs[0]) + mm(f_right, vs[1])
    cde[core, 0] = jnp.concatenate([p_rows[:R].T, p_rows[B : B + R].T], axis=1)
    cde[core, 1] = jnp.concatenate(
        [F[0, :R, :R].astype(f32).T, F[1, :R, :R].astype(f32).T], axis=1
    )
    cde[core, 2] = jnp.concatenate([src_re[:R].T, src_im[:R].T], axis=1)
    pair_cde.start()
    p_out[...] = jnp.concatenate([p_rows[:B], p_rows[B:]], axis=1)
    r_p = [fresh(1) for _ in range(1, nq)]
    r_b = [fresh(1) for _ in range(1, nq)]
    r_wt = [fresh(1) for _ in range(2 * nq)]
    away = lax.rem(q - target + nq, nq)
    slot = jnp.maximum(away - 1, 0)
    send_p = remote(p_out, p_in.at[slot], r_p[0] + slot, quad=target)
    send_b = remote(s_buf, b_in.at[slot], r_b[0] + slot, quad=target)

    @pl.when(q != target)
    def _():
        send_p.start()

    rows = pl.ds(pl.multiple_of(core * hb, hb), hb)
    other_rows = pl.ds(pl.multiple_of((1 - core) * hb, hb), hb)

    def half(x):
        return jnp.where(core == 0, x[:hb], x[hb:])

    r_u, r_t, r_dm, r_dv, r_relay, r_c, r_e = (fresh(1) for _ in range(7))
    left = jnp.maximum(s - 2, core)
    forward = remote(uout, uin, r_u, slab=jnp.minimum(s + 2, ns - 2 + core))
    back = [remote(tout, tmid, r_t, slab=2 * c + core) for c in range(mid)]
    send_dm = remote(dm_out.at[rows], dm_in.at[rows], r_dm, slab=left)
    send_dv = remote(dv_out, dv_in, r_dv, slab=left)
    relay = remote(dm_in.at[rows], dm_in.at[rows], r_relay, slab=buddy)
    send_c = remote(c_out, c_in, r_c, slab=left)
    send_e = remote(e_out, e_in, r_e, slab=left)
    inner_left = jnp.logical_and(chip > 0, chip < mid)

    arrival(abs_.at[1 - core], r_ab).wait_recv()
    ab_l = split(abs_[0])
    zero_map = jnp.zeros((R, 2 * R), f32)
    ab = dot3(ab_l, embed(abs_[1, :R])) + jnp.concatenate([zero_map, abs_[1, R:]], axis=0)

    @pl.when(chip == 0)
    def _():
        uin[...] = jnp.zeros_like(uin)
        uout[...] = half(ab[R:])
        forward.start()

    arrival(cde.at[1 - core], r_cde).wait_recv()
    cl, dl, el = cde[0, 0], cde[0, 1], cde[0, 2]
    cr, dr, er = cde[1, 0], cde[1, 1], cde[1, 2]
    e_dr = embed(dr)
    g = dot3(ab_l, e_dr) + jnp.concatenate([zero_map, er], axis=0)
    gc = times(jnp.concatenate([g, cr], axis=0), embed(cl))
    chip_d = gc[: R + M] + jnp.concatenate([dl, el], axis=0)
    chip_c = gc[R + M :]

    d_half = half(chip_d[R:])
    b_half = half(ab[R:])

    @pl.when(chip == nc - 1)
    def _():
        dm_out[...] = chip_d[:R]
        dv_out[...] = d_half
        send_dm.start()
        send_dv.start()

    @pl.when(jnp.logical_and(chip >= mid, chip < nc - 1))
    def _():
        send_dm.wait_recv()
        relay.start()

        @pl.when(chip > mid)
        def _():
            arrival(dm_in.at[other_rows], r_relay).wait_recv()
            z = times(jnp.concatenate([ab[:R], b_half], axis=0), embed(dm_in[...]))
            send_dv.wait_recv()
            z_b = z[R:] + dv_in[...]
            out = times(jnp.concatenate([z[:R], z_b], axis=0), embed(chip_c))
            dm_out[...] = out[:R] + chip_d[:R]
            dv_out[...] = out[R:] + d_half
            send_dm.start()
            send_dv.start()

    @pl.when(chip == mid - 1)
    def _():
        c_out[...] = chip_c

    @pl.when(chip < mid - 1)
    def _():
        send_c.wait_recv()

        @pl.when(chip > 0)
        def _():
            c_out[...] = times(c_in[...], embed(chip_c))

    @pl.when(inner_left)
    def _():
        send_c.start()

    e_out_map = embed(ab[:R])
    e_d = embed(chip_d[:R])
    e_c = embed(chip_c)

    @pl.when(chip > 0)
    def _():
        forward.wait_recv()

    u_in = uin[...]
    us = split(u_in)

    @pl.when(chip == nc - 1)
    def _():
        t_buf[...] = jnp.zeros_like(t_buf)

    @pl.when(jnp.logical_and(chip > 0, chip < nc - 1))
    def _():
        u_out = dot3(us, e_out_map) + b_half
        uout[...] = u_out
        forward.start()

        @pl.when(chip >= mid)
        def _():
            const = dot3(us, e_d) + d_half

            @pl.when(chip == mid)
            def _():
                arrival(dm_in.at[other_rows], r_relay).wait_recv()
                send_dv.wait_recv()

            t_in = times(u_out, embed(dm_in[...])) + dv_in[...]
            t_buf[...] = t_in

            @pl.when(chip == mid)
            def _():
                tout[...] = times(t_in, e_c) + const
                for copy in back:
                    copy.start()

    r_cu = fresh(1)
    ufull[rows, :] = u_in
    cross_u = remote(ufull.at[rows], ufull.at[rows], r_cu, slab=buddy)
    cross_u.start()

    @pl.when(inner_left)
    def _():
        const = dot3(us, e_d) + d_half

        @pl.when(chip == mid - 1)
        def _():
            e_out[...] = const

        @pl.when(chip < mid - 1)
        def _():
            send_e.wait_recv()
            e_out[...] = times(e_in[...], e_c) + const

        send_e.start()

    @pl.when(chip == 0)
    def _():
        if mid > 1:
            send_e.wait_recv()

    wr, wi = w_ref[0, 0], w_ref[0, 1]

    def weighted(x):
        re, im = x[:, :R], x[:, R:]
        return wr * re - wi * im, -(wr * im + wi * re)

    arrival(ufull.at[other_rows], r_cu).wait_recv()
    u_chip = ufull[...]
    e_al = embed(abs_[0, :R])
    e_cr = embed(cr)
    u_left = times(u_chip, e_al) + abs_[0, R:]
    u_own = jnp.where(core == 0, u_chip, u_left)
    wu = split(jnp.concatenate(weighted(u_own), axis=1))
    f_left = jnp.concatenate([F[0, :, :R], F[1, :, :R]], axis=1)
    s_buf[...] = wr * src_re - wi * src_im + (nt(f_left, wu[0]) + nt(f_left, wu[1]))

    @pl.when(q != target)
    def _():
        send_b.start()

    t_const = times(dot3(us, e_al) + half(abs_[0, R:]), e_dr) + half(er)
    loads[6].wait()

    @pl.when(q == target)
    def _():
        on = split(0.5 * ON[...])
        onh[...] = on[0]
        onl[...] = on[1]

    @pl.when(chip < mid)
    def _():
        back[0].wait_recv()

        @pl.when(chip == mid - 1)
        def _():
            t_buf[...] = tmid[...]

        @pl.when(chip < mid - 1)
        def _():
            t_buf[...] = times(tmid[...], embed(c_in[...])) + e_in[...]

    t_in = t_buf[...]
    wt_out[1] = jnp.concatenate(weighted(t_in), axis=1)
    to_home = []
    for k in (1, 0):
        if k == 0:
            wt_out[0] = jnp.concatenate(weighted(times(t_in, e_cr) + t_const), axis=1)
        at = nq // 2 - 1 + k
        hop = lax.rem(q - at + nq, nq)
        mine = jnp.logical_and(q == at, core == k)
        copy = remote(wt_out.at[k], wt_in.at[hop, rows], r_wt[0] + 2 * hop + core,
                      quad=at, slab=jnp.where(mine, buddy, chip * 2 + k))
        to_home.append((mine, copy))

        @pl.when(mine)
        def _():
            wt_in[0, rows] = wt_out[k]

        @pl.when(jnp.logical_not(mine))
        def _():
            copy.start()

    r_sub, r_line = fresh(1), fresh(1)
    shares = [
        remote(s_buf.at[slice(p * qrows, (p + 1) * qrows)], land, r_sub, quad=p)
        for p in range(nq)
    ]
    r_red = [fresh(1) for _ in range(1, ns)]
    scatter = []
    for d in range(1, ns):
        to = lax.rem(s + d, ns)
        scatter.append(remote(red.at[to], red_in.at[d - 1], r_red[d - 1], quad=home(to), slab=to))
    line = [remote(full.at[s], full.at[s], r_line, quad=lax.rem(q + d, nq)) for d in range(1, nq)]

    @pl.when(q == target)
    def _():
        total = s_buf[...]
        for d in range(1, nq):
            arrival(b_in.at[d - 1], r_b[d - 1]).wait_recv()
            total += b_in[d - 1]
        for d in range(nq):
            if d > 0:
                arrival(p_in.at[d - 1], r_p[d - 1]).wait_recv()
            piece = split(p_out[...] if d == 0 else p_in[d - 1])
            ph[:, d * 2 * R : (d + 1) * 2 * R] = piece[0]
            pl_[:, d * 2 * R : (d + 1) * 2 * R] = piece[1]
        for d in range(nq):
            for k in (0, 1):
                if d > 0:
                    arrival(wt_in.at[d, k * hb : (k + 1) * hb], r_wt[2 * d + k]).wait_recv()
                else:
                    @pl.when(core != k)
                    def _():
                        arrival(wt_in.at[0, k * hb : (k + 1) * hb], r_wt[k]).wait_recv()
        zh, zl = split(jnp.concatenate([wt_in[d] for d in range(nq)], axis=1))
        total += nt(ph[...], zh) + (nt(ph[...], zl) + nt(pl_[...], zh))
        s_buf[...] = total
        for p in range(nq):
            @pl.when(q == p)
            def _():
                land[...] = s_buf[p * qrows : (p + 1) * qrows]

            @pl.when(q != p)
            def _():
                shares[p].start()
        ts = split(total)
        half_h = dot3((onh[...], onl[...]), ts)
        following = wt_in[0, :, :R]
        for d in range(1, nq):
            following += wt_in[d, :, :R]
        fs = split(following)
        upper = nt(vs[0], fs[0]) + (nt(vs[0], fs[1]) + nt(vs[1], fs[0]))
        weighted_rows = split(jnp.concatenate([half_h[top], half_h[last] + upper], axis=0))
        both = tuple(jnp.concatenate([a, b], axis=1) for a, b in zip(ts, weighted_rows))
        products = dot3(split(total.T), both)
        gram, x = products[:, :M], products[:, M:]
        proj = x + x.T

        at_row = lax.broadcasted_iota(jnp.int32, (M, M), 0)
        at_col = lax.broadcasted_iota(jnp.int32, (M, M), 1)
        tile = jnp.where(at_row <= at_col, gram, proj)
        diag = jnp.sum(jnp.where(at_row == at_col, proj, 0.0), axis=0, keepdims=True)
        diag = jnp.broadcast_to(diag, (8, M))
        for i in range(ns):
            red[i, :ch] = tile[i * ch : (i + 1) * ch]
            red[i, ch : ch + 8] = diag
        for copy in scatter:
            copy.start()
        part = red[s]
        for d in range(1, ns):
            scatter[d - 1].wait_recv()
            part += red_in[d - 1]
        full[s] = part
        for copy in line:
            copy.start()

    @pl.when(q != target)
    def _():
        arrival(full.at[s], r_line).wait_recv()
        shares[0].wait_recv()

    spread, r_spread = [], []
    for d in range(1, ns):
        r_spread.append(fresh(1))
        copy = remote(full.at[s], full.at[s], r_spread[-1], slab=lax.rem(s + d, ns))
        copy.start()
        spread.append(copy)
    sub_ref[0] = land[...]
    for d in range(1, ns):
        arrival(full.at[lax.rem(s - d + ns, ns)], r_spread[d - 1]).wait_recv()
    scale = 1.0 / (ns * B)
    for i in range(ns):
        tile_ref[i * ch : (i + 1) * ch, :] = full[i, :ch] * scale
    tile_ref[M : M + 8, :] = full[0, ch : ch + 8] * scale

    for copy in [pair_ab, pair_cde, cross_u] + spread:
        copy.wait_send()

    @pl.when(chip < nc - 1)
    def _():
        forward.wait_send()

    @pl.when(chip > mid)
    def _():
        send_dm.wait_send()
        send_dv.wait_send()

    @pl.when(jnp.logical_and(chip >= mid, chip < nc - 1))
    def _():
        relay.wait_send()

    @pl.when(inner_left)
    def _():
        send_c.wait_send()
        send_e.wait_send()

    @pl.when(chip == mid)
    def _():
        for copy in back:
            copy.wait_send()

    for mine, copy in to_home:
        @pl.when(jnp.logical_not(mine))
        def _():
            copy.wait_send()

    @pl.when(q != target)
    def _():
        send_p.wait_send()
        send_b.wait_send()

    @pl.when(q == target)
    def _():
        for copy in scatter + line:
            copy.wait_send()

        for p in range(nq):
            @pl.when(q != p)
            def _():
                shares[p].wait_send()


def unpack(sub_ref, tile_ref, out_ref, corr_ref, proj_ref):
    M = corr_ref.shape[0]
    out_ref[...] = sub_ref[...]
    tile = tile_ref[:M]
    diag = tile_ref[M : M + 1]
    at_row = lax.broadcasted_iota(jnp.int32, (M, M), 0)
    at_col = lax.broadcasted_iota(jnp.int32, (M, M), 1)
    flipped = tile.T
    corr_ref[...] = jnp.where(at_row <= at_col, tile, flipped)
    low = jnp.where(at_row > at_col, tile, flipped)
    proj_ref[...] = jnp.where(at_row == at_col, jnp.broadcast_to(diag, (M, M)), low)


def per_device(nq, ns, factors, onsite, coupling, vectors, quad_weight):
    B = factors.shape[3]
    R = coupling.shape[1]
    M = vectors.shape[2]
    hb, ch, qrows = M // 2, M // ns, B // nq
    sends = 13 + ns // 4 + nq + 2 * (ns - 1) + (nq - 1)
    recvs = 12 + 2 * (nq - 1) + 2 * nq + 2 * (ns - 1)
    vm = pltpu.VMEM
    in_hbm = pl.BlockSpec(memory_space=pltpu.HBM)
    here = pl.BlockSpec(memory_space=pltpu.VMEM)
    wide = vm((M, 2 * R), f32)
    thin = vm((hb, 2 * R), f32)
    sub, tile = pl.pallas_call(
        functools.partial(body, nq, ns),
        out_shape=(
            jax.ShapeDtypeStruct((1, qrows, M), f32),
            jax.ShapeDtypeStruct((M + 8, M), f32),
        ),
        in_specs=[in_hbm] * 4 + [pl.BlockSpec(memory_space=pltpu.SMEM)],
        out_specs=(here, here),
        scratch_shapes=[
            vm((2, B, B), bf16), vm((B, B), f32), vm((R, R), f32), vm((B, M), bf16),
            vm((B, B), bf16), vm((B, B), bf16),
            vm((2, R + M, 2 * R), f32), vm((2, 3, R, 2 * R), f32),
            thin, thin, thin, thin, wide, thin,
            wide, wide, thin, thin, wide, wide, thin, thin,
            vm((B, M), f32), vm((nq - 1, B, M), f32),
            vm((B, 2 * R), f32), vm((nq - 1, B, 2 * R), f32),
            vm((B, 2 * nq * R), bf16), vm((B, 2 * nq * R), bf16),
            vm((2, hb, 2 * R), f32), vm((nq, M, 2 * R), f32), vm((qrows, M), f32),
            vm((ns, ch + 8, M), f32), vm((ns - 1, ch + 8, M), f32), vm((ns, ch + 8, M), f32),
            pltpu.SemaphoreType.DMA((7,)),
            pltpu.SemaphoreType.DMA((sends,)),
            pltpu.SemaphoreType.DMA((recvs,)),
        ],
        compiler_params=pltpu.CompilerParams(
            collective_id=0, has_side_effects=True, vmem_limit_bytes=VMEM_BYTES
        ),
    )(factors, onsite, coupling, vectors, quad_weight)
    return pl.pallas_call(
        unpack,
        out_shape=(
            jax.ShapeDtypeStruct((1, qrows, M), f32),
            jax.ShapeDtypeStruct((M, M), f32),
            jax.ShapeDtypeStruct((M, M), f32),
        ),
        in_specs=[here, here],
        out_specs=(here, here, here),
        compiler_params=pltpu.CompilerParams(vmem_limit_bytes=VMEM_BYTES),
    )(sub, tile)


def solution(mesh):
    placed = (
        P("quad", "slab", None, None, None),
        P("slab", None, None),
        P("slab", None, None),
        P("slab", None, None),
        P("quad", None),
    )
    return jax.shard_map(
        functools.partial(per_device, mesh.shape["quad"], mesh.shape["slab"]),
        mesh=mesh,
        in_specs=placed,
        out_specs=(P("slab", "quad", None), P(), P()),
        check_vma=False,
    )
```

```python
import functools

import jax
import jax.numpy as jnp
from jax import lax
from jax.experimental import pallas as pl
from jax.experimental.pallas import tpu as pltpu
from jax.sharding import PartitionSpec as P

MESH = pl.DeviceIdType.MESH
f32, bf16 = jnp.float32, jnp.bfloat16
VMEM_BYTES = 64 * 2**20 - 64 * 2**10


def split(x):
    high = x.astype(bf16)
    return high, (x - high.astype(f32)).astype(bf16)


def mm(a, b):
    return jnp.dot(a, b, preferred_element_type=f32)


def dot3(a, b):
    (ah, al), (bh, bl) = a, b
    return mm(ah, bh) + (mm(ah, bl) + mm(al, bh))


def nt(a, b):
    return lax.dot_general(a, b, (((1,), (1,)), ((), ())), preferred_element_type=f32)


def tn(a, b):
    return lax.dot_general(a, b, (((0,), (0,)), ((), ())), preferred_element_type=f32)


def tn3(a, b):
    (ah, al), (bh, bl) = a, b
    return tn(ah, bh) + (tn(ah, bl) + tn(al, bh))


def embed(w):
    n = w.shape[1] // 2
    return split(
        jnp.concatenate([w, jnp.concatenate([-w[:, n:], w[:, :n]], axis=1)], axis=0)
    )


def times(x, e):
    return dot3(split(x), e)


def body(nq, ns, f_hbm, on_hbm, v_hbm, y_hbm, w_ref, sub_ref, tile_ref,
         F, ON, V, Y, onh, onl, abs_, cde, uin, uout, tmid, tout, ufull, t_buf,
         dm_in, dm_out, dv_in, dv_out, c_in, c_out, e_in, e_out, s_buf, b_in, p_in, ph, pl_,
         wt_out, wt_in, land, src, v_parts, s_parts, h_buf, red, red_in, full, lsem, ssem, rsem):
    B = F.shape[1]
    R = V.shape[0]
    M = Y.shape[1]
    hb = M // 2
    nc = ns // 2
    mid = nc // 2
    qrows = B // nq
    ch = M // ns
    q = lax.axis_index("quad")
    s = lax.axis_index("slab")
    chip = s // 2
    core = s % 2
    buddy = chip * 2 + (1 - core)

    def home(slab):
        return nq // 2 - 1 + slab % 2

    target = home(s)

    top, last = slice(0, B - R), slice(B - R, B)
    loads = [
        pltpu.make_async_copy(src, dst, lsem.at[i])
        for i, (src, dst) in enumerate([
            (y_hbm.at[0], Y), (v_hbm.at[0], V),
            (f_hbm.at[0, 0, 0, last], F.at[0, last]), (f_hbm.at[0, 0, 1, last], F.at[1, last]),
            (f_hbm.at[0, 0, 0, top], F.at[0, top]), (f_hbm.at[0, 0, 1, top], F.at[1, top]),
            (on_hbm.at[0], ON)])
    ]
    for copy in loads:
        copy.start()

    barrier = pltpu.get_barrier_semaphore()
    for d in range(1, ns):
        pl.semaphore_signal(barrier, inc=1, device_id={"slab": lax.rem(s + d, ns)}, device_id_type=MESH)
    for d in range(1, nq):
        pl.semaphore_signal(barrier, inc=1, device_id={"quad": lax.rem(q + d, nq)}, device_id_type=MESH)
        pl.semaphore_signal(
            barrier, inc=1, device_id={"quad": lax.rem(q + d, nq), "slab": buddy}, device_id_type=MESH)

    @pl.when(q == target)
    def _():
        for d in range(2, ns, 2):
            to = lax.rem(buddy + d, ns)
            pl.semaphore_signal(barrier, inc=1, device_id={"quad": home(to), "slab": to}, device_id_type=MESH)

    counts = [0, 0]

    def fresh(which):
        counts[which] += 1
        return counts[which] - 1

    def remote(src, dst, recv, **where):
        return pltpu.make_async_remote_copy(
            src_ref=src, dst_ref=dst, send_sem=ssem.at[fresh(0)], recv_sem=rsem.at[recv],
            device_id=where, device_id_type=MESH,
        )

    def arrival(dst, recv):
        return pltpu.make_async_remote_copy(
            src_ref=dst, dst_ref=dst, send_sem=ssem.at[0], recv_sem=rsem.at[recv],
            device_id={"slab": buddy}, device_id_type=MESH,
        )

    for copy in loads[:4]:
        copy.wait()
    y = Y[...]
    last_re = mm(F[0, last], y)
    last_im = mm(F[1, last], y)
    vs = split(V[...])
    vts = split(V[...].T)
    f21 = jnp.concatenate([F[0, last, :R], F[1, last, :R]], axis=1)
    a_cols = mm(vts[0], f21) + mm(vts[1], f21)
    s_last = split(jnp.concatenate([last_re, last_im], axis=1))
    b_cols = dot3(vts, s_last)
    abs_[core, :R] = jnp.concatenate([a_cols[:, :R].T, a_cols[:, R:].T], axis=1)
    abs_[core, R:] = jnp.concatenate([b_cols[:, :M].T, b_cols[:, M:].T], axis=1)

    base_wait = ns - 1 + 2 * (nq - 1)

    @pl.when(q == target)
    def _():
        pl.semaphore_wait(barrier, base_wait + ns // 2 - 1)

    @pl.when(q != target)
    def _():
        pl.semaphore_wait(barrier, base_wait)

    r_ab, r_cde = fresh(1), fresh(1)
    pair_ab = remote(abs_.at[core], abs_.at[core], r_ab, slab=buddy)
    pair_cde = remote(cde.at[core], cde.at[core], r_cde, slab=buddy)
    pair_ab.start()

    for copy in loads[4:6]:
        copy.wait()
    v_parts[0] = vs[0]
    v_parts[1] = vs[1]

    @pl.loop(0, 2)
    def _(part):
        lanes = pl.ds(pl.multiple_of(part * R, R), R)
        rows_src = mm(F[part], Y[...])
        src[part] = rows_src
        right = F[part, :, last]
        p_part = mm(right, v_parts[0]) + mm(right, v_parts[1])
        p_in[0, :, lanes] = p_part
        cde[core, 0, :, lanes] = p_part[:R].T
        cde[core, 1, :, lanes] = F[part, :R, :R].astype(f32).T
        cde[core, 2, :, lanes] = rows_src[:R].T

    pair_cde.start()
    r_p = [fresh(1) for _ in range(1, nq)]
    r_b = [fresh(1) for _ in range(1, nq)]
    r_wt = [fresh(1) for _ in range(2 * nq)]
    away = lax.rem(q - target + nq, nq)
    slot = jnp.maximum(away - 1, 0)
    send_p = remote(p_in.at[0], p_in.at[slot + 1], r_p[0] + slot, quad=target)
    send_b = remote(s_buf, b_in.at[slot], r_b[0] + slot, quad=target)

    @pl.when(q != target)
    def _():
        send_p.start()

    rows = pl.ds(pl.multiple_of(core * hb, hb), hb)
    other_rows = pl.ds(pl.multiple_of((1 - core) * hb, hb), hb)

    def half(x):
        return jnp.where(core == 0, x[:hb], x[hb:])

    r_u, r_t, r_dm, r_dv, r_relay, r_c, r_e = (fresh(1) for _ in range(7))
    left = jnp.maximum(s - 2, core)
    forward = remote(uout, uin, r_u, slab=jnp.minimum(s + 2, ns - 2 + core))
    back = [remote(tout, tmid, r_t, slab=2 * c + core) for c in range(mid)]
    send_dm = remote(dm_out.at[rows], dm_in.at[rows], r_dm, slab=left)
    send_dv = remote(dv_out, dv_in, r_dv, slab=left)
    relay = remote(dm_in.at[rows], dm_in.at[rows], r_relay, slab=buddy)
    send_c = remote(c_out, c_in, r_c, slab=left)
    send_e = remote(e_out, e_in, r_e, slab=left)
    inner_left = jnp.logical_and(chip > 0, chip < mid)

    arrival(abs_.at[1 - core], r_ab).wait_recv()
    ab_l = split(abs_[0])
    zero_map = jnp.zeros((R, 2 * R), f32)
    ab = dot3(ab_l, embed(abs_[1, :R])) + jnp.concatenate([zero_map, abs_[1, R:]], axis=0)

    @pl.when(chip == 0)
    def _():
        uin[...] = jnp.zeros_like(uin)
        uout[...] = half(ab[R:])
        forward.start()

    arrival(cde.at[1 - core], r_cde).wait_recv()
    cl, dl, el = cde[0, 0], cde[0, 1], cde[0, 2]
    cr, dr, er = cde[1, 0], cde[1, 1], cde[1, 2]
    e_dr = embed(dr)
    g = dot3(ab_l, e_dr) + jnp.concatenate([zero_map, er], axis=0)
    gc = times(jnp.concatenate([g, cr], axis=0), embed(cl))
    chip_d = gc[: R + M] + jnp.concatenate([dl, el], axis=0)
    chip_c = gc[R + M :]

    d_half = half(chip_d[R:])
    b_half = half(ab[R:])

    @pl.when(chip == nc - 1)
    def _():
        dm_out[...] = chip_d[:R]
        dv_out[...] = d_half
        send_dm.start()
        send_dv.start()

    @pl.when(jnp.logical_and(chip >= mid, chip < nc - 1))
    def _():
        send_dm.wait_recv()
        relay.start()

        @pl.when(chip > mid)
        def _():
            arrival(dm_in.at[other_rows], r_relay).wait_recv()
            z = times(jnp.concatenate([ab[:R], b_half], axis=0), embed(dm_in[...]))
            send_dv.wait_recv()
            z_b = z[R:] + dv_in[...]
            out = times(jnp.concatenate([z[:R], z_b], axis=0), embed(chip_c))
            dm_out[...] = out[:R] + chip_d[:R]
            dv_out[...] = out[R:] + d_half
            send_dm.start()
            send_dv.start()

    @pl.when(chip == mid - 1)
    def _():
        c_out[...] = chip_c

    @pl.when(chip < mid - 1)
    def _():
        send_c.wait_recv()

        @pl.when(chip > 0)
        def _():
            c_out[...] = times(c_in[...], embed(chip_c))

    @pl.when(inner_left)
    def _():
        send_c.start()

    e_out_map = embed(ab[:R])
    e_d = embed(chip_d[:R])
    e_c = embed(chip_c)

    @pl.when(chip > 0)
    def _():
        forward.wait_recv()

    u_in = uin[...]
    us = split(u_in)

    @pl.when(chip == nc - 1)
    def _():
        t_buf[...] = jnp.zeros_like(t_buf)

    @pl.when(jnp.logical_and(chip > 0, chip < nc - 1))
    def _():
        u_out = dot3(us, e_out_map) + b_half
        uout[...] = u_out
        forward.start()

        @pl.when(chip >= mid)
        def _():
            const = dot3(us, e_d) + d_half

            @pl.when(chip == mid)
            def _():
                arrival(dm_in.at[other_rows], r_relay).wait_recv()
                send_dv.wait_recv()

            t_in = times(u_out, embed(dm_in[...])) + dv_in[...]
            t_buf[...] = t_in

            @pl.when(chip == mid)
            def _():
                tout[...] = times(t_in, e_c) + const
                for copy in back:
                    copy.start()

    r_cu = fresh(1)
    ufull[rows, :] = u_in
    cross_u = remote(ufull.at[rows], ufull.at[rows], r_cu, slab=buddy)
    cross_u.start()

    @pl.when(inner_left)
    def _():
        const = dot3(us, e_d) + d_half

        @pl.when(chip == mid - 1)
        def _():
            e_out[...] = const

        @pl.when(chip < mid - 1)
        def _():
            send_e.wait_recv()
            e_out[...] = times(e_in[...], e_c) + const

        send_e.start()

    @pl.when(chip == 0)
    def _():
        if mid > 1:
            send_e.wait_recv()

    wr, wi = w_ref[0, 0], w_ref[0, 1]

    def weighted(x):
        re, im = x[:, :R], x[:, R:]
        return wr * re - wi * im, -(wr * im + wi * re)

    arrival(ufull.at[other_rows], r_cu).wait_recv()
    u_chip = ufull[...]
    e_al = embed(abs_[0, :R])
    e_cr = embed(cr)
    u_left = times(u_chip, e_al) + abs_[0, R:]
    u_own = jnp.where(core == 0, u_chip, u_left)
    wu = split(jnp.concatenate(weighted(u_own), axis=1))

    @pl.loop(0, 2)
    def _(part):
        some = pl.ds(pl.multiple_of(part * (B // 2), B // 2), B // 2)
        f_left = jnp.concatenate([F[0, some, :R], F[1, some, :R]], axis=1)
        s_buf[some, :] = wr * src[0, some] - wi * src[1, some] + (nt(f_left, wu[0]) + nt(f_left, wu[1]))

    @pl.when(q != target)
    def _():
        send_b.start()

    t_const = times(dot3(us, e_al) + half(abs_[0, R:]), e_dr) + half(er)
    loads[6].wait()

    @pl.when(q == target)
    def _():
        on = split(0.5 * ON[...])
        onh[...] = on[0]
        onl[...] = on[1]

    @pl.when(chip < mid)
    def _():
        back[0].wait_recv()

        @pl.when(chip == mid - 1)
        def _():
            t_buf[...] = tmid[...]

        @pl.when(chip < mid - 1)
        def _():
            t_buf[...] = times(tmid[...], embed(c_in[...])) + e_in[...]

    t_in = t_buf[...]
    wt_out[1] = jnp.concatenate(weighted(t_in), axis=1)
    to_home = []
    for k in (1, 0):
        if k == 0:
            wt_out[0] = jnp.concatenate(weighted(times(t_in, e_cr) + t_const), axis=1)
        at = nq // 2 - 1 + k
        hop = lax.rem(q - at + nq, nq)
        mine = jnp.logical_and(q == at, core == k)
        copy = remote(wt_out.at[k], wt_in.at[hop, rows], r_wt[0] + 2 * hop + core,
                      quad=at, slab=jnp.where(mine, buddy, chip * 2 + k))
        to_home.append((mine, copy))

        @pl.when(mine)
        def _():
            wt_in[0, rows] = wt_out[k]

        @pl.when(jnp.logical_not(mine))
        def _():
            copy.start()

    r_sub, r_line = fresh(1), fresh(1)
    shares = [
        remote(s_buf.at[slice(p * qrows, (p + 1) * qrows)], land, r_sub, quad=p)
        for p in range(nq)
    ]
    r_red = [fresh(1) for _ in range(1, ns)]
    scatter = []
    for d in range(1, ns):
        to = lax.rem(s + d, ns)
        scatter.append(remote(red.at[to], red_in.at[d - 1], r_red[d - 1], quad=home(to), slab=to))
    line = [remote(full.at[s], full.at[s], r_line, quad=lax.rem(q + d, nq)) for d in range(1, nq)]

    @pl.when(q == target)
    def _():
        for d in range(1, nq):
            arrival(b_in.at[d - 1], r_b[d - 1]).wait_recv()
            arrival(p_in.at[d], r_p[d - 1]).wait_recv()

        @pl.loop(0, nq)
        def _(d):
            piece = split(p_in[d])
            ph[d] = piece[0]
            pl_[d] = piece[1]

        @pl.loop(0, nq - 1)
        def _(d):
            s_buf[...] += b_in[d]

        for d in range(nq):
            for k in (0, 1):
                if d > 0:
                    arrival(wt_in.at[d, k * hb : (k + 1) * hb], r_wt[2 * d + k]).wait_recv()
                else:
                    @pl.when(core != k)
                    def _():
                        arrival(wt_in.at[0, k * hb : (k + 1) * hb], r_wt[k]).wait_recv()

        @pl.loop(0, nq)
        def _(d):
            zh, zl = split(wt_in[d])
            s_buf[...] += nt(ph[d], zh) + (nt(ph[d], zl) + nt(pl_[d], zh))

        total = s_buf[...]
        for p in range(nq):
            @pl.when(q == p)
            def _():
                land[...] = s_buf[p * qrows : (p + 1) * qrows]

            @pl.when(q != p)
            def _():
                shares[p].start()
        ts = split(total)
        s_parts[0] = ts[0]
        s_parts[1] = ts[1]

        @pl.loop(0, 2)
        def _(part):
            some = pl.ds(pl.multiple_of(part * (B // 2), B // 2), B // 2)
            h_buf[some, :] = dot3((onh[some, :], onl[some, :]), (s_parts[0], s_parts[1]))

        following = wt_in[0, :, :R]
        for d in range(1, nq):
            following += wt_in[d, :, :R]
        fs = split(following)
        upper = nt(vs[0], fs[0]) + (nt(vs[0], fs[1]) + nt(vs[1], fs[0]))
        weighted_rows = split(jnp.concatenate([h_buf[top], h_buf[last] + upper], axis=0))
        both = tuple(jnp.concatenate([a, b], axis=1) for a, b in zip(ts, weighted_rows))
        products = dot3(split(total.T), both)
        gram, x = products[:, :M], products[:, M:]
        proj = x + x.T

        at_row = lax.broadcasted_iota(jnp.int32, (M, M), 0)
        at_col = lax.broadcasted_iota(jnp.int32, (M, M), 1)
        tile = jnp.where(at_row <= at_col, gram, proj)
        diag = jnp.sum(jnp.where(at_row == at_col, proj, 0.0), axis=0, keepdims=True)
        diag = jnp.broadcast_to(diag, (8, M))
        for i in range(ns):
            red[i, :ch] = tile[i * ch : (i + 1) * ch]
            red[i, ch : ch + 8] = diag
        for copy in scatter:
            copy.start()
        part = red[s]
        for d in range(1, ns):
            scatter[d - 1].wait_recv()
            part += red_in[d - 1]
        full[s] = part
        for copy in line:
            copy.start()

    @pl.when(q != target)
    def _():
        arrival(full.at[s], r_line).wait_recv()
        shares[0].wait_recv()

    spread, r_spread = [], []
    for d in range(1, ns):
        r_spread.append(fresh(1))
        copy = remote(full.at[s], full.at[s], r_spread[-1], slab=lax.rem(s + d, ns))
        copy.start()
        spread.append(copy)
    sub_ref[0] = land[...]
    for d in range(1, ns):
        arrival(full.at[lax.rem(s - d + ns, ns)], r_spread[d - 1]).wait_recv()
    scale = 1.0 / (ns * B)
    for i in range(ns):
        tile_ref[i * ch : (i + 1) * ch, :] = full[i, :ch] * scale
    tile_ref[M : M + 8, :] = full[0, ch : ch + 8] * scale

    for copy in [pair_ab, pair_cde, cross_u] + spread:
        copy.wait_send()

    @pl.when(chip < nc - 1)
    def _():
        forward.wait_send()

    @pl.when(chip > mid)
    def _():
        send_dm.wait_send()
        send_dv.wait_send()

    @pl.when(jnp.logical_and(chip >= mid, chip < nc - 1))
    def _():
        relay.wait_send()

    @pl.when(inner_left)
    def _():
        send_c.wait_send()
        send_e.wait_send()

    @pl.when(chip == mid)
    def _():
        for copy in back:
            copy.wait_send()

    for mine, copy in to_home:
        @pl.when(jnp.logical_not(mine))
        def _():
            copy.wait_send()

    @pl.when(q != target)
    def _():
        send_p.wait_send()
        send_b.wait_send()

    @pl.when(q == target)
    def _():
        for copy in scatter + line:
            copy.wait_send()

        for p in range(nq):
            @pl.when(q != p)
            def _():
                shares[p].wait_send()


def unpack(sub_ref, tile_ref, out_ref, corr_ref, proj_ref):
    M = corr_ref.shape[0]
    out_ref[...] = sub_ref[...]
    tile = tile_ref[:M]
    diag = tile_ref[M : M + 1]
    at_row = lax.broadcasted_iota(jnp.int32, (M, M), 0)
    at_col = lax.broadcasted_iota(jnp.int32, (M, M), 1)
    flipped = tile.T
    corr_ref[...] = jnp.where(at_row <= at_col, tile, flipped)
    low = jnp.where(at_row > at_col, tile, flipped)
    proj_ref[...] = jnp.where(at_row == at_col, jnp.broadcast_to(diag, (M, M)), low)


def per_device(nq, ns, factors, onsite, coupling, vectors, quad_weight):
    B = factors.shape[3]
    R = coupling.shape[1]
    M = vectors.shape[2]
    hb, ch, qrows = M // 2, M // ns, B // nq
    sends = 13 + ns // 4 + nq + 2 * (ns - 1) + (nq - 1)
    recvs = 12 + 2 * (nq - 1) + 2 * nq + 2 * (ns - 1)
    vm = pltpu.VMEM
    in_hbm = pl.BlockSpec(memory_space=pltpu.HBM)
    here = pl.BlockSpec(memory_space=pltpu.VMEM)
    wide = vm((M, 2 * R), f32)
    thin = vm((hb, 2 * R), f32)
    sub, tile = pl.pallas_call(
        functools.partial(body, nq, ns),
        out_shape=(
            jax.ShapeDtypeStruct((1, qrows, M), f32),
            jax.ShapeDtypeStruct((M + 8, M), f32),
        ),
        in_specs=[in_hbm] * 4 + [pl.BlockSpec(memory_space=pltpu.SMEM)],
        out_specs=(here, here),
        scratch_shapes=[
            vm((2, B, B), bf16), vm((B, B), f32), vm((R, R), f32), vm((B, M), bf16),
            vm((B, B), bf16), vm((B, B), bf16),
            vm((2, R + M, 2 * R), f32), vm((2, 3, R, 2 * R), f32),
            thin, thin, thin, thin, wide, thin,
            wide, wide, thin, thin, wide, wide, thin, thin,
            vm((B, M), f32), vm((nq - 1, B, M), f32),
            vm((nq, B, 2 * R), f32),
            vm((nq, B, 2 * R), bf16), vm((nq, B, 2 * R), bf16),
            vm((2, hb, 2 * R), f32), vm((nq, M, 2 * R), f32), vm((qrows, M), f32),
            vm((2, B, M), f32), vm((2, R, R), bf16), vm((2, B, M), bf16), vm((B, M), f32),
            vm((ns, ch + 8, M), f32), vm((ns - 1, ch + 8, M), f32), vm((ns, ch + 8, M), f32),
            pltpu.SemaphoreType.DMA((7,)),
            pltpu.SemaphoreType.DMA((sends,)),
            pltpu.SemaphoreType.DMA((recvs,)),
        ],
        compiler_params=pltpu.CompilerParams(
            collective_id=0, has_side_effects=True, vmem_limit_bytes=VMEM_BYTES
        ),
    )(factors, onsite, coupling, vectors, quad_weight)
    return pl.pallas_call(
        unpack,
        out_shape=(
            jax.ShapeDtypeStruct((1, qrows, M), f32),
            jax.ShapeDtypeStruct((M, M), f32),
            jax.ShapeDtypeStruct((M, M), f32),
        ),
        in_specs=[here, here],
        out_specs=(here, here, here),
        compiler_params=pltpu.CompilerParams(vmem_limit_bytes=VMEM_BYTES),
    )(sub, tile)


def solution(mesh):
    placed = (
        P("quad", "slab", None, None, None),
        P("slab", None, None),
        P("slab", None, None),
        P("slab", None, None),
        P("quad", None),
    )
    return jax.shard_map(
        functools.partial(per_device, mesh.shape["quad"], mesh.shape["slab"]),
        mesh=mesh,
        in_specs=placed,
        out_specs=(P("slab", "quad", None), P(), P()),
        check_vma=False,
    )
```

```python
import functools

import jax
import jax.numpy as jnp
from jax import lax
from jax.experimental import pallas as pl
from jax.experimental.pallas import tpu as pltpu
from jax.sharding import PartitionSpec as P

MESH = pl.DeviceIdType.MESH
f32, bf16 = jnp.float32, jnp.bfloat16
VMEM_BYTES = 64 * 2**20 - 64 * 2**10


def split(x):
    high = x.astype(bf16)
    return high, (x - high.astype(f32)).astype(bf16)


def mm(a, b):
    return jnp.dot(a, b, preferred_element_type=f32)


def dot3(a, b):
    (ah, al), (bh, bl) = a, b
    return mm(ah, bh) + (mm(ah, bl) + mm(al, bh))


def nt(a, b):
    return lax.dot_general(a, b, (((1,), (1,)), ((), ())), preferred_element_type=f32)


def tn(a, b):
    return lax.dot_general(a, b, (((0,), (0,)), ((), ())), preferred_element_type=f32)


def tn3(a, b):
    (ah, al), (bh, bl) = a, b
    return tn(ah, bh) + (tn(ah, bl) + tn(al, bh))


def embed(w):
    n = w.shape[1] // 2
    return split(
        jnp.concatenate([w, jnp.concatenate([-w[:, n:], w[:, :n]], axis=1)], axis=0)
    )


def times(x, e):
    return dot3(split(x), e)


def body(nq, ns, f_hbm, on_hbm, v_hbm, y_hbm, w_ref, sub_ref, tile_ref,
         F, ON, V, Y, onh, onl, abs_, cde, uin, uout, tmid, tout, ufull, t_buf,
         dm_in, dm_out, dv_in, dv_out, c_in, c_out, e_in, e_out, s_buf, b_in, p_out, p_in, ph, pl_,
         wt_out, wt_in, land, red, red_in, full, lsem, ssem, rsem):
    B = F.shape[1]
    R = V.shape[0]
    M = Y.shape[1]
    hb = M // 2
    nc = ns // 2
    mid = nc // 2
    qrows = B // nq
    ch = M // ns
    q = lax.axis_index("quad")
    s = lax.axis_index("slab")
    chip = s // 2
    core = s % 2
    buddy = chip * 2 + (1 - core)

    def home(slab):
        return nq // 2 - 1 + slab % 2

    target = home(s)

    top, last = slice(0, B - R), slice(B - R, B)
    loads = [
        pltpu.make_async_copy(src, dst, lsem.at[i])
        for i, (src, dst) in enumerate([
            (y_hbm.at[0], Y), (v_hbm.at[0], V),
            (f_hbm.at[0, 0, 0, last], F.at[0, last]), (f_hbm.at[0, 0, 1, last], F.at[1, last]),
            (f_hbm.at[0, 0, 0, top], F.at[0, top]), (f_hbm.at[0, 0, 1, top], F.at[1, top]),
            (on_hbm.at[0], ON)])
    ]
    for copy in loads:
        copy.start()

    barrier = pltpu.get_barrier_semaphore()
    for d in range(1, ns):
        pl.semaphore_signal(barrier, inc=1, device_id={"slab": lax.rem(s + d, ns)}, device_id_type=MESH)
    for d in range(1, nq):
        pl.semaphore_signal(barrier, inc=1, device_id={"quad": lax.rem(q + d, nq)}, device_id_type=MESH)
        pl.semaphore_signal(
            barrier, inc=1, device_id={"quad": lax.rem(q + d, nq), "slab": buddy}, device_id_type=MESH)

    @pl.when(q == target)
    def _():
        for d in range(2, ns, 2):
            to = lax.rem(buddy + d, ns)
            pl.semaphore_signal(barrier, inc=1, device_id={"quad": home(to), "slab": to}, device_id_type=MESH)

    counts = [0, 0]

    def fresh(which):
        counts[which] += 1
        return counts[which] - 1

    def remote(src, dst, recv, **where):
        return pltpu.make_async_remote_copy(
            src_ref=src, dst_ref=dst, send_sem=ssem.at[fresh(0)], recv_sem=rsem.at[recv],
            device_id=where, device_id_type=MESH,
        )

    def arrival(dst, recv):
        return pltpu.make_async_remote_copy(
            src_ref=dst, dst_ref=dst, send_sem=ssem.at[0], recv_sem=rsem.at[recv],
            device_id={"slab": buddy}, device_id_type=MESH,
        )

    for copy in loads[:4]:
        copy.wait()
    y = Y[...]
    last_re = mm(F[0, last], y)
    last_im = mm(F[1, last], y)
    vs = split(V[...])
    vts = split(V[...].T)
    f21 = jnp.concatenate([F[0, last, :R], F[1, last, :R]], axis=1)
    a_cols = mm(vts[0], f21) + mm(vts[1], f21)
    s_last = split(jnp.concatenate([last_re, last_im], axis=1))
    b_cols = dot3(vts, s_last)
    abs_[core, :R] = jnp.concatenate([a_cols[:, :R].T, a_cols[:, R:].T], axis=1)
    abs_[core, R:] = jnp.concatenate([b_cols[:, :M].T, b_cols[:, M:].T], axis=1)

    base_wait = ns - 1 + 2 * (nq - 1)

    @pl.when(q == target)
    def _():
        pl.semaphore_wait(barrier, base_wait + ns // 2 - 1)

    @pl.when(q != target)
    def _():
        pl.semaphore_wait(barrier, base_wait)

    r_ab, r_cde = fresh(1), fresh(1)
    pair_ab = remote(abs_.at[core], abs_.at[core], r_ab, slab=buddy)
    pair_cde = remote(cde.at[core], cde.at[core], r_cde, slab=buddy)
    pair_ab.start()

    for copy in loads[4:6]:
        copy.wait()
    src_re = jnp.concatenate([mm(F[0, top], y), last_re], axis=0)
    src_im = jnp.concatenate([mm(F[1, top], y), last_im], axis=0)
    f_right = jnp.concatenate([F[0, :, last], F[1, :, last]], axis=0)
    p_rows = mm(f_right, vs[0]) + mm(f_right, vs[1])
    cde[core, 0] = jnp.concatenate([p_rows[:R].T, p_rows[B : B + R].T], axis=1)
    cde[core, 1] = jnp.concatenate(
        [F[0, :R, :R].astype(f32).T, F[1, :R, :R].astype(f32).T], axis=1
    )
    cde[core, 2] = jnp.concatenate([src_re[:R].T, src_im[:R].T], axis=1)
    pair_cde.start()
    p_out[...] = jnp.concatenate([p_rows[R:B], p_rows[B + R :]], axis=1)
    r_p = [fresh(1) for _ in range(1, nq)]
    r_b = [fresh(1) for _ in range(1, nq)]
    r_wt = [fresh(1) for _ in range(2 * nq)]
    away = lax.rem(q - target + nq, nq)
    slot = jnp.maximum(away - 1, 0)
    send_p = remote(p_out, p_in.at[slot], r_p[0] + slot, quad=target)
    send_b = remote(s_buf.at[R:], b_in.at[slot], r_b[0] + slot, quad=target)

    @pl.when(q != target)
    def _():
        send_p.start()

    rows = pl.ds(pl.multiple_of(core * hb, hb), hb)
    other_rows = pl.ds(pl.multiple_of((1 - core) * hb, hb), hb)

    def half(x):
        return jnp.where(core == 0, x[:hb], x[hb:])

    r_u, r_t, r_dm, r_dv, r_relay, r_c, r_e = (fresh(1) for _ in range(7))
    left = jnp.maximum(s - 2, core)
    forward = remote(uout, uin, r_u, slab=jnp.minimum(s + 2, ns - 2 + core))
    back = [remote(tout, tmid, r_t, slab=2 * c + core) for c in range(mid)]
    send_dm = remote(dm_out.at[rows], dm_in.at[rows], r_dm, slab=left)
    send_dv = remote(dv_out, dv_in, r_dv, slab=left)
    relay = remote(dm_in.at[rows], dm_in.at[rows], r_relay, slab=buddy)
    send_c = remote(c_out, c_in, r_c, slab=left)
    send_e = remote(e_out, e_in, r_e, slab=left)
    inner_left = jnp.logical_and(chip > 0, chip < mid)

    arrival(abs_.at[1 - core], r_ab).wait_recv()
    ab_l = split(abs_[0])
    zero_map = jnp.zeros((R, 2 * R), f32)
    ab = dot3(ab_l, embed(abs_[1, :R])) + jnp.concatenate([zero_map, abs_[1, R:]], axis=0)

    @pl.when(chip == 0)
    def _():
        uin[...] = jnp.zeros_like(uin)
        uout[...] = half(ab[R:])
        forward.start()

    arrival(cde.at[1 - core], r_cde).wait_recv()
    cl, dl, el = cde[0, 0], cde[0, 1], cde[0, 2]
    cr, dr, er = cde[1, 0], cde[1, 1], cde[1, 2]
    e_dr = embed(dr)
    g = dot3(ab_l, e_dr) + jnp.concatenate([zero_map, er], axis=0)
    gc = times(jnp.concatenate([g, cr], axis=0), embed(cl))
    chip_d = gc[: R + M] + jnp.concatenate([dl, el], axis=0)
    chip_c = gc[R + M :]

    d_half = half(chip_d[R:])
    b_half = half(ab[R:])

    @pl.when(chip == nc - 1)
    def _():
        dm_out[...] = chip_d[:R]
        dv_out[...] = d_half
        send_dm.start()
        send_dv.start()

    @pl.when(jnp.logical_and(chip >= mid, chip < nc - 1))
    def _():
        send_dm.wait_recv()
        relay.start()

        @pl.when(chip > mid)
        def _():
            arrival(dm_in.at[other_rows], r_relay).wait_recv()
            z = times(jnp.concatenate([ab[:R], b_half], axis=0), embed(dm_in[...]))
            send_dv.wait_recv()
            z_b = z[R:] + dv_in[...]
            out = times(jnp.concatenate([z[:R], z_b], axis=0), embed(chip_c))
            dm_out[...] = out[:R] + chip_d[:R]
            dv_out[...] = out[R:] + d_half
            send_dm.start()
            send_dv.start()

    @pl.when(chip == mid - 1)
    def _():
        c_out[...] = chip_c

    @pl.when(chip < mid - 1)
    def _():
        send_c.wait_recv()

        @pl.when(chip > 0)
        def _():
            c_out[...] = times(c_in[...], embed(chip_c))

    @pl.when(inner_left)
    def _():
        send_c.start()

    e_out_map = embed(ab[:R])
    e_d = embed(chip_d[:R])
    e_c = embed(chip_c)

    @pl.when(chip > 0)
    def _():
        forward.wait_recv()

    u_in = uin[...]
    us = split(u_in)

    @pl.when(chip == nc - 1)
    def _():
        t_buf[...] = jnp.zeros_like(t_buf)

    @pl.when(jnp.logical_and(chip > 0, chip < nc - 1))
    def _():
        u_out = dot3(us, e_out_map) + b_half
        uout[...] = u_out
        forward.start()

        @pl.when(chip >= mid)
        def _():
            const = dot3(us, e_d) + d_half

            @pl.when(chip == mid)
            def _():
                arrival(dm_in.at[other_rows], r_relay).wait_recv()
                send_dv.wait_recv()

            t_in = times(u_out, embed(dm_in[...])) + dv_in[...]
            t_buf[...] = t_in

            @pl.when(chip == mid)
            def _():
                tout[...] = times(t_in, e_c) + const
                for copy in back:
                    copy.start()

    r_cu = fresh(1)
    ufull[rows, :] = u_in
    cross_u = remote(ufull.at[rows], ufull.at[rows], r_cu, slab=buddy)
    cross_u.start()

    @pl.when(inner_left)
    def _():
        const = dot3(us, e_d) + d_half

        @pl.when(chip == mid - 1)
        def _():
            e_out[...] = const

        @pl.when(chip < mid - 1)
        def _():
            send_e.wait_recv()
            e_out[...] = times(e_in[...], e_c) + const

        send_e.start()

    @pl.when(chip == 0)
    def _():
        if mid > 1:
            send_e.wait_recv()

    wr, wi = w_ref[0, 0], w_ref[0, 1]

    def weighted(x):
        re, im = x[:, :R], x[:, R:]
        return wr * re - wi * im, -(wr * im + wi * re)

    arrival(ufull.at[other_rows], r_cu).wait_recv()
    u_chip = ufull[...]
    e_al = embed(abs_[0, :R])
    e_cr = embed(cr)
    u_left = times(u_chip, e_al) + abs_[0, R:]
    u_own = jnp.where(core == 0, u_chip, u_left)
    wu = split(jnp.concatenate(weighted(u_own), axis=1))
    f_left = jnp.concatenate([F[0, R:, :R], F[1, R:, :R]], axis=1)
    s_buf[R:, :] = wr * src_re[R:] - wi * src_im[R:] + (nt(f_left, wu[0]) + nt(f_left, wu[1]))

    @pl.when(q != target)
    def _():
        send_b.start()

    t_const = times(dot3(us, e_al) + half(abs_[0, R:]), e_dr) + half(er)
    first_const = dot3(us, e_d) + d_half
    e_both = tuple(jnp.concatenate([a, b], axis=1) for a, b in zip(e_cr, e_c))
    loads[6].wait()

    @pl.when(q == target)
    def _():
        on = split(0.5 * ON[...])
        onh[...] = on[0]
        onl[...] = on[1]

    @pl.when(chip < mid)
    def _():
        back[0].wait_recv()

        @pl.when(chip == mid - 1)
        def _():
            t_buf[...] = tmid[...]

        @pl.when(chip < mid - 1)
        def _():
            t_buf[...] = times(tmid[...], embed(c_in[...])) + e_in[...]

    t_in = t_buf[...]
    t_both = times(t_in, e_both)
    w_left = weighted(t_both[:, : 2 * R] + t_const)
    w_first = weighted(t_both[:, 2 * R :] + first_const)
    wt_out[1] = jnp.concatenate([*weighted(t_in), w_left[0]], axis=1)
    wt_out[0] = jnp.concatenate([*w_left, w_first[0]], axis=1)
    to_home = []
    for k in (1, 0):
        at = nq // 2 - 1 + k
        hop = lax.rem(q - at + nq, nq)
        mine = jnp.logical_and(q == at, core == k)
        copy = remote(wt_out.at[k], wt_in.at[hop, rows], r_wt[0] + 2 * hop + core,
                      quad=at, slab=jnp.where(mine, buddy, chip * 2 + k))
        to_home.append((mine, copy))

        @pl.when(mine)
        def _():
            wt_in[0, rows] = wt_out[k]

        @pl.when(jnp.logical_not(mine))
        def _():
            copy.start()

    r_sub, r_line = fresh(1), fresh(1)
    shares = [
        remote(s_buf.at[slice(p * qrows, (p + 1) * qrows)], land, r_sub, quad=p)
        for p in range(nq)
    ]
    r_red = [fresh(1) for _ in range(1, ns)]
    scatter = []
    for d in range(1, ns):
        to = lax.rem(s + d, ns)
        scatter.append(remote(red.at[to], red_in.at[d - 1], r_red[d - 1], quad=home(to), slab=to))
    line = [remote(full.at[s], full.at[s], r_line, quad=lax.rem(q + d, nq)) for d in range(1, nq)]

    @pl.when(q == target)
    def _():
        total = s_buf[R:, :]
        for d in range(1, nq):
            arrival(b_in.at[d - 1], r_b[d - 1]).wait_recv()
            total += b_in[d - 1]
        for d in range(nq):
            if d > 0:
                arrival(p_in.at[d - 1], r_p[d - 1]).wait_recv()
            piece = split(p_out[...] if d == 0 else p_in[d - 1])
            ph[:, d * 2 * R : (d + 1) * 2 * R] = piece[0]
            pl_[:, d * 2 * R : (d + 1) * 2 * R] = piece[1]
        for d in range(nq):
            for k in (0, 1):
                if d > 0:
                    arrival(wt_in.at[d, k * hb : (k + 1) * hb], r_wt[2 * d + k]).wait_recv()
                else:
                    @pl.when(core != k)
                    def _():
                        arrival(wt_in.at[0, k * hb : (k + 1) * hb], r_wt[k]).wait_recv()
        zh, zl = split(jnp.concatenate([wt_in[d, :, : 2 * R] for d in range(nq)], axis=1))
        total += nt(ph[...], zh) + (nt(ph[...], zl) + nt(pl_[...], zh))
        first = wt_in[0, :, 2 * R :]
        for d in range(1, nq):
            first += wt_in[d, :, 2 * R :]
        total = jnp.concatenate([first.T, total], axis=0)
        s_buf[...] = total
        for p in range(nq):
            @pl.when(q == p)
            def _():
                land[...] = s_buf[p * qrows : (p + 1) * qrows]

            @pl.when(q != p)
            def _():
                shares[p].start()
        ts = split(total)
        half_h = dot3((onh[...], onl[...]), ts)
        following = wt_in[0, :, :R]
        for d in range(1, nq):
            following += wt_in[d, :, :R]
        fs = split(following)
        upper = nt(vs[0], fs[0]) + (nt(vs[0], fs[1]) + nt(vs[1], fs[0]))
        weighted_rows = split(jnp.concatenate([half_h[top], half_h[last] + upper], axis=0))
        both = tuple(jnp.concatenate([a, b], axis=1) for a, b in zip(ts, weighted_rows))
        products = dot3(split(total.T), both)
        gram, x = products[:, :M], products[:, M:]
        proj = x + x.T

        at_row = lax.broadcasted_iota(jnp.int32, (M, M), 0)
        at_col = lax.broadcasted_iota(jnp.int32, (M, M), 1)
        tile = jnp.where(at_row <= at_col, gram, proj)
        diag = jnp.sum(jnp.where(at_row == at_col, proj, 0.0), axis=0, keepdims=True)
        diag = jnp.broadcast_to(diag, (8, M))
        for i in range(ns):
            red[i, :ch] = tile[i * ch : (i + 1) * ch]
            red[i, ch : ch + 8] = diag
        for copy in scatter:
            copy.start()
        part = red[s]
        for d in range(1, ns):
            scatter[d - 1].wait_recv()
            part += red_in[d - 1]
        full[s] = part
        for copy in line:
            copy.start()

    @pl.when(q != target)
    def _():
        arrival(full.at[s], r_line).wait_recv()
        shares[0].wait_recv()

    spread, r_spread = [], []
    for d in range(1, ns):
        r_spread.append(fresh(1))
        copy = remote(full.at[s], full.at[s], r_spread[-1], slab=lax.rem(s + d, ns))
        copy.start()
        spread.append(copy)
    sub_ref[0] = land[...]
    for d in range(1, ns):
        arrival(full.at[lax.rem(s - d + ns, ns)], r_spread[d - 1]).wait_recv()
    scale = 1.0 / (ns * B)
    for i in range(ns):
        tile_ref[i * ch : (i + 1) * ch, :] = full[i, :ch] * scale
    tile_ref[M : M + 8, :] = full[0, ch : ch + 8] * scale

    for copy in [pair_ab, pair_cde, cross_u] + spread:
        copy.wait_send()

    @pl.when(chip < nc - 1)
    def _():
        forward.wait_send()

    @pl.when(chip > mid)
    def _():
        send_dm.wait_send()
        send_dv.wait_send()

    @pl.when(jnp.logical_and(chip >= mid, chip < nc - 1))
    def _():
        relay.wait_send()

    @pl.when(inner_left)
    def _():
        send_c.wait_send()
        send_e.wait_send()

    @pl.when(chip == mid)
    def _():
        for copy in back:
            copy.wait_send()

    for mine, copy in to_home:
        @pl.when(jnp.logical_not(mine))
        def _():
            copy.wait_send()

    @pl.when(q != target)
    def _():
        send_p.wait_send()
        send_b.wait_send()

    @pl.when(q == target)
    def _():
        for copy in scatter + line:
            copy.wait_send()

        for p in range(nq):
            @pl.when(q != p)
            def _():
                shares[p].wait_send()


def unpack(sub_ref, tile_ref, out_ref, corr_ref, proj_ref):
    M = corr_ref.shape[0]
    out_ref[...] = sub_ref[...]
    tile = tile_ref[:M]
    diag = tile_ref[M : M + 1]
    at_row = lax.broadcasted_iota(jnp.int32, (M, M), 0)
    at_col = lax.broadcasted_iota(jnp.int32, (M, M), 1)
    flipped = tile.T
    corr_ref[...] = jnp.where(at_row <= at_col, tile, flipped)
    low = jnp.where(at_row > at_col, tile, flipped)
    proj_ref[...] = jnp.where(at_row == at_col, jnp.broadcast_to(diag, (M, M)), low)


def per_device(nq, ns, factors, onsite, coupling, vectors, quad_weight):
    B = factors.shape[3]
    R = coupling.shape[1]
    M = vectors.shape[2]
    hb, ch, qrows = M // 2, M // ns, B // nq
    sends = 13 + ns // 4 + nq + 2 * (ns - 1) + (nq - 1)
    recvs = 12 + 2 * (nq - 1) + 2 * nq + 2 * (ns - 1)
    vm = pltpu.VMEM
    in_hbm = pl.BlockSpec(memory_space=pltpu.HBM)
    here = pl.BlockSpec(memory_space=pltpu.VMEM)
    wide = vm((M, 2 * R), f32)
    thin = vm((hb, 2 * R), f32)
    sub, tile = pl.pallas_call(
        functools.partial(body, nq, ns),
        out_shape=(
            jax.ShapeDtypeStruct((1, qrows, M), f32),
            jax.ShapeDtypeStruct((M + 8, M), f32),
        ),
        in_specs=[in_hbm] * 4 + [pl.BlockSpec(memory_space=pltpu.SMEM)],
        out_specs=(here, here),
        scratch_shapes=[
            vm((2, B, B), bf16), vm((B, B), f32), vm((R, R), f32), vm((B, M), bf16),
            vm((B, B), bf16), vm((B, B), bf16),
            vm((2, R + M, 2 * R), f32), vm((2, 3, R, 2 * R), f32),
            thin, thin, thin, thin, wide, thin,
            wide, wide, thin, thin, wide, wide, thin, thin,
            vm((B, M), f32), vm((nq - 1, B - R, M), f32),
            vm((B - R, 2 * R), f32), vm((nq - 1, B - R, 2 * R), f32),
            vm((B - R, 2 * nq * R), bf16), vm((B - R, 2 * nq * R), bf16),
            vm((2, hb, 3 * R), f32), vm((nq, M, 3 * R), f32), vm((qrows, M), f32),
            vm((ns, ch + 8, M), f32), vm((ns - 1, ch + 8, M), f32), vm((ns, ch + 8, M), f32),
            pltpu.SemaphoreType.DMA((7,)),
            pltpu.SemaphoreType.DMA((sends,)),
            pltpu.SemaphoreType.DMA((recvs,)),
        ],
        compiler_params=pltpu.CompilerParams(
            collective_id=0, has_side_effects=True, vmem_limit_bytes=VMEM_BYTES
        ),
    )(factors, onsite, coupling, vectors, quad_weight)
    return pl.pallas_call(
        unpack,
        out_shape=(
            jax.ShapeDtypeStruct((1, qrows, M), f32),
            jax.ShapeDtypeStruct((M, M), f32),
            jax.ShapeDtypeStruct((M, M), f32),
        ),
        in_specs=[here, here],
        out_specs=(here, here, here),
        compiler_params=pltpu.CompilerParams(vmem_limit_bytes=VMEM_BYTES),
    )(sub, tile)


def solution(mesh):
    placed = (
        P("quad", "slab", None, None, None),
        P("slab", None, None),
        P("slab", None, None),
        P("slab", None, None),
        P("quad", None),
    )
    return jax.shard_map(
        functools.partial(per_device, mesh.shape["quad"], mesh.shape["slab"]),
        mesh=mesh,
        in_specs=placed,
        out_specs=(P("slab", "quad", None), P(), P()),
        check_vma=False,
    )
```

```python
import functools

import jax
import jax.numpy as jnp
from jax import lax
from jax.experimental import pallas as pl
from jax.experimental.pallas import tpu as pltpu
from jax.sharding import PartitionSpec as P

MESH = pl.DeviceIdType.MESH
f32, bf16 = jnp.float32, jnp.bfloat16
VMEM_BYTES = 64 * 2**20 - 64 * 2**10


def split(x):
    high = x.astype(bf16)
    return high, (x - high.astype(f32)).astype(bf16)


def mm(a, b):
    return jnp.dot(a, b, preferred_element_type=f32)


def dot3(a, b):
    (ah, al), (bh, bl) = a, b
    return mm(ah, bh) + (mm(ah, bl) + mm(al, bh))


def nt(a, b):
    return lax.dot_general(a, b, (((1,), (1,)), ((), ())), preferred_element_type=f32)


def tn(a, b):
    return lax.dot_general(a, b, (((0,), (0,)), ((), ())), preferred_element_type=f32)


def tn3(a, b):
    (ah, al), (bh, bl) = a, b
    return tn(ah, bh) + (tn(ah, bl) + tn(al, bh))


def embed(w):
    n = w.shape[1] // 2
    return split(
        jnp.concatenate([w, jnp.concatenate([-w[:, n:], w[:, :n]], axis=1)], axis=0)
    )


def times(x, e):
    return dot3(split(x), e)


def body(nq, ns, f_hbm, on_hbm, v_hbm, y_hbm, w_ref, sub_ref, tile_ref,
         F, ON, V, Y, onh, onl, abs_, cde, uin, uout, tmid, tout, ufull, t_buf,
         dm_in, dm_out, dv_in, dv_out, c_in, c_out, e_in, e_out, s_buf, b_in, p_out, p_in, ph, pl_,
         wt_out, wt_in, land, red, red_in, full, lsem, ssem, rsem):
    B = F.shape[1]
    R = V.shape[0]
    M = Y.shape[1]
    hb = M // 2
    nc = ns // 2
    mid = nc // 2
    qrows = B // nq
    ch = M // ns
    q = lax.axis_index("quad")
    s = lax.axis_index("slab")
    chip = s // 2
    core = s % 2
    buddy = chip * 2 + (1 - core)

    def home(slab):
        return nq // 2 - 1 + slab % 2

    target = home(s)

    top, last = slice(0, B - R), slice(B - R, B)
    loads = [
        pltpu.make_async_copy(src, dst, lsem.at[i])
        for i, (src, dst) in enumerate([
            (y_hbm.at[0], Y), (v_hbm.at[0], V),
            (f_hbm.at[0, 0, 0, last], F.at[0, last]), (f_hbm.at[0, 0, 1, last], F.at[1, last]),
            (f_hbm.at[0, 0, 0, top], F.at[0, top]), (f_hbm.at[0, 0, 1, top], F.at[1, top]),
            (on_hbm.at[0], ON)])
    ]
    for copy in loads:
        copy.start()

    barrier = pltpu.get_barrier_semaphore()
    for d in range(1, ns):
        pl.semaphore_signal(barrier, inc=1, device_id={"slab": lax.rem(s + d, ns)}, device_id_type=MESH)
    for d in range(1, nq):
        pl.semaphore_signal(barrier, inc=1, device_id={"quad": lax.rem(q + d, nq)}, device_id_type=MESH)
        pl.semaphore_signal(
            barrier, inc=1, device_id={"quad": lax.rem(q + d, nq), "slab": buddy}, device_id_type=MESH)

    @pl.when(q == target)
    def _():
        for d in range(2, ns, 2):
            to = lax.rem(buddy + d, ns)
            pl.semaphore_signal(barrier, inc=1, device_id={"quad": home(to), "slab": to}, device_id_type=MESH)

    counts = [0, 0]

    def fresh(which):
        counts[which] += 1
        return counts[which] - 1

    def remote(src, dst, recv, **where):
        return pltpu.make_async_remote_copy(
            src_ref=src, dst_ref=dst, send_sem=ssem.at[fresh(0)], recv_sem=rsem.at[recv],
            device_id=where, device_id_type=MESH,
        )

    def arrival(dst, recv):
        return pltpu.make_async_remote_copy(
            src_ref=dst, dst_ref=dst, send_sem=ssem.at[0], recv_sem=rsem.at[recv],
            device_id={"slab": buddy}, device_id_type=MESH,
        )

    for copy in loads[:4]:
        copy.wait()
    y = Y[...]
    last_re = mm(F[0, last], y)
    last_im = mm(F[1, last], y)
    vs = split(V[...])
    vts = split(V[...].T)
    f21 = jnp.concatenate([F[0, last, :R], F[1, last, :R]], axis=1)
    a_cols = mm(vts[0], f21) + mm(vts[1], f21)
    s_last = split(jnp.concatenate([last_re, last_im], axis=1))
    b_cols = dot3(vts, s_last)
    abs_[core, :R] = jnp.concatenate([a_cols[:, :R].T, a_cols[:, R:].T], axis=1)
    abs_[core, R:] = jnp.concatenate([b_cols[:, :M].T, b_cols[:, M:].T], axis=1)

    base_wait = ns - 1 + 2 * (nq - 1)

    @pl.when(q == target)
    def _():
        pl.semaphore_wait(barrier, base_wait + ns // 2 - 1)

    @pl.when(q != target)
    def _():
        pl.semaphore_wait(barrier, base_wait)

    r_ab, r_cde = fresh(1), fresh(1)
    pair_ab = remote(abs_.at[core], abs_.at[core], r_ab, slab=buddy)
    pair_cde = remote(cde.at[core], cde.at[core], r_cde, slab=buddy)
    pair_ab.start()

    for copy in loads[4:6]:
        copy.wait()
    src_re = jnp.concatenate([mm(F[0, top], y), last_re], axis=0)
    src_im = jnp.concatenate([mm(F[1, top], y), last_im], axis=0)
    f_right = jnp.concatenate([F[0, :, last], F[1, :, last]], axis=0)
    p_flat = nt(vts[0], f_right) + nt(vts[1], f_right)
    cde[core, 0] = jnp.concatenate([p_flat[:, :R], p_flat[:, B : B + R]], axis=1)
    cde[core, 1] = jnp.concatenate(
        [F[0, :R, :R].astype(f32).T, F[1, :R, :R].astype(f32).T], axis=1
    )
    cde[core, 2] = jnp.concatenate([src_re[:R].T, src_im[:R].T], axis=1)
    pair_cde.start()
    p_out[...] = jnp.concatenate([p_flat[:, R:B], p_flat[:, B + R :]], axis=0)
    r_p = [fresh(1) for _ in range(1, nq)]
    r_b = [fresh(1) for _ in range(1, nq)]
    r_wt = [fresh(1) for _ in range(2 * nq)]
    away = lax.rem(q - target + nq, nq)
    slot = jnp.maximum(away - 1, 0)
    send_p = remote(p_out, p_in.at[slot], r_p[0] + slot, quad=target)
    send_b = remote(s_buf.at[R:], b_in.at[slot], r_b[0] + slot, quad=target)

    @pl.when(q != target)
    def _():
        send_p.start()

    rows = pl.ds(pl.multiple_of(core * hb, hb), hb)
    other_rows = pl.ds(pl.multiple_of((1 - core) * hb, hb), hb)

    def half(x):
        return jnp.where(core == 0, x[:hb], x[hb:])

    r_u, r_t, r_dm, r_dv, r_relay, r_c, r_e = (fresh(1) for _ in range(7))
    left = jnp.maximum(s - 2, core)
    forward = remote(uout, uin, r_u, slab=jnp.minimum(s + 2, ns - 2 + core))
    back = [remote(tout, tmid, r_t, slab=2 * c + core) for c in range(mid)]
    send_dm = remote(dm_out.at[rows], dm_in.at[rows], r_dm, slab=left)
    send_dv = remote(dv_out, dv_in, r_dv, slab=left)
    relay = remote(dm_in.at[rows], dm_in.at[rows], r_relay, slab=buddy)
    send_c = remote(c_out, c_in, r_c, slab=left)
    send_e = remote(e_out, e_in, r_e, slab=left)
    inner_left = jnp.logical_and(chip > 0, chip < mid)

    arrival(abs_.at[1 - core], r_ab).wait_recv()
    ab_l = split(abs_[0])
    zero_map = jnp.zeros((R, 2 * R), f32)
    ab = dot3(ab_l, embed(abs_[1, :R])) + jnp.concatenate([zero_map, abs_[1, R:]], axis=0)

    @pl.when(chip == 0)
    def _():
        uin[...] = jnp.zeros_like(uin)
        uout[...] = half(ab[R:])
        forward.start()

    arrival(cde.at[1 - core], r_cde).wait_recv()
    cl, dl, el = cde[0, 0], cde[0, 1], cde[0, 2]
    cr, dr, er = cde[1, 0], cde[1, 1], cde[1, 2]
    e_dr = embed(dr)
    g = dot3(ab_l, e_dr) + jnp.concatenate([zero_map, er], axis=0)
    gc = times(jnp.concatenate([g, cr], axis=0), embed(cl))
    chip_d = gc[: R + M] + jnp.concatenate([dl, el], axis=0)
    chip_c = gc[R + M :]

    d_half = half(chip_d[R:])
    b_half = half(ab[R:])

    @pl.when(chip == nc - 1)
    def _():
        dm_out[...] = chip_d[:R]
        dv_out[...] = d_half
        send_dm.start()
        send_dv.start()

    @pl.when(jnp.logical_and(chip >= mid, chip < nc - 1))
    def _():
        send_dm.wait_recv()
        relay.start()

        @pl.when(chip > mid)
        def _():
            arrival(dm_in.at[other_rows], r_relay).wait_recv()
            z = times(jnp.concatenate([ab[:R], b_half], axis=0), embed(dm_in[...]))
            send_dv.wait_recv()
            z_b = z[R:] + dv_in[...]
            out = times(jnp.concatenate([z[:R], z_b], axis=0), embed(chip_c))
            dm_out[...] = out[:R] + chip_d[:R]
            dv_out[...] = out[R:] + d_half
            send_dm.start()
            send_dv.start()

    @pl.when(chip == mid - 1)
    def _():
        c_out[...] = chip_c

    @pl.when(chip < mid - 1)
    def _():
        send_c.wait_recv()

        @pl.when(chip > 0)
        def _():
            c_out[...] = times(c_in[...], embed(chip_c))

    @pl.when(inner_left)
    def _():
        send_c.start()

    e_out_map = embed(ab[:R])
    e_d = embed(chip_d[:R])
    e_c = embed(chip_c)

    @pl.when(chip > 0)
    def _():
        forward.wait_recv()

    u_in = uin[...]
    us = split(u_in)

    @pl.when(chip == nc - 1)
    def _():
        t_buf[...] = jnp.zeros_like(t_buf)

    @pl.when(jnp.logical_and(chip > 0, chip < nc - 1))
    def _():
        u_out = dot3(us, e_out_map) + b_half
        uout[...] = u_out
        forward.start()

        @pl.when(chip >= mid)
        def _():
            const = dot3(us, e_d) + d_half

            @pl.when(chip == mid)
            def _():
                arrival(dm_in.at[other_rows], r_relay).wait_recv()
                send_dv.wait_recv()

            t_in = times(u_out, embed(dm_in[...])) + dv_in[...]
            t_buf[...] = t_in

            @pl.when(chip == mid)
            def _():
                tout[...] = times(t_in, e_c) + const
                for copy in back:
                    copy.start()

    r_cu = fresh(1)
    ufull[rows, :] = u_in
    cross_u = remote(ufull.at[rows], ufull.at[rows], r_cu, slab=buddy)
    cross_u.start()

    @pl.when(inner_left)
    def _():
        const = dot3(us, e_d) + d_half

        @pl.when(chip == mid - 1)
        def _():
            e_out[...] = const

        @pl.when(chip < mid - 1)
        def _():
            send_e.wait_recv()
            e_out[...] = times(e_in[...], e_c) + const

        send_e.start()

    @pl.when(chip == 0)
    def _():
        if mid > 1:
            send_e.wait_recv()

    wr, wi = w_ref[0, 0], w_ref[0, 1]

    def weighted(x):
        re, im = x[:, :R], x[:, R:]
        return wr * re - wi * im, -(wr * im + wi * re)

    arrival(ufull.at[other_rows], r_cu).wait_recv()
    u_chip = ufull[...]
    e_al = embed(abs_[0, :R])
    e_cr = embed(cr)
    u_left = times(u_chip, e_al) + abs_[0, R:]
    u_own = jnp.where(core == 0, u_chip, u_left)
    wu = split(jnp.concatenate(weighted(u_own), axis=1))
    f_left = jnp.concatenate([F[0, R:, :R], F[1, R:, :R]], axis=1)
    s_buf[R:, :] = wr * src_re[R:] - wi * src_im[R:] + (nt(f_left, wu[0]) + nt(f_left, wu[1]))

    @pl.when(q != target)
    def _():
        send_b.start()

    t_const = times(dot3(us, e_al) + half(abs_[0, R:]), e_dr) + half(er)
    first_const = dot3(us, e_d) + d_half
    e_both = tuple(jnp.concatenate([a, b], axis=1) for a, b in zip(e_cr, e_c))
    loads[6].wait()

    @pl.when(q == target)
    def _():
        on = split(0.5 * ON[...])
        onh[...] = on[0]
        onl[...] = on[1]

    @pl.when(chip == mid - 1)
    def _():
        back[0].wait_recv()
        t_buf[...] = tmid[...]

    @pl.when(chip < mid - 1)
    def _():
        e_cin = embed(c_in[...])
        back[0].wait_recv()
        t_buf[...] = times(tmid[...], e_cin) + e_in[...]

    t_in = t_buf[...]
    t_both = times(t_in, e_both)
    w_left = weighted(t_both[:, : 2 * R] + t_const)
    w_first = weighted(t_both[:, 2 * R :] + first_const)
    wt_out[1] = jnp.concatenate([*weighted(t_in), w_left[0]], axis=1)
    wt_out[0] = jnp.concatenate([*w_left, w_first[0]], axis=1)
    to_home = []
    for k in (1, 0):
        at = nq // 2 - 1 + k
        hop = lax.rem(q - at + nq, nq)
        mine = jnp.logical_and(q == at, core == k)
        copy = remote(wt_out.at[k], wt_in.at[hop, rows], r_wt[0] + 2 * hop + core,
                      quad=at, slab=jnp.where(mine, buddy, chip * 2 + k))
        to_home.append((mine, copy))

        @pl.when(mine)
        def _():
            wt_in[0, rows] = wt_out[k]

        @pl.when(jnp.logical_not(mine))
        def _():
            copy.start()

    r_sub, r_line = fresh(1), fresh(1)
    shares = [
        remote(s_buf.at[slice(p * qrows, (p + 1) * qrows)], land, r_sub, quad=p)
        for p in range(nq)
    ]
    r_red = [fresh(1) for _ in range(1, ns)]
    scatter = []
    for d in range(1, ns):
        to = lax.rem(s + d, ns)
        scatter.append(remote(red.at[to], red_in.at[d - 1], r_red[d - 1], quad=home(to), slab=to))
    line = [remote(full.at[s], full.at[s], r_line, quad=lax.rem(q + d, nq)) for d in range(1, nq)]

    @pl.when(q == target)
    def _():
        total = s_buf[R:, :]
        for d in range(1, nq):
            arrival(b_in.at[d - 1], r_b[d - 1]).wait_recv()
            total += b_in[d - 1]
        total = total.T
        for d in range(nq):
            if d > 0:
                arrival(p_in.at[d - 1], r_p[d - 1]).wait_recv()
            piece = split(p_out[...] if d == 0 else p_in[d - 1])
            ph[d * 2 * R : (d + 1) * 2 * R] = piece[0]
            pl_[d * 2 * R : (d + 1) * 2 * R] = piece[1]
        for d in range(nq):
            for k in (0, 1):
                if d > 0:
                    arrival(wt_in.at[d, k * hb : (k + 1) * hb], r_wt[2 * d + k]).wait_recv()
                else:
                    @pl.when(core != k)
                    def _():
                        arrival(wt_in.at[0, k * hb : (k + 1) * hb], r_wt[k]).wait_recv()
        zh, zl = split(jnp.concatenate([wt_in[d, :, : 2 * R] for d in range(nq)], axis=1))
        total += mm(zh, ph[...]) + (mm(zl, ph[...]) + mm(zh, pl_[...]))
        first = wt_in[0, :, 2 * R :]
        for d in range(1, nq):
            first += wt_in[d, :, 2 * R :]
        flipped = jnp.concatenate([first, total], axis=1)
        fs = split(flipped)
        half_h = dot3(fs, (onh[...], onl[...]))
        total = flipped.T
        s_buf[...] = total
        for p in range(nq):
            @pl.when(q == p)
            def _():
                land[...] = s_buf[p * qrows : (p + 1) * qrows]

            @pl.when(q != p)
            def _():
                shares[p].start()
        ts = split(total)
        following = wt_in[0, :, :R]
        for d in range(1, nq):
            following += wt_in[d, :, :R]
        upper = dot3(split(following), vts)
        weighted_rows = split(jnp.concatenate([half_h[:, top], half_h[:, last] + upper], axis=1))
        both = tuple(jnp.concatenate([a, b], axis=0) for a, b in zip(fs, weighted_rows))
        products = dot3(both, ts)
        gram, x = products[:M], products[M:]
        proj = x + x.T

        at_row = lax.broadcasted_iota(jnp.int32, (M, M), 0)
        at_col = lax.broadcasted_iota(jnp.int32, (M, M), 1)
        tile = jnp.where(at_row <= at_col, gram, proj)
        diag = jnp.sum(jnp.where(at_row == at_col, proj, 0.0), axis=0, keepdims=True)
        diag = jnp.broadcast_to(diag, (8, M))
        for i in range(ns):
            red[i, :ch] = tile[i * ch : (i + 1) * ch]
            red[i, ch : ch + 8] = diag
        for copy in scatter:
            copy.start()
        part = red[s]
        for d in range(1, ns):
            scatter[d - 1].wait_recv()
            part += red_in[d - 1]
        full[s] = part
        for copy in line:
            copy.start()

    @pl.when(q != target)
    def _():
        arrival(full.at[s], r_line).wait_recv()
        shares[0].wait_recv()

    spread, r_spread = [], []
    for d in range(1, ns):
        r_spread.append(fresh(1))
        copy = remote(full.at[s], full.at[s], r_spread[-1], slab=lax.rem(s + d, ns))
        copy.start()
        spread.append(copy)
    sub_ref[0] = land[...]
    for d in range(1, ns):
        arrival(full.at[lax.rem(s - d + ns, ns)], r_spread[d - 1]).wait_recv()
    scale = 1.0 / (ns * B)
    for i in range(ns):
        tile_ref[i * ch : (i + 1) * ch, :] = full[i, :ch] * scale
    tile_ref[M : M + 8, :] = full[0, ch : ch + 8] * scale

    for copy in [pair_ab, pair_cde, cross_u] + spread:
        copy.wait_send()

    @pl.when(chip < nc - 1)
    def _():
        forward.wait_send()

    @pl.when(chip > mid)
    def _():
        send_dm.wait_send()
        send_dv.wait_send()

    @pl.when(jnp.logical_and(chip >= mid, chip < nc - 1))
    def _():
        relay.wait_send()

    @pl.when(inner_left)
    def _():
        send_c.wait_send()
        send_e.wait_send()

    @pl.when(chip == mid)
    def _():
        for copy in back:
            copy.wait_send()

    for mine, copy in to_home:
        @pl.when(jnp.logical_not(mine))
        def _():
            copy.wait_send()

    @pl.when(q != target)
    def _():
        send_p.wait_send()
        send_b.wait_send()

    @pl.when(q == target)
    def _():
        for copy in scatter + line:
            copy.wait_send()

        for p in range(nq):
            @pl.when(q != p)
            def _():
                shares[p].wait_send()


def unpack(sub_ref, tile_ref, out_ref, corr_ref, proj_ref):
    M = corr_ref.shape[0]
    out_ref[...] = sub_ref[...]
    tile = tile_ref[:M]
    diag = tile_ref[M : M + 1]
    at_row = lax.broadcasted_iota(jnp.int32, (M, M), 0)
    at_col = lax.broadcasted_iota(jnp.int32, (M, M), 1)
    flipped = tile.T
    corr_ref[...] = jnp.where(at_row <= at_col, tile, flipped)
    low = jnp.where(at_row > at_col, tile, flipped)
    proj_ref[...] = jnp.where(at_row == at_col, jnp.broadcast_to(diag, (M, M)), low)


def per_device(nq, ns, factors, onsite, coupling, vectors, quad_weight):
    B = factors.shape[3]
    R = coupling.shape[1]
    M = vectors.shape[2]
    hb, ch, qrows = M // 2, M // ns, B // nq
    sends = 13 + ns // 4 + nq + 2 * (ns - 1) + (nq - 1)
    recvs = 12 + 2 * (nq - 1) + 2 * nq + 2 * (ns - 1)
    vm = pltpu.VMEM
    in_hbm = pl.BlockSpec(memory_space=pltpu.HBM)
    here = pl.BlockSpec(memory_space=pltpu.VMEM)
    wide = vm((M, 2 * R), f32)
    thin = vm((hb, 2 * R), f32)
    sub, tile = pl.pallas_call(
        functools.partial(body, nq, ns),
        out_shape=(
            jax.ShapeDtypeStruct((1, qrows, M), f32),
            jax.ShapeDtypeStruct((M + 8, M), f32),
        ),
        in_specs=[in_hbm] * 4 + [pl.BlockSpec(memory_space=pltpu.SMEM)],
        out_specs=(here, here),
        scratch_shapes=[
            vm((2, B, B), bf16), vm((B, B), f32), vm((R, R), f32), vm((B, M), bf16),
            vm((B, B), bf16), vm((B, B), bf16),
            vm((2, R + M, 2 * R), f32), vm((2, 3, R, 2 * R), f32),
            thin, thin, thin, thin, wide, thin,
            wide, wide, thin, thin, wide, wide, thin, thin,
            vm((B, M), f32), vm((nq - 1, B - R, M), f32),
            vm((2 * R, B - R), f32), vm((nq - 1, 2 * R, B - R), f32),
            vm((2 * nq * R, B - R), bf16), vm((2 * nq * R, B - R), bf16),
            vm((2, hb, 3 * R), f32), vm((nq, M, 3 * R), f32), vm((qrows, M), f32),
            vm((ns, ch + 8, M), f32), vm((ns - 1, ch + 8, M), f32), vm((ns, ch + 8, M), f32),
            pltpu.SemaphoreType.DMA((7,)),
            pltpu.SemaphoreType.DMA((sends,)),
            pltpu.SemaphoreType.DMA((recvs,)),
        ],
        compiler_params=pltpu.CompilerParams(
            collective_id=0, has_side_effects=True, vmem_limit_bytes=VMEM_BYTES
        ),
    )(factors, onsite, coupling, vectors, quad_weight)
    return pl.pallas_call(
        unpack,
        out_shape=(
            jax.ShapeDtypeStruct((1, qrows, M), f32),
            jax.ShapeDtypeStruct((M, M), f32),
            jax.ShapeDtypeStruct((M, M), f32),
        ),
        in_specs=[here, here],
        out_specs=(here, here, here),
        compiler_params=pltpu.CompilerParams(vmem_limit_bytes=VMEM_BYTES),
    )(sub, tile)


def solution(mesh):
    placed = (
        P("quad", "slab", None, None, None),
        P("slab", None, None),
        P("slab", None, None),
        P("slab", None, None),
        P("quad", None),
    )
    return jax.shard_map(
        functools.partial(per_device, mesh.shape["quad"], mesh.shape["slab"]),
        mesh=mesh,
        in_specs=placed,
        out_specs=(P("slab", "quad", None), P(), P()),
        check_vma=False,
    )
```

```python
import functools

import jax
import jax.numpy as jnp
from jax import lax
from jax.experimental import pallas as pl
from jax.experimental.pallas import tpu as pltpu
from jax.sharding import PartitionSpec as P

MESH = pl.DeviceIdType.MESH
f32, bf16 = jnp.float32, jnp.bfloat16
VMEM_BYTES = 64 * 2**20 - 64 * 2**10


def split(x):
    high = x.astype(bf16)
    return high, (x - high.astype(f32)).astype(bf16)


def mm(a, b):
    return jnp.dot(a, b, preferred_element_type=f32)


def dot3(a, b):
    (ah, al), (bh, bl) = a, b
    return mm(ah, bh) + (mm(ah, bl) + mm(al, bh))


def nt(a, b):
    return lax.dot_general(a, b, (((1,), (1,)), ((), ())), preferred_element_type=f32)


def tn(a, b):
    return lax.dot_general(a, b, (((0,), (0,)), ((), ())), preferred_element_type=f32)


def tn3(a, b):
    (ah, al), (bh, bl) = a, b
    return tn(ah, bh) + (tn(ah, bl) + tn(al, bh))


def embed(w):
    n = w.shape[1] // 2
    return split(
        jnp.concatenate([w, jnp.concatenate([-w[:, n:], w[:, :n]], axis=1)], axis=0)
    )


def times(x, e):
    return dot3(split(x), e)


def body(nq, ns, f_hbm, on_hbm, v_hbm, y_hbm, w_ref, sub_ref, tile_ref,
         F, ON, V, Y, onh, onl, abs_, cde, uin, uout, tmid, tout, ufull, t_buf,
         dm_in, dm_out, dv_in, dv_out, c_in, c_out, e_in, e_out, s_buf, b_in, p_out, p_in, ph, pl_,
         wt_out, wt_in, land, red, red_in, full, lsem, ssem, rsem, bsem):
    B = F.shape[1]
    R = V.shape[0]
    M = Y.shape[1]
    hb = M // 2
    nc = ns // 2
    mid = nc // 2
    qrows = B // nq
    ch = M // ns
    q = lax.axis_index("quad")
    s = lax.axis_index("slab")
    chip = s // 2
    core = s % 2
    buddy = chip * 2 + (1 - core)

    def home(slab):
        return nq // 2 - 1 + slab % 2

    target = home(s)

    top, last = slice(0, B - R), slice(B - R, B)
    loads = [
        pltpu.make_async_copy(src, dst, lsem.at[i])
        for i, (src, dst) in enumerate([
            (y_hbm.at[0], Y), (v_hbm.at[0], V),
            (f_hbm.at[0, 0, 0, last], F.at[0, last]), (f_hbm.at[0, 0, 1, last], F.at[1, last]),
            (f_hbm.at[0, 0, 0, top], F.at[0, top]), (f_hbm.at[0, 0, 1, top], F.at[1, top]),
            (on_hbm.at[0], ON)])
    ]
    for copy in loads:
        copy.start()

    barrier = pltpu.get_barrier_semaphore()
    others = ns * nq - 1

    def peer(i):
        to = lax.rem(q * ns + s + 1 + i, ns * nq)
        return {"quad": to // ns, "slab": lax.rem(to, ns)}

    @pl.loop(0, others)
    def _(i):
        pl.semaphore_signal(barrier, inc=1, device_id=peer(i), device_id_type=MESH)

    counts = [0, 0]

    def fresh(which):
        counts[which] += 1
        return counts[which] - 1

    def remote(src, dst, recv, **where):
        return pltpu.make_async_remote_copy(
            src_ref=src, dst_ref=dst, send_sem=ssem.at[fresh(0)], recv_sem=rsem.at[recv],
            device_id=where, device_id_type=MESH,
        )

    def arrival(dst, recv):
        return pltpu.make_async_remote_copy(
            src_ref=dst, dst_ref=dst, send_sem=ssem.at[0], recv_sem=rsem.at[recv],
            device_id={"slab": buddy}, device_id_type=MESH,
        )

    for copy in loads[:4]:
        copy.wait()
    y = Y[...]
    last_re = mm(F[0, last], y)
    last_im = mm(F[1, last], y)
    vs = split(V[...])
    vts = split(V[...].T)
    f21 = jnp.concatenate([F[0, last, :R], F[1, last, :R]], axis=1)
    a_cols = mm(vts[0], f21) + mm(vts[1], f21)
    s_last = split(jnp.concatenate([last_re, last_im], axis=1))
    b_cols = dot3(vts, s_last)
    abs_[core, :R] = jnp.concatenate([a_cols[:, :R].T, a_cols[:, R:].T], axis=1)
    abs_[core, R:] = jnp.concatenate([b_cols[:, :M].T, b_cols[:, M:].T], axis=1)

    pl.semaphore_wait(barrier, others)

    r_ab, r_cde = fresh(1), fresh(1)
    pair_ab = remote(abs_.at[core], abs_.at[core], r_ab, slab=buddy)
    pair_cde = remote(cde.at[core], cde.at[core], r_cde, slab=buddy)
    pair_ab.start()

    for copy in loads[4:6]:
        copy.wait()
    src_re = jnp.concatenate([mm(F[0, top], y), last_re], axis=0)
    src_im = jnp.concatenate([mm(F[1, top], y), last_im], axis=0)
    f_right = jnp.concatenate([F[0, :, last], F[1, :, last]], axis=0)
    p_flat = nt(vts[0], f_right) + nt(vts[1], f_right)
    cde[core, 0] = jnp.concatenate([p_flat[:, :R], p_flat[:, B : B + R]], axis=1)
    cde[core, 1] = jnp.concatenate(
        [F[0, :R, :R].astype(f32).T, F[1, :R, :R].astype(f32).T], axis=1
    )
    cde[core, 2] = jnp.concatenate([src_re[:R].T, src_im[:R].T], axis=1)
    pair_cde.start()
    p_out[...] = jnp.concatenate([p_flat[:, R:B], p_flat[:, B + R :]], axis=0)
    r_p = [fresh(1) for _ in range(1, nq)]
    r_b = [fresh(1) for _ in range(1, nq)]
    r_wt = [fresh(1) for _ in range(2 * nq)]
    away = lax.rem(q - target + nq, nq)
    slot = jnp.maximum(away - 1, 0)
    send_p = remote(p_out, p_in.at[slot], r_p[0] + slot, quad=target)
    send_b = remote(s_buf.at[R:], b_in.at[slot], r_b[0] + slot, quad=target)

    @pl.when(q != target)
    def _():
        send_p.start()

    rows = pl.ds(pl.multiple_of(core * hb, hb), hb)
    other_rows = pl.ds(pl.multiple_of((1 - core) * hb, hb), hb)

    def half(x):
        return jnp.where(core == 0, x[:hb], x[hb:])

    r_u, r_t, r_dm, r_dv, r_c, r_e = (fresh(1) for _ in range(6))
    left = jnp.maximum(s - 2, core)
    forward = remote(uout, uin, r_u, slab=jnp.minimum(s + 2, ns - 2 + core))
    back = [remote(tout, tmid, r_t, slab=2 * c + core) for c in range(mid)]
    send_dm = remote(dm_out, dm_in, r_dm, slab=left)
    send_dv = remote(dv_out, dv_in, r_dv, slab=left)
    send_c = remote(c_out, c_in, r_c, slab=left)
    send_e = remote(e_out, e_in, r_e, slab=left)
    inner_left = jnp.logical_and(chip > 0, chip < mid)

    arrival(abs_.at[1 - core], r_ab).wait_recv()
    ab_l = split(abs_[0])
    zero_map = jnp.zeros((R, 2 * R), f32)
    ab = dot3(ab_l, embed(abs_[1, :R])) + jnp.concatenate([zero_map, abs_[1, R:]], axis=0)

    @pl.when(chip == 0)
    def _():
        uin[...] = jnp.zeros_like(uin)
        uout[...] = half(ab[R:])
        forward.start()

    arrival(cde.at[1 - core], r_cde).wait_recv()
    cl, dl, el = cde[0, 0], cde[0, 1], cde[0, 2]
    cr, dr, er = cde[1, 0], cde[1, 1], cde[1, 2]
    e_dr = embed(dr)
    g = dot3(ab_l, e_dr) + jnp.concatenate([zero_map, er], axis=0)
    gc = times(jnp.concatenate([g, cr], axis=0), embed(cl))
    chip_d = gc[: R + M] + jnp.concatenate([dl, el], axis=0)
    chip_c = gc[R + M :]

    d_half = half(chip_d[R:])
    b_half = half(ab[R:])

    @pl.when(chip == nc - 1)
    def _():
        dm_out[...] = chip_d[:R]
        dv_out[...] = d_half
        send_dm.start()
        send_dv.start()

    @pl.when(jnp.logical_and(chip >= mid, chip < nc - 1))
    def _():
        @pl.when(chip > mid)
        def _():
            send_dm.wait_recv()
            z = times(jnp.concatenate([ab[:R], b_half], axis=0), embed(dm_in[...]))
            send_dv.wait_recv()
            z_b = z[R:] + dv_in[...]
            out = times(jnp.concatenate([z[:R], z_b], axis=0), embed(chip_c))
            dm_out[...] = out[:R] + chip_d[:R]
            dv_out[...] = out[R:] + d_half
            send_dm.start()
            send_dv.start()

    @pl.when(chip == mid - 1)
    def _():
        c_out[...] = chip_c

    @pl.when(chip < mid - 1)
    def _():
        send_c.wait_recv()

        @pl.when(chip > 0)
        def _():
            c_out[...] = times(c_in[...], embed(chip_c))

    @pl.when(inner_left)
    def _():
        send_c.start()

    e_out_map = embed(ab[:R])
    e_d = embed(chip_d[:R])
    e_c = embed(chip_c)

    @pl.when(chip > 0)
    def _():
        forward.wait_recv()

    u_in = uin[...]
    us = split(u_in)

    @pl.when(chip == nc - 1)
    def _():
        t_buf[...] = jnp.zeros_like(t_buf)

    @pl.when(jnp.logical_and(chip > 0, chip < nc - 1))
    def _():
        u_out = dot3(us, e_out_map) + b_half
        uout[...] = u_out
        forward.start()

        @pl.when(chip >= mid)
        def _():
            const = dot3(us, e_d) + d_half

            @pl.when(chip == mid)
            def _():
                send_dm.wait_recv()
                send_dv.wait_recv()

            t_in = times(u_out, embed(dm_in[...])) + dv_in[...]
            t_buf[...] = t_in

            @pl.when(chip == mid)
            def _():
                tout[...] = times(t_in, e_c) + const
                for copy in back:
                    copy.start()

    r_cu = fresh(1)
    ufull[rows, :] = u_in
    cross_u = remote(ufull.at[rows], ufull.at[rows], r_cu, slab=buddy)
    cross_u.start()

    @pl.when(inner_left)
    def _():
        const = dot3(us, e_d) + d_half

        @pl.when(chip == mid - 1)
        def _():
            e_out[...] = const

        @pl.when(chip < mid - 1)
        def _():
            send_e.wait_recv()
            e_out[...] = times(e_in[...], e_c) + const

        send_e.start()

    @pl.when(chip == 0)
    def _():
        if mid > 1:
            send_e.wait_recv()

    wr, wi = w_ref[0, 0], w_ref[0, 1]

    def weighted(x):
        re, im = x[:, :R], x[:, R:]
        return wr * re - wi * im, -(wr * im + wi * re)

    arrival(ufull.at[other_rows], r_cu).wait_recv()
    u_chip = ufull[...]
    e_al = embed(abs_[0, :R])
    e_cr = embed(cr)
    u_left = times(u_chip, e_al) + abs_[0, R:]
    u_own = jnp.where(core == 0, u_chip, u_left)
    wu = split(jnp.concatenate(weighted(u_own), axis=1))
    f_left = jnp.concatenate([F[0, R:, :R], F[1, R:, :R]], axis=1)
    s_buf[R:, :] = wr * src_re[R:] - wi * src_im[R:] + (nt(f_left, wu[0]) + nt(f_left, wu[1]))

    @pl.when(q != target)
    def _():
        send_b.start()

    t_const = times(dot3(us, e_al) + half(abs_[0, R:]), e_dr) + half(er)
    first_const = dot3(us, e_d) + d_half
    e_both = tuple(jnp.concatenate([a, b], axis=1) for a, b in zip(e_cr, e_c))
    loads[6].wait()

    @pl.when(q == target)
    def _():
        on = split(0.5 * ON[...])
        onh[...] = on[0]
        onl[...] = on[1]

    @pl.when(chip == mid - 1)
    def _():
        back[0].wait_recv()
        t_buf[...] = tmid[...]

    @pl.when(chip < mid - 1)
    def _():
        e_cin = embed(c_in[...])
        back[0].wait_recv()
        t_buf[...] = times(tmid[...], e_cin) + e_in[...]

    t_in = t_buf[...]
    t_both = times(t_in, e_both)
    w_left = weighted(t_both[:, : 2 * R] + t_const)
    w_first = weighted(t_both[:, 2 * R :] + first_const)
    wt_out[1] = jnp.concatenate([*weighted(t_in), w_left[0]], axis=1)
    wt_out[0] = jnp.concatenate([*w_left, w_first[0]], axis=1)
    to_home = []
    for k in (1, 0):
        at = nq // 2 - 1 + k
        hop = lax.rem(q - at + nq, nq)
        mine = jnp.logical_and(q == at, core == k)
        copy = remote(wt_out.at[k], wt_in.at[hop, rows], r_wt[0] + 2 * hop + core,
                      quad=at, slab=jnp.where(mine, buddy, chip * 2 + k))
        to_home.append((mine, copy))

        @pl.when(mine)
        def _():
            wt_in[0, rows] = wt_out[k]

        @pl.when(jnp.logical_not(mine))
        def _():
            copy.start()

    r_sub = fresh(1)
    r_full = [fresh(1) for _ in range(ns)]
    shares = [
        remote(s_buf.at[slice(p * qrows, (p + 1) * qrows)], land, r_sub, quad=p)
        for p in range(nq)
    ]
    r_red = [fresh(1) for _ in range(1, ns)]
    scatter = []
    for d in range(1, ns):
        to = lax.rem(s + d, ns)
        scatter.append(remote(red.at[to], red_in.at[d - 1], r_red[d - 1], quad=home(to), slab=to))

    def whole(i):
        return pltpu.make_async_remote_copy(
            src_ref=full.at[s], dst_ref=full.at[s], send_sem=bsem.at[i],
            recv_sem=rsem.at[r_full[0] + s], device_id=peer(i), device_id_type=MESH,
        )

    @pl.when(q == target)
    def _():
        total = s_buf[R:, :]
        for d in range(1, nq):
            arrival(b_in.at[d - 1], r_b[d - 1]).wait_recv()
            total += b_in[d - 1]
        total = total.T
        for d in range(nq):
            if d > 0:
                arrival(p_in.at[d - 1], r_p[d - 1]).wait_recv()
            piece = split(p_out[...] if d == 0 else p_in[d - 1])
            ph[d * 2 * R : (d + 1) * 2 * R] = piece[0]
            pl_[d * 2 * R : (d + 1) * 2 * R] = piece[1]
        for d in range(nq):
            for k in (0, 1):
                if d > 0:
                    arrival(wt_in.at[d, k * hb : (k + 1) * hb], r_wt[2 * d + k]).wait_recv()
                else:
                    @pl.when(core != k)
                    def _():
                        arrival(wt_in.at[0, k * hb : (k + 1) * hb], r_wt[k]).wait_recv()
        zh, zl = split(jnp.concatenate([wt_in[d, :, : 2 * R] for d in range(nq)], axis=1))
        total += mm(zh, ph[...]) + (mm(zl, ph[...]) + mm(zh, pl_[...]))
        first = wt_in[0, :, 2 * R :]
        for d in range(1, nq):
            first += wt_in[d, :, 2 * R :]
        flipped = jnp.concatenate([first, total], axis=1)
        fs = split(flipped)
        half_h = dot3(fs, (onh[...], onl[...]))
        total = flipped.T
        s_buf[...] = total
        for p in range(nq):
            @pl.when(q == p)
            def _():
                land[...] = s_buf[p * qrows : (p + 1) * qrows]

            @pl.when(q != p)
            def _():
                shares[p].start()
        ts = split(total)
        following = wt_in[0, :, :R]
        for d in range(1, nq):
            following += wt_in[d, :, :R]
        upper = dot3(split(following), vts)
        weighted_rows = split(jnp.concatenate([half_h[:, top], half_h[:, last] + upper], axis=1))
        both = tuple(jnp.concatenate([a, b], axis=0) for a, b in zip(fs, weighted_rows))
        products = dot3(both, ts)
        gram, x = products[:M], products[M:]
        proj = x + x.T

        at_row = lax.broadcasted_iota(jnp.int32, (M, M), 0)
        at_col = lax.broadcasted_iota(jnp.int32, (M, M), 1)
        tile = jnp.where(at_row <= at_col, gram, proj)
        diag = jnp.sum(jnp.where(at_row == at_col, proj, 0.0), axis=0, keepdims=True)
        diag = jnp.broadcast_to(diag, (8, M))
        for i in range(ns):
            red[i, :ch] = tile[i * ch : (i + 1) * ch]
            red[i, ch : ch + 8] = diag
        for copy in scatter:
            copy.start()
        part = red[s]
        for d in range(1, ns):
            scatter[d - 1].wait_recv()
            part += red_in[d - 1]
        full[s] = part

        @pl.loop(0, others)
        def _(i):
            whole(i).start()

    @pl.when(q != target)
    def _():
        shares[0].wait_recv()

    sub_ref[0] = land[...]
    for i in range(ns):
        @pl.when(jnp.logical_or(q != target, s != i))
        def _():
            arrival(full.at[i], r_full[i]).wait_recv()
    scale = 1.0 / (ns * B)
    for i in range(ns):
        tile_ref[i * ch : (i + 1) * ch, :] = full[i, :ch] * scale
    tile_ref[M : M + 8, :] = full[0, ch : ch + 8] * scale

    for copy in [pair_ab, pair_cde, cross_u]:
        copy.wait_send()

    @pl.when(chip < nc - 1)
    def _():
        forward.wait_send()

    @pl.when(chip > mid)
    def _():
        send_dm.wait_send()
        send_dv.wait_send()

    @pl.when(inner_left)
    def _():
        send_c.wait_send()
        send_e.wait_send()

    @pl.when(chip == mid)
    def _():
        for copy in back:
            copy.wait_send()

    for mine, copy in to_home:
        @pl.when(jnp.logical_not(mine))
        def _():
            copy.wait_send()

    @pl.when(q != target)
    def _():
        send_p.wait_send()
        send_b.wait_send()

    @pl.when(q == target)
    def _():
        for copy in scatter:
            copy.wait_send()

        @pl.loop(0, others)
        def _(i):
            whole(i).wait_send()

        for p in range(nq):
            @pl.when(q != p)
            def _():
                shares[p].wait_send()


def unpack(sub_ref, tile_ref, out_ref, corr_ref, proj_ref):
    M = corr_ref.shape[0]
    out_ref[...] = sub_ref[...]
    tile = tile_ref[:M]
    diag = tile_ref[M : M + 1]
    at_row = lax.broadcasted_iota(jnp.int32, (M, M), 0)
    at_col = lax.broadcasted_iota(jnp.int32, (M, M), 1)
    flipped = tile.T
    corr_ref[...] = jnp.where(at_row <= at_col, tile, flipped)
    low = jnp.where(at_row > at_col, tile, flipped)
    proj_ref[...] = jnp.where(at_row == at_col, jnp.broadcast_to(diag, (M, M)), low)


def per_device(nq, ns, factors, onsite, coupling, vectors, quad_weight):
    B = factors.shape[3]
    R = coupling.shape[1]
    M = vectors.shape[2]
    hb, ch, qrows = M // 2, M // ns, B // nq
    sends = 12 + ns // 4 + nq + (ns - 1)
    recvs = 10 + 2 * (nq - 1) + 2 * nq + (ns - 1) + ns
    vm = pltpu.VMEM
    in_hbm = pl.BlockSpec(memory_space=pltpu.HBM)
    here = pl.BlockSpec(memory_space=pltpu.VMEM)
    wide = vm((M, 2 * R), f32)
    thin = vm((hb, 2 * R), f32)
    sub, tile = pl.pallas_call(
        functools.partial(body, nq, ns),
        out_shape=(
            jax.ShapeDtypeStruct((1, qrows, M), f32),
            jax.ShapeDtypeStruct((M + 8, M), f32),
        ),
        in_specs=[in_hbm] * 4 + [pl.BlockSpec(memory_space=pltpu.SMEM)],
        out_specs=(here, here),
        scratch_shapes=[
            vm((2, B, B), bf16), vm((B, B), f32), vm((R, R), f32), vm((B, M), bf16),
            vm((B, B), bf16), vm((B, B), bf16),
            vm((2, R + M, 2 * R), f32), vm((2, 3, R, 2 * R), f32),
            thin, thin, thin, thin, wide, thin,
            wide, wide, thin, thin, wide, wide, thin, thin,
            vm((B, M), f32), vm((nq - 1, B - R, M), f32),
            vm((2 * R, B - R), f32), vm((nq - 1, 2 * R, B - R), f32),
            vm((2 * nq * R, B - R), bf16), vm((2 * nq * R, B - R), bf16),
            vm((2, hb, 3 * R), f32), vm((nq, M, 3 * R), f32), vm((qrows, M), f32),
            vm((ns, ch + 8, M), f32), vm((ns - 1, ch + 8, M), f32), vm((ns, ch + 8, M), f32),
            pltpu.SemaphoreType.DMA((7,)),
            pltpu.SemaphoreType.DMA((sends,)),
            pltpu.SemaphoreType.DMA((recvs,)),
            pltpu.SemaphoreType.DMA((ns * nq,)),
        ],
        compiler_params=pltpu.CompilerParams(
            collective_id=0, has_side_effects=True, vmem_limit_bytes=VMEM_BYTES
        ),
    )(factors, onsite, coupling, vectors, quad_weight)
    return pl.pallas_call(
        unpack,
        out_shape=(
            jax.ShapeDtypeStruct((1, qrows, M), f32),
            jax.ShapeDtypeStruct((M, M), f32),
            jax.ShapeDtypeStruct((M, M), f32),
        ),
        in_specs=[here, here],
        out_specs=(here, here, here),
        compiler_params=pltpu.CompilerParams(vmem_limit_bytes=VMEM_BYTES),
    )(sub, tile)


def solution(mesh):
    placed = (
        P("quad", "slab", None, None, None),
        P("slab", None, None),
        P("slab", None, None),
        P("slab", None, None),
        P("quad", None),
    )
    return jax.shard_map(
        functools.partial(per_device, mesh.shape["quad"], mesh.shape["slab"]),
        mesh=mesh,
        in_specs=placed,
        out_specs=(P("slab", "quad", None), P(), P()),
        check_vma=False,
    )
```

```python
import functools

import jax
import jax.numpy as jnp
from jax import lax
from jax.experimental import pallas as pl
from jax.experimental.pallas import tpu as pltpu
from jax.sharding import PartitionSpec as P

MESH = pl.DeviceIdType.MESH
f32, bf16 = jnp.float32, jnp.bfloat16
VMEM_BYTES = 64 * 2**20 - 64 * 2**10


def split(x):
    high = x.astype(bf16)
    return high, (x - high.astype(f32)).astype(bf16)


def mm(a, b):
    return jnp.dot(a, b, preferred_element_type=f32)


def dot3(a, b):
    (ah, al), (bh, bl) = a, b
    return mm(ah, bh) + (mm(ah, bl) + mm(al, bh))


def nt(a, b):
    return lax.dot_general(a, b, (((1,), (1,)), ((), ())), preferred_element_type=f32)


def tn(a, b):
    return lax.dot_general(a, b, (((0,), (0,)), ((), ())), preferred_element_type=f32)


def tn3(a, b):
    (ah, al), (bh, bl) = a, b
    return tn(ah, bh) + (tn(ah, bl) + tn(al, bh))


def embed(w):
    n = w.shape[1] // 2
    return split(
        jnp.concatenate([w, jnp.concatenate([-w[:, n:], w[:, :n]], axis=1)], axis=0)
    )


def times(x, e):
    return dot3(split(x), e)


def body(nq, ns, f_hbm, on_hbm, v_hbm, y_hbm, w_ref, sub_ref, tile_ref,
         F, ON, V, Y, onh, onl, abs_, cde, uin, uout, tmid, tout, ufull, t_buf,
         dm_in, dm_out, dv_in, dv_out, c_in, c_out, e_in, e_out, s_buf, b_in, p_out, p_in, ph, pl_,
         wt_out, wt_in, land, red, red_in, full, lsem, ssem, rsem, bsem):
    B = F.shape[1]
    R = V.shape[0]
    M = Y.shape[1]
    hb = M // 2
    nc = ns // 2
    mid = nc // 2
    qrows = B // nq
    ch = M // ns
    q = lax.axis_index("quad")
    s = lax.axis_index("slab")
    chip = s // 2
    core = s % 2
    buddy = chip * 2 + (1 - core)

    def home(slab):
        return nq // 2 - 1 + slab % 2

    target = home(s)

    top, last = slice(0, B - R), slice(B - R, B)
    loads = [
        pltpu.make_async_copy(src, dst, lsem.at[i])
        for i, (src, dst) in enumerate([
            (y_hbm.at[0], Y), (v_hbm.at[0], V),
            (f_hbm.at[0, 0, 0, last], F.at[0, last]), (f_hbm.at[0, 0, 1, last], F.at[1, last]),
            (f_hbm.at[0, 0, 0, top], F.at[0, top]), (f_hbm.at[0, 0, 1, top], F.at[1, top]),
            (on_hbm.at[0], ON)])
    ]
    for copy in loads:
        copy.start()

    barrier = pltpu.get_barrier_semaphore()
    others = ns * nq - 1

    def peer(i):
        to = lax.rem(q * ns + s + 1 + i, ns * nq)
        return {"quad": to // ns, "slab": lax.rem(to, ns)}

    @pl.loop(0, others)
    def _(i):
        pl.semaphore_signal(barrier, inc=1, device_id=peer(i), device_id_type=MESH)

    counts = [0, 0]

    def fresh(which):
        counts[which] += 1
        return counts[which] - 1

    def remote(src, dst, recv, **where):
        return pltpu.make_async_remote_copy(
            src_ref=src, dst_ref=dst, send_sem=ssem.at[fresh(0)], recv_sem=rsem.at[recv],
            device_id=where, device_id_type=MESH,
        )

    def arrival(dst, recv):
        return pltpu.make_async_remote_copy(
            src_ref=dst, dst_ref=dst, send_sem=ssem.at[0], recv_sem=rsem.at[recv],
            device_id={"slab": buddy}, device_id_type=MESH,
        )

    for copy in loads[:4]:
        copy.wait()
    y = Y[...]
    last_re = mm(F[0, last], y)
    last_im = mm(F[1, last], y)
    vs = split(V[...])
    vts = split(V[...].T)
    f21 = jnp.concatenate([F[0, last, :R], F[1, last, :R]], axis=1)
    a_cols = mm(vts[0], f21) + mm(vts[1], f21)
    s_last = split(jnp.concatenate([last_re, last_im], axis=1))
    b_cols = dot3(vts, s_last)
    abs_[core, :R] = jnp.concatenate([a_cols[:, :R].T, a_cols[:, R:].T], axis=1)
    abs_[core, R:] = jnp.concatenate([b_cols[:, :M].T, b_cols[:, M:].T], axis=1)

    pl.semaphore_wait(barrier, others)

    r_ab, r_cde = fresh(1), fresh(1)
    pair_ab = remote(abs_.at[core], abs_.at[core], r_ab, slab=buddy)
    pair_cde = remote(cde.at[core], cde.at[core], r_cde, slab=buddy)
    pair_ab.start()

    for copy in loads[4:6]:
        copy.wait()
    src_re = jnp.concatenate([mm(F[0, top], y), last_re], axis=0)
    src_im = jnp.concatenate([mm(F[1, top], y), last_im], axis=0)
    f_right = jnp.concatenate([F[0, :, last], F[1, :, last]], axis=0)
    p_flat = nt(vts[0], f_right) + nt(vts[1], f_right)
    cde[core, 0] = jnp.concatenate([p_flat[:, :R], p_flat[:, B : B + R]], axis=1)
    cde[core, 1] = jnp.concatenate(
        [F[0, :R, :R].astype(f32).T, F[1, :R, :R].astype(f32).T], axis=1
    )
    cde[core, 2] = jnp.concatenate([src_re[:R].T, src_im[:R].T], axis=1)
    pair_cde.start()
    p_out[...] = jnp.concatenate([p_flat[:, R:B], p_flat[:, B + R :]], axis=0)
    r_p = [fresh(1) for _ in range(1, nq)]
    r_b = [fresh(1) for _ in range(1, nq)]
    r_wt = [fresh(1) for _ in range(2 * nq)]
    away = lax.rem(q - target + nq, nq)
    slot = jnp.maximum(away - 1, 0)
    send_p = remote(p_out, p_in.at[slot], r_p[0] + slot, quad=target)
    send_b = remote(s_buf.at[R:], b_in.at[slot], r_b[0] + slot, quad=target)

    def start_p():
        @pl.when(q != target)
        def _():
            send_p.start()

    rows = pl.ds(pl.multiple_of(core * hb, hb), hb)
    other_rows = pl.ds(pl.multiple_of((1 - core) * hb, hb), hb)

    def half(x):
        return jnp.where(core == 0, x[:hb], x[hb:])

    r_u, r_t, r_dm, r_dv, r_c, r_e = (fresh(1) for _ in range(6))
    left = jnp.maximum(s - 2, core)
    forward = remote(uout, uin, r_u, slab=jnp.minimum(s + 2, ns - 2 + core))
    back = [remote(tout, tmid, r_t, slab=2 * c + core) for c in range(mid)]
    send_dm = remote(dm_out, dm_in, r_dm, slab=left)
    send_dv = remote(dv_out, dv_in, r_dv, slab=left)
    send_c = remote(c_out, c_in, r_c, slab=left)
    send_e = remote(e_out, e_in, r_e, slab=left)
    inner_left = jnp.logical_and(chip > 0, chip < mid)

    arrival(abs_.at[1 - core], r_ab).wait_recv()
    ab_l = split(abs_[0])
    zero_map = jnp.zeros((R, 2 * R), f32)
    ab = dot3(ab_l, embed(abs_[1, :R])) + jnp.concatenate([zero_map, abs_[1, R:]], axis=0)

    @pl.when(chip == 0)
    def _():
        uin[...] = jnp.zeros_like(uin)
        uout[...] = half(ab[R:])
        forward.start()
        start_p()

    arrival(cde.at[1 - core], r_cde).wait_recv()
    cl, dl, el = cde[0, 0], cde[0, 1], cde[0, 2]
    cr, dr, er = cde[1, 0], cde[1, 1], cde[1, 2]
    e_dr = embed(dr)
    g = dot3(ab_l, e_dr) + jnp.concatenate([zero_map, er], axis=0)
    gc = times(jnp.concatenate([g, cr], axis=0), embed(cl))
    chip_d = gc[: R + M] + jnp.concatenate([dl, el], axis=0)
    chip_c = gc[R + M :]

    d_half = half(chip_d[R:])
    b_half = half(ab[R:])

    @pl.when(chip == nc - 1)
    def _():
        dm_out[...] = chip_d[:R]
        dv_out[...] = d_half
        send_dm.start()
        send_dv.start()
        start_p()

    @pl.when(jnp.logical_and(chip >= mid, chip < nc - 1))
    def _():
        @pl.when(chip > mid)
        def _():
            send_dm.wait_recv()
            z = times(jnp.concatenate([ab[:R], b_half], axis=0), embed(dm_in[...]))
            send_dv.wait_recv()
            z_b = z[R:] + dv_in[...]
            out = times(jnp.concatenate([z[:R], z_b], axis=0), embed(chip_c))
            dm_out[...] = out[:R] + chip_d[:R]
            dv_out[...] = out[R:] + d_half
            send_dm.start()
            send_dv.start()

    @pl.when(chip == mid - 1)
    def _():
        c_out[...] = chip_c

    @pl.when(chip < mid - 1)
    def _():
        send_c.wait_recv()

        @pl.when(chip > 0)
        def _():
            c_out[...] = times(c_in[...], embed(chip_c))

    @pl.when(inner_left)
    def _():
        send_c.start()

    e_out_map = embed(ab[:R])
    e_d = embed(chip_d[:R])
    e_c = embed(chip_c)

    @pl.when(chip > 0)
    def _():
        forward.wait_recv()

    u_in = uin[...]
    us = split(u_in)

    @pl.when(chip == nc - 1)
    def _():
        t_buf[...] = jnp.zeros_like(t_buf)

    @pl.when(jnp.logical_and(chip > 0, chip < nc - 1))
    def _():
        u_out = dot3(us, e_out_map) + b_half
        uout[...] = u_out
        forward.start()

        @pl.when(chip >= mid)
        def _():
            const = dot3(us, e_d) + d_half

            @pl.when(chip == mid)
            def _():
                send_dm.wait_recv()
                send_dv.wait_recv()

            t_in = times(u_out, embed(dm_in[...])) + dv_in[...]
            t_buf[...] = t_in

            @pl.when(chip == mid)
            def _():
                tout[...] = times(t_in, e_c) + const
                for copy in back:
                    copy.start()

        start_p()

    r_cu = fresh(1)
    ufull[rows, :] = u_in
    cross_u = remote(ufull.at[rows], ufull.at[rows], r_cu, slab=buddy)
    cross_u.start()

    @pl.when(inner_left)
    def _():
        const = dot3(us, e_d) + d_half

        @pl.when(chip == mid - 1)
        def _():
            e_out[...] = const

        @pl.when(chip < mid - 1)
        def _():
            send_e.wait_recv()
            e_out[...] = times(e_in[...], e_c) + const

        send_e.start()

    @pl.when(chip == 0)
    def _():
        if mid > 1:
            send_e.wait_recv()

    wr, wi = w_ref[0, 0], w_ref[0, 1]

    def weighted(x):
        re, im = x[:, :R], x[:, R:]
        return wr * re - wi * im, -(wr * im + wi * re)

    arrival(ufull.at[other_rows], r_cu).wait_recv()
    u_chip = ufull[...]
    e_al = embed(abs_[0, :R])
    e_cr = embed(cr)
    u_left = times(u_chip, e_al) + abs_[0, R:]
    u_own = jnp.where(core == 0, u_chip, u_left)
    wu = split(jnp.concatenate(weighted(u_own), axis=1))
    f_left = jnp.concatenate([F[0, R:, :R], F[1, R:, :R]], axis=1)
    s_buf[R:, :] = wr * src_re[R:] - wi * src_im[R:] + (nt(f_left, wu[0]) + nt(f_left, wu[1]))

    @pl.when(q != target)
    def _():
        send_b.start()

    t_const = times(dot3(us, e_al) + half(abs_[0, R:]), e_dr) + half(er)
    first_const = dot3(us, e_d) + d_half
    e_both = tuple(jnp.concatenate([a, b], axis=1) for a, b in zip(e_cr, e_c))
    loads[6].wait()

    @pl.when(q == target)
    def _():
        on = split(0.5 * ON[...])
        onh[...] = on[0]
        onl[...] = on[1]

    @pl.when(chip == mid - 1)
    def _():
        back[0].wait_recv()
        t_buf[...] = tmid[...]

    @pl.when(chip < mid - 1)
    def _():
        e_cin = embed(c_in[...])
        back[0].wait_recv()
        t_buf[...] = times(tmid[...], e_cin) + e_in[...]

    t_in = t_buf[...]
    t_both = times(t_in, e_both)
    w_left = weighted(t_both[:, : 2 * R] + t_const)
    w_first = weighted(t_both[:, 2 * R :] + first_const)
    wt_out[1] = jnp.concatenate([*weighted(t_in), w_left[0]], axis=1)
    wt_out[0] = jnp.concatenate([*w_left, w_first[0]], axis=1)
    to_home = []
    for k in (1, 0):
        at = nq // 2 - 1 + k
        hop = lax.rem(q - at + nq, nq)
        mine = jnp.logical_and(q == at, core == k)
        copy = remote(wt_out.at[k], wt_in.at[hop, rows], r_wt[0] + 2 * hop + core,
                      quad=at, slab=jnp.where(mine, buddy, chip * 2 + k))
        to_home.append((mine, copy))

        @pl.when(mine)
        def _():
            wt_in[0, rows] = wt_out[k]

        @pl.when(jnp.logical_not(mine))
        def _():
            copy.start()

    r_sub = fresh(1)
    r_full = [fresh(1) for _ in range(ns)]
    shares = [
        remote(s_buf.at[slice(p * qrows, (p + 1) * qrows)], land, r_sub, quad=p)
        for p in range(nq)
    ]
    r_red = [fresh(1) for _ in range(1, ns)]
    scatter = []
    for d in range(1, ns):
        to = lax.rem(s + d, ns)
        scatter.append(remote(red.at[to], red_in.at[d - 1], r_red[d - 1], quad=home(to), slab=to))

    def whole(i):
        return pltpu.make_async_remote_copy(
            src_ref=full.at[s], dst_ref=full.at[s], send_sem=bsem.at[i],
            recv_sem=rsem.at[r_full[0] + s], device_id=peer(i), device_id_type=MESH,
        )

    @pl.when(q == target)
    def _():
        total = s_buf[R:, :]
        for d in range(1, nq):
            arrival(b_in.at[d - 1], r_b[d - 1]).wait_recv()
            total += b_in[d - 1]
        total = total.T
        for d in range(nq):
            if d > 0:
                arrival(p_in.at[d - 1], r_p[d - 1]).wait_recv()
            piece = split(p_out[...] if d == 0 else p_in[d - 1])
            ph[d * 2 * R : (d + 1) * 2 * R] = piece[0]
            pl_[d * 2 * R : (d + 1) * 2 * R] = piece[1]
        for d in range(nq):
            for k in (0, 1):
                if d > 0:
                    arrival(wt_in.at[d, k * hb : (k + 1) * hb], r_wt[2 * d + k]).wait_recv()
                else:
                    @pl.when(core != k)
                    def _():
                        arrival(wt_in.at[0, k * hb : (k + 1) * hb], r_wt[k]).wait_recv()
        zh, zl = split(jnp.concatenate([wt_in[d, :, : 2 * R] for d in range(nq)], axis=1))
        total += mm(zh, ph[...]) + (mm(zl, ph[...]) + mm(zh, pl_[...]))
        first = wt_in[0, :, 2 * R :]
        for d in range(1, nq):
            first += wt_in[d, :, 2 * R :]
        flipped = jnp.concatenate([first, total], axis=1)
        fs = split(flipped)
        half_h = dot3(fs, (onh[...], onl[...]))
        total = flipped.T
        s_buf[...] = total
        for p in range(nq):
            @pl.when(q == p)
            def _():
                land[...] = s_buf[p * qrows : (p + 1) * qrows]

            @pl.when(q != p)
            def _():
                shares[p].start()
        ts = split(total)
        following = wt_in[0, :, :R]
        for d in range(1, nq):
            following += wt_in[d, :, :R]
        upper = dot3(split(following), vts)
        weighted_rows = split(jnp.concatenate([half_h[:, top], half_h[:, last] + upper], axis=1))
        both = tuple(jnp.concatenate([a, b], axis=0) for a, b in zip(fs, weighted_rows))
        products = dot3(both, ts)
        gram, x = products[:M], products[M:]
        proj = x + x.T

        at_row = lax.broadcasted_iota(jnp.int32, (M, M), 0)
        at_col = lax.broadcasted_iota(jnp.int32, (M, M), 1)
        tile = jnp.where(at_row <= at_col, gram, proj)
        diag = jnp.sum(jnp.where(at_row == at_col, proj, 0.0), axis=0, keepdims=True)
        diag = jnp.broadcast_to(diag, (8, M))
        for i in range(ns):
            red[i, :ch] = tile[i * ch : (i + 1) * ch]
            red[i, ch : ch + 8] = diag
        for copy in scatter:
            copy.start()
        part = red[s]
        for d in range(1, ns):
            scatter[d - 1].wait_recv()
            part += red_in[d - 1]
        full[s] = part

        @pl.loop(0, others)
        def _(i):
            whole(i).start()

    @pl.when(q != target)
    def _():
        shares[0].wait_recv()

    sub_ref[0] = land[...]
    for i in range(ns):
        @pl.when(jnp.logical_or(q != target, s != i))
        def _():
            arrival(full.at[i], r_full[i]).wait_recv()
    scale = 1.0 / (ns * B)
    for i in range(ns):
        tile_ref[i * ch : (i + 1) * ch, :] = full[i, :ch] * scale
    tile_ref[M : M + 8, :] = full[0, ch : ch + 8] * scale

    for copy in [pair_ab, pair_cde, cross_u]:
        copy.wait_send()

    @pl.when(chip < nc - 1)
    def _():
        forward.wait_send()

    @pl.when(chip > mid)
    def _():
        send_dm.wait_send()
        send_dv.wait_send()

    @pl.when(inner_left)
    def _():
        send_c.wait_send()
        send_e.wait_send()

    @pl.when(chip == mid)
    def _():
        for copy in back:
            copy.wait_send()

    for mine, copy in to_home:
        @pl.when(jnp.logical_not(mine))
        def _():
            copy.wait_send()

    @pl.when(q != target)
    def _():
        send_p.wait_send()
        send_b.wait_send()

    @pl.when(q == target)
    def _():
        for copy in scatter:
            copy.wait_send()

        @pl.loop(0, others)
        def _(i):
            whole(i).wait_send()

        for p in range(nq):
            @pl.when(q != p)
            def _():
                shares[p].wait_send()


def unpack(sub_ref, tile_ref, out_ref, corr_ref, proj_ref):
    M = corr_ref.shape[0]
    out_ref[...] = sub_ref[...]
    tile = tile_ref[:M]
    diag = tile_ref[M : M + 1]
    at_row = lax.broadcasted_iota(jnp.int32, (M, M), 0)
    at_col = lax.broadcasted_iota(jnp.int32, (M, M), 1)
    flipped = tile.T
    corr_ref[...] = jnp.where(at_row <= at_col, tile, flipped)
    low = jnp.where(at_row > at_col, tile, flipped)
    proj_ref[...] = jnp.where(at_row == at_col, jnp.broadcast_to(diag, (M, M)), low)


def per_device(nq, ns, factors, onsite, coupling, vectors, quad_weight):
    B = factors.shape[3]
    R = coupling.shape[1]
    M = vectors.shape[2]
    hb, ch, qrows = M // 2, M // ns, B // nq
    sends = 12 + ns // 4 + nq + (ns - 1)
    recvs = 10 + 2 * (nq - 1) + 2 * nq + (ns - 1) + ns
    vm = pltpu.VMEM
    in_hbm = pl.BlockSpec(memory_space=pltpu.HBM)
    here = pl.BlockSpec(memory_space=pltpu.VMEM)
    wide = vm((M, 2 * R), f32)
    thin = vm((hb, 2 * R), f32)
    sub, tile = pl.pallas_call(
        functools.partial(body, nq, ns),
        out_shape=(
            jax.ShapeDtypeStruct((1, qrows, M), f32),
            jax.ShapeDtypeStruct((M + 8, M), f32),
        ),
        in_specs=[in_hbm] * 4 + [pl.BlockSpec(memory_space=pltpu.SMEM)],
        out_specs=(here, here),
        scratch_shapes=[
            vm((2, B, B), bf16), vm((B, B), f32), vm((R, R), f32), vm((B, M), bf16),
            vm((B, B), bf16), vm((B, B), bf16),
            vm((2, R + M, 2 * R), f32), vm((2, 3, R, 2 * R), f32),
            thin, thin, thin, thin, wide, thin,
            wide, wide, thin, thin, wide, wide, thin, thin,
            vm((B, M), f32), vm((nq - 1, B - R, M), f32),
            vm((2 * R, B - R), f32), vm((nq - 1, 2 * R, B - R), f32),
            vm((2 * nq * R, B - R), bf16), vm((2 * nq * R, B - R), bf16),
            vm((2, hb, 3 * R), f32), vm((nq, M, 3 * R), f32), vm((qrows, M), f32),
            vm((ns, ch + 8, M), f32), vm((ns - 1, ch + 8, M), f32), vm((ns, ch + 8, M), f32),
            pltpu.SemaphoreType.DMA((7,)),
            pltpu.SemaphoreType.DMA((sends,)),
            pltpu.SemaphoreType.DMA((recvs,)),
            pltpu.SemaphoreType.DMA((ns * nq,)),
        ],
        compiler_params=pltpu.CompilerParams(
            collective_id=0, has_side_effects=True, vmem_limit_bytes=VMEM_BYTES
        ),
    )(factors, onsite, coupling, vectors, quad_weight)
    return pl.pallas_call(
        unpack,
        out_shape=(
            jax.ShapeDtypeStruct((1, qrows, M), f32),
            jax.ShapeDtypeStruct((M, M), f32),
            jax.ShapeDtypeStruct((M, M), f32),
        ),
        in_specs=[here, here],
        out_specs=(here, here, here),
        compiler_params=pltpu.CompilerParams(vmem_limit_bytes=VMEM_BYTES),
    )(sub, tile)


def solution(mesh):
    placed = (
        P("quad", "slab", None, None, None),
        P("slab", None, None),
        P("slab", None, None),
        P("slab", None, None),
        P("quad", None),
    )
    return jax.shard_map(
        functools.partial(per_device, mesh.shape["quad"], mesh.shape["slab"]),
        mesh=mesh,
        in_specs=placed,
        out_specs=(P("slab", "quad", None), P(), P()),
        check_vma=False,
    )
```

```python
import functools

import jax
import jax.numpy as jnp
from jax import lax
from jax.experimental import pallas as pl
from jax.experimental.pallas import tpu as pltpu
from jax.sharding import PartitionSpec as P

MESH = pl.DeviceIdType.MESH
f32, bf16 = jnp.float32, jnp.bfloat16
VMEM_BYTES = 64 * 2**20 - 64 * 2**10


def split(x):
    high = x.astype(bf16)
    return high, (x - high.astype(f32)).astype(bf16)


def mm(a, b):
    return jnp.dot(a, b, preferred_element_type=f32)


def dot3(a, b):
    (ah, al), (bh, bl) = a, b
    return mm(ah, bh) + (mm(ah, bl) + mm(al, bh))


def nt(a, b):
    return lax.dot_general(a, b, (((1,), (1,)), ((), ())), preferred_element_type=f32)


def tn(a, b):
    return lax.dot_general(a, b, (((0,), (0,)), ((), ())), preferred_element_type=f32)


def tn3(a, b):
    (ah, al), (bh, bl) = a, b
    return tn(ah, bh) + (tn(ah, bl) + tn(al, bh))


def embed(w):
    n = w.shape[1] // 2
    return split(
        jnp.concatenate([w, jnp.concatenate([-w[:, n:], w[:, :n]], axis=1)], axis=0)
    )


def times(x, e):
    return dot3(split(x), e)


def body(nq, ns, f_hbm, on_hbm, v_hbm, y_hbm, w_ref, sub_ref, tile_ref,
         F, ON, V, Y, onh, onl, abs_, cde, uin, uout, tmid, tout, ufull, t_buf,
         dm_in, dm_out, dv_in, dv_out, c_in, c_out, e_in, e_out, s_buf, b_in, p_out, p_in, ph, pl_,
         wt_out, wt_in, land, red, red_in, full, lsem, ssem, rsem, bsem):
    B = F.shape[1]
    R = V.shape[0]
    M = Y.shape[1]
    hb = M // 2
    nc = ns // 2
    mid = nc // 2
    qrows = B // nq
    ch = M // ns
    q = lax.axis_index("quad")
    s = lax.axis_index("slab")
    chip = s // 2
    core = s % 2
    buddy = chip * 2 + (1 - core)

    def home(slab):
        return nq // 2 - 1 + slab % 2

    target = home(s)

    top, last = slice(0, B - R), slice(B - R, B)
    loads = [
        pltpu.make_async_copy(src, dst, lsem.at[i])
        for i, (src, dst) in enumerate([
            (y_hbm.at[0], Y), (v_hbm.at[0], V),
            (f_hbm.at[0, 0, 0, last], F.at[0, last]), (f_hbm.at[0, 0, 1, last], F.at[1, last]),
            (f_hbm.at[0, 0, 0, top], F.at[0, top]), (f_hbm.at[0, 0, 1, top], F.at[1, top]),
            (on_hbm.at[0], ON)])
    ]
    for copy in loads:
        copy.start()

    barrier = pltpu.get_barrier_semaphore()
    others = ns * nq - 1

    def peer(i):
        to = lax.rem(q * ns + s + 1 + i, ns * nq)
        return {"quad": to // ns, "slab": lax.rem(to, ns)}

    @pl.loop(0, others)
    def _(i):
        pl.semaphore_signal(barrier, inc=1, device_id=peer(i), device_id_type=MESH)

    counts = [0, 0]

    def fresh(which):
        counts[which] += 1
        return counts[which] - 1

    def remote(src, dst, recv, **where):
        return pltpu.make_async_remote_copy(
            src_ref=src, dst_ref=dst, send_sem=ssem.at[fresh(0)], recv_sem=rsem.at[recv],
            device_id=where, device_id_type=MESH,
        )

    def arrival(dst, recv):
        return pltpu.make_async_remote_copy(
            src_ref=dst, dst_ref=dst, send_sem=ssem.at[0], recv_sem=rsem.at[recv],
            device_id={"slab": buddy}, device_id_type=MESH,
        )

    for copy in loads[:4]:
        copy.wait()
    y = Y[...]
    last_re = mm(F[0, last], y)
    last_im = mm(F[1, last], y)
    vs = split(V[...])
    vts = split(V[...].T)
    f21 = jnp.concatenate([F[0, last, :R], F[1, last, :R]], axis=1)
    a_cols = mm(vts[0], f21) + mm(vts[1], f21)
    s_last = split(jnp.concatenate([last_re, last_im], axis=1))
    b_cols = dot3(vts, s_last)
    abs_[core, :R] = jnp.concatenate([a_cols[:, :R].T, a_cols[:, R:].T], axis=1)
    abs_[core, R:] = jnp.concatenate([b_cols[:, :M].T, b_cols[:, M:].T], axis=1)

    pl.semaphore_wait(barrier, others)

    r_ab, r_cde = fresh(1), fresh(1)
    pair_ab = remote(abs_.at[core], abs_.at[core], r_ab, slab=buddy)
    pair_cde = remote(cde.at[core], cde.at[core], r_cde, slab=buddy)
    pair_ab.start()

    for copy in loads[4:6]:
        copy.wait()
    src_re = jnp.concatenate([mm(F[0, top], y), last_re], axis=0)
    src_im = jnp.concatenate([mm(F[1, top], y), last_im], axis=0)
    f_right = jnp.concatenate([F[0, :, last], F[1, :, last]], axis=0)
    p_flat = nt(vts[0], f_right) + nt(vts[1], f_right)
    cde[core, 0] = jnp.concatenate([p_flat[:, :R], p_flat[:, B : B + R]], axis=1)
    cde[core, 1] = jnp.concatenate(
        [F[0, :R, :R].astype(f32).T, F[1, :R, :R].astype(f32).T], axis=1
    )
    cde[core, 2] = jnp.concatenate([src_re[:R].T, src_im[:R].T], axis=1)
    pair_cde.start()
    p_out[...] = jnp.concatenate([p_flat[:, R:B], p_flat[:, B + R :]], axis=0)
    r_p = [fresh(1) for _ in range(1, nq)]
    r_b = [fresh(1) for _ in range(1, nq)]
    r_wt = [fresh(1) for _ in range(2 * nq)]
    away = lax.rem(q - target + nq, nq)
    slot = jnp.maximum(away - 1, 0)
    send_p = remote(p_out, p_in.at[slot], r_p[0] + slot, quad=target)
    send_b = remote(s_buf.at[R:], b_in.at[slot], r_b[0] + slot, quad=target)

    @pl.when(q != target)
    def _():
        send_p.start()

    rows = pl.ds(pl.multiple_of(core * hb, hb), hb)
    other_rows = pl.ds(pl.multiple_of((1 - core) * hb, hb), hb)

    def half(x):
        return jnp.where(core == 0, x[:hb], x[hb:])

    r_u, r_t, r_dm, r_dv, r_c, r_e = (fresh(1) for _ in range(6))
    left = jnp.maximum(s - 2, core)
    forward = remote(uout, uin, r_u, slab=jnp.minimum(s + 2, ns - 2 + core))
    r_cu = fresh(1)
    cross_u = remote(uout, ufull.at[rows], r_cu, slab=jnp.minimum(s + 2, ns - 2 + core) + 1 - 2 * core)
    back = [remote(tout, tmid, r_t, slab=2 * c + core) for c in range(mid)]
    send_dm = remote(dm_out, dm_in, r_dm, slab=left)
    send_dv = remote(dv_out, dv_in, r_dv, slab=left)
    send_c = remote(c_out, c_in, r_c, slab=left)
    send_e = remote(e_out, e_in, r_e, slab=left)
    inner_left = jnp.logical_and(chip > 0, chip < mid)

    arrival(abs_.at[1 - core], r_ab).wait_recv()
    ab_l = split(abs_[0])
    zero_map = jnp.zeros((R, 2 * R), f32)
    ab = dot3(ab_l, embed(abs_[1, :R])) + jnp.concatenate([zero_map, abs_[1, R:]], axis=0)

    @pl.when(chip == 0)
    def _():
        uin[...] = jnp.zeros_like(uin)
        ufull[...] = jnp.zeros_like(ufull)
        uout[...] = half(ab[R:])
        forward.start()
        cross_u.start()

    arrival(cde.at[1 - core], r_cde).wait_recv()
    cl, dl, el = cde[0, 0], cde[0, 1], cde[0, 2]
    cr, dr, er = cde[1, 0], cde[1, 1], cde[1, 2]
    e_dr = embed(dr)
    g = dot3(ab_l, e_dr) + jnp.concatenate([zero_map, er], axis=0)
    gc = times(jnp.concatenate([g, cr], axis=0), embed(cl))
    chip_d = gc[: R + M] + jnp.concatenate([dl, el], axis=0)
    chip_c = gc[R + M :]

    d_half = half(chip_d[R:])
    b_half = half(ab[R:])

    @pl.when(chip == nc - 1)
    def _():
        dm_out[...] = chip_d[:R]
        dv_out[...] = d_half
        send_dm.start()
        send_dv.start()

    @pl.when(jnp.logical_and(chip >= mid, chip < nc - 1))
    def _():
        @pl.when(chip > mid)
        def _():
            send_dm.wait_recv()
            z = times(jnp.concatenate([ab[:R], b_half], axis=0), embed(dm_in[...]))
            send_dv.wait_recv()
            z_b = z[R:] + dv_in[...]
            out = times(jnp.concatenate([z[:R], z_b], axis=0), embed(chip_c))
            dm_out[...] = out[:R] + chip_d[:R]
            dv_out[...] = out[R:] + d_half
            send_dm.start()
            send_dv.start()

    @pl.when(chip == mid - 1)
    def _():
        c_out[...] = chip_c

    @pl.when(chip < mid - 1)
    def _():
        send_c.wait_recv()

        @pl.when(chip > 0)
        def _():
            c_out[...] = times(c_in[...], embed(chip_c))

    @pl.when(inner_left)
    def _():
        send_c.start()

    e_out_map = embed(ab[:R])
    e_d = embed(chip_d[:R])
    e_c = embed(chip_c)

    @pl.when(chip > 0)
    def _():
        forward.wait_recv()

    u_in = uin[...]
    us = split(u_in)

    @pl.when(chip == nc - 1)
    def _():
        t_buf[...] = jnp.zeros_like(t_buf)

    @pl.when(jnp.logical_and(chip > 0, chip < nc - 1))
    def _():
        u_out = dot3(us, e_out_map) + b_half
        uout[...] = u_out
        forward.start()
        cross_u.start()

        @pl.when(chip >= mid)
        def _():
            const = dot3(us, e_d) + d_half

            @pl.when(chip == mid)
            def _():
                send_dm.wait_recv()
                send_dv.wait_recv()

            t_in = times(u_out, embed(dm_in[...])) + dv_in[...]
            t_buf[...] = t_in

            @pl.when(chip == mid)
            def _():
                tout[...] = times(t_in, e_c) + const
                for copy in back:
                    copy.start()

    ufull[rows, :] = u_in

    @pl.when(inner_left)
    def _():
        const = dot3(us, e_d) + d_half

        @pl.when(chip == mid - 1)
        def _():
            e_out[...] = const

        @pl.when(chip < mid - 1)
        def _():
            send_e.wait_recv()
            e_out[...] = times(e_in[...], e_c) + const

        send_e.start()

    @pl.when(chip == 0)
    def _():
        if mid > 1:
            send_e.wait_recv()

    wr, wi = w_ref[0, 0], w_ref[0, 1]

    def weighted(x):
        re, im = x[:, :R], x[:, R:]
        return wr * re - wi * im, -(wr * im + wi * re)

    @pl.when(chip > 0)
    def _():
        arrival(ufull.at[other_rows], r_cu).wait_recv()

    u_chip = ufull[...]
    e_al = embed(abs_[0, :R])
    e_cr = embed(cr)
    u_left = times(u_chip, e_al) + abs_[0, R:]
    u_own = jnp.where(core == 0, u_chip, u_left)
    wu = split(jnp.concatenate(weighted(u_own), axis=1))
    f_left = jnp.concatenate([F[0, R:, :R], F[1, R:, :R]], axis=1)
    s_buf[R:, :] = wr * src_re[R:] - wi * src_im[R:] + (nt(f_left, wu[0]) + nt(f_left, wu[1]))

    @pl.when(q != target)
    def _():
        send_b.start()

    t_const = times(dot3(us, e_al) + half(abs_[0, R:]), e_dr) + half(er)
    first_const = dot3(us, e_d) + d_half
    e_both = tuple(jnp.concatenate([a, b], axis=1) for a, b in zip(e_cr, e_c))
    loads[6].wait()

    @pl.when(q == target)
    def _():
        on = split(0.5 * ON[...])
        onh[...] = on[0]
        onl[...] = on[1]

    @pl.when(chip == mid - 1)
    def _():
        back[0].wait_recv()
        t_buf[...] = tmid[...]

    @pl.when(chip < mid - 1)
    def _():
        e_cin = embed(c_in[...])
        back[0].wait_recv()
        t_buf[...] = times(tmid[...], e_cin) + e_in[...]

    t_in = t_buf[...]
    t_both = times(t_in, e_both)
    w_left = weighted(t_both[:, : 2 * R] + t_const)
    w_first = weighted(t_both[:, 2 * R :] + first_const)
    wt_out[1] = jnp.concatenate([*weighted(t_in), w_left[0]], axis=1)
    wt_out[0] = jnp.concatenate([*w_left, w_first[0]], axis=1)
    to_home = []
    for k in (1, 0):
        at = nq // 2 - 1 + k
        hop = lax.rem(q - at + nq, nq)
        mine = jnp.logical_and(q == at, core == k)
        copy = remote(wt_out.at[k], wt_in.at[hop, rows], r_wt[0] + 2 * hop + core,
                      quad=at, slab=jnp.where(mine, buddy, chip * 2 + k))
        to_home.append((mine, copy))

        @pl.when(mine)
        def _():
            wt_in[0, rows] = wt_out[k]

        @pl.when(jnp.logical_not(mine))
        def _():
            copy.start()

    r_sub = fresh(1)
    r_full = [fresh(1) for _ in range(ns)]
    shares = [
        remote(s_buf.at[slice(p * qrows, (p + 1) * qrows)], land, r_sub, quad=p)
        for p in range(nq)
    ]
    r_red = [fresh(1) for _ in range(1, ns)]
    scatter = []
    for d in range(1, ns):
        to = lax.rem(s + d, ns)
        scatter.append(remote(red.at[to], red_in.at[d - 1], r_red[d - 1], quad=home(to), slab=to))

    def whole(i):
        return pltpu.make_async_remote_copy(
            src_ref=full.at[s], dst_ref=full.at[s], send_sem=bsem.at[i],
            recv_sem=rsem.at[r_full[0] + s], device_id=peer(i), device_id_type=MESH,
        )

    @pl.when(q == target)
    def _():
        total = s_buf[R:, :]
        for d in range(1, nq):
            arrival(b_in.at[d - 1], r_b[d - 1]).wait_recv()
            total += b_in[d - 1]
        total = total.T
        for d in range(nq):
            if d > 0:
                arrival(p_in.at[d - 1], r_p[d - 1]).wait_recv()
            piece = split(p_out[...] if d == 0 else p_in[d - 1])
            ph[d * 2 * R : (d + 1) * 2 * R] = piece[0]
            pl_[d * 2 * R : (d + 1) * 2 * R] = piece[1]
        for d in range(nq):
            for k in (0, 1):
                if d > 0:
                    arrival(wt_in.at[d, k * hb : (k + 1) * hb], r_wt[2 * d + k]).wait_recv()
                else:
                    @pl.when(core != k)
                    def _():
                        arrival(wt_in.at[0, k * hb : (k + 1) * hb], r_wt[k]).wait_recv()
        zh, zl = split(jnp.concatenate([wt_in[d, :, : 2 * R] for d in range(nq)], axis=1))
        total += mm(zh, ph[...]) + (mm(zl, ph[...]) + mm(zh, pl_[...]))
        first = wt_in[0, :, 2 * R :]
        for d in range(1, nq):
            first += wt_in[d, :, 2 * R :]
        flipped = jnp.concatenate([first, total], axis=1)
        fs = split(flipped)
        half_h = dot3(fs, (onh[...], onl[...]))
        total = flipped.T
        s_buf[...] = total
        for p in range(nq):
            @pl.when(q == p)
            def _():
                land[...] = s_buf[p * qrows : (p + 1) * qrows]

            @pl.when(q != p)
            def _():
                shares[p].start()
        ts = split(total)
        following = wt_in[0, :, :R]
        for d in range(1, nq):
            following += wt_in[d, :, :R]
        upper = dot3(split(following), vts)
        weighted_rows = split(jnp.concatenate([half_h[:, top], half_h[:, last] + upper], axis=1))
        both = tuple(jnp.concatenate([a, b], axis=0) for a, b in zip(fs, weighted_rows))
        products = dot3(both, ts)
        gram, x = products[:M], products[M:]
        proj = x + x.T

        at_row = lax.broadcasted_iota(jnp.int32, (M, M), 0)
        at_col = lax.broadcasted_iota(jnp.int32, (M, M), 1)
        tile = jnp.where(at_row <= at_col, gram, proj)
        diag = jnp.sum(jnp.where(at_row == at_col, proj, 0.0), axis=0, keepdims=True)
        diag = jnp.broadcast_to(diag, (8, M))
        for i in range(ns):
            red[i, :ch] = tile[i * ch : (i + 1) * ch]
            red[i, ch : ch + 8] = diag
        for copy in scatter:
            copy.start()
        part = red[s]
        for d in range(1, ns):
            scatter[d - 1].wait_recv()
            part += red_in[d - 1]
        full[s] = part

        @pl.loop(0, others)
        def _(i):
            whole(i).start()

    @pl.when(q != target)
    def _():
        shares[0].wait_recv()

    sub_ref[0] = land[...]
    for i in range(ns):
        @pl.when(jnp.logical_or(q != target, s != i))
        def _():
            arrival(full.at[i], r_full[i]).wait_recv()
    scale = 1.0 / (ns * B)
    for i in range(ns):
        tile_ref[i * ch : (i + 1) * ch, :] = full[i, :ch] * scale
    tile_ref[M : M + 8, :] = full[0, ch : ch + 8] * scale

    for copy in [pair_ab, pair_cde]:
        copy.wait_send()

    @pl.when(chip < nc - 1)
    def _():
        forward.wait_send()
        cross_u.wait_send()

    @pl.when(chip > mid)
    def _():
        send_dm.wait_send()
        send_dv.wait_send()

    @pl.when(inner_left)
    def _():
        send_c.wait_send()
        send_e.wait_send()

    @pl.when(chip == mid)
    def _():
        for copy in back:
            copy.wait_send()

    for mine, copy in to_home:
        @pl.when(jnp.logical_not(mine))
        def _():
            copy.wait_send()

    @pl.when(q != target)
    def _():
        send_p.wait_send()
        send_b.wait_send()

    @pl.when(q == target)
    def _():
        for copy in scatter:
            copy.wait_send()

        @pl.loop(0, others)
        def _(i):
            whole(i).wait_send()

        for p in range(nq):
            @pl.when(q != p)
            def _():
                shares[p].wait_send()


def unpack(sub_ref, tile_ref, out_ref, corr_ref, proj_ref):
    M = corr_ref.shape[0]
    out_ref[...] = sub_ref[...]
    tile = tile_ref[:M]
    diag = tile_ref[M : M + 1]
    at_row = lax.broadcasted_iota(jnp.int32, (M, M), 0)
    at_col = lax.broadcasted_iota(jnp.int32, (M, M), 1)
    flipped = tile.T
    corr_ref[...] = jnp.where(at_row <= at_col, tile, flipped)
    low = jnp.where(at_row > at_col, tile, flipped)
    proj_ref[...] = jnp.where(at_row == at_col, jnp.broadcast_to(diag, (M, M)), low)


def per_device(nq, ns, factors, onsite, coupling, vectors, quad_weight):
    B = factors.shape[3]
    R = coupling.shape[1]
    M = vectors.shape[2]
    hb, ch, qrows = M // 2, M // ns, B // nq
    sends = 12 + ns // 4 + nq + (ns - 1)
    recvs = 10 + 2 * (nq - 1) + 2 * nq + (ns - 1) + ns
    vm = pltpu.VMEM
    in_hbm = pl.BlockSpec(memory_space=pltpu.HBM)
    here = pl.BlockSpec(memory_space=pltpu.VMEM)
    wide = vm((M, 2 * R), f32)
    thin = vm((hb, 2 * R), f32)
    sub, tile = pl.pallas_call(
        functools.partial(body, nq, ns),
        out_shape=(
            jax.ShapeDtypeStruct((1, qrows, M), f32),
            jax.ShapeDtypeStruct((M + 8, M), f32),
        ),
        in_specs=[in_hbm] * 4 + [pl.BlockSpec(memory_space=pltpu.SMEM)],
        out_specs=(here, here),
        scratch_shapes=[
            vm((2, B, B), bf16), vm((B, B), f32), vm((R, R), f32), vm((B, M), bf16),
            vm((B, B), bf16), vm((B, B), bf16),
            vm((2, R + M, 2 * R), f32), vm((2, 3, R, 2 * R), f32),
            thin, thin, thin, thin, wide, thin,
            wide, wide, thin, thin, wide, wide, thin, thin,
            vm((B, M), f32), vm((nq - 1, B - R, M), f32),
            vm((2 * R, B - R), f32), vm((nq - 1, 2 * R, B - R), f32),
            vm((2 * nq * R, B - R), bf16), vm((2 * nq * R, B - R), bf16),
            vm((2, hb, 3 * R), f32), vm((nq, M, 3 * R), f32), vm((qrows, M), f32),
            vm((ns, ch + 8, M), f32), vm((ns - 1, ch + 8, M), f32), vm((ns, ch + 8, M), f32),
            pltpu.SemaphoreType.DMA((7,)),
            pltpu.SemaphoreType.DMA((sends,)),
            pltpu.SemaphoreType.DMA((recvs,)),
            pltpu.SemaphoreType.DMA((ns * nq,)),
        ],
        compiler_params=pltpu.CompilerParams(
            collective_id=0, has_side_effects=True, vmem_limit_bytes=VMEM_BYTES
        ),
    )(factors, onsite, coupling, vectors, quad_weight)
    return pl.pallas_call(
        unpack,
        out_shape=(
            jax.ShapeDtypeStruct((1, qrows, M), f32),
            jax.ShapeDtypeStruct((M, M), f32),
            jax.ShapeDtypeStruct((M, M), f32),
        ),
        in_specs=[here, here],
        out_specs=(here, here, here),
        compiler_params=pltpu.CompilerParams(vmem_limit_bytes=VMEM_BYTES),
    )(sub, tile)


def solution(mesh):
    placed = (
        P("quad", "slab", None, None, None),
        P("slab", None, None),
        P("slab", None, None),
        P("slab", None, None),
        P("quad", None),
    )
    return jax.shard_map(
        functools.partial(per_device, mesh.shape["quad"], mesh.shape["slab"]),
        mesh=mesh,
        in_specs=placed,
        out_specs=(P("slab", "quad", None), P(), P()),
        check_vma=False,
    )
```

```python
import functools

import jax
import jax.numpy as jnp
from jax import lax
from jax.experimental import pallas as pl
from jax.experimental.pallas import tpu as pltpu
from jax.sharding import PartitionSpec as P

MESH = pl.DeviceIdType.MESH
f32, bf16 = jnp.float32, jnp.bfloat16
VMEM_BYTES = 64 * 2**20 - 64 * 2**10


def split(x):
    high = x.astype(bf16)
    return high, (x - high.astype(f32)).astype(bf16)


def mm(a, b):
    return jnp.dot(a, b, preferred_element_type=f32)


def dot3(a, b):
    (ah, al), (bh, bl) = a, b
    return mm(ah, bh) + (mm(ah, bl) + mm(al, bh))


def nt(a, b):
    return lax.dot_general(a, b, (((1,), (1,)), ((), ())), preferred_element_type=f32)


def tn(a, b):
    return lax.dot_general(a, b, (((0,), (0,)), ((), ())), preferred_element_type=f32)


def tn3(a, b):
    (ah, al), (bh, bl) = a, b
    return tn(ah, bh) + (tn(ah, bl) + tn(al, bh))


def embed(w):
    n = w.shape[1] // 2
    return split(
        jnp.concatenate([w, jnp.concatenate([-w[:, n:], w[:, :n]], axis=1)], axis=0)
    )


def times(x, e):
    return dot3(split(x), e)


def body(nq, ns, f_hbm, on_hbm, v_hbm, y_hbm, w_ref, sub_ref, tile_ref,
         F, ON, V, Y, onh, onl, abs_, cde, uin, uout, tmid, tout, ufull, t_buf,
         dm_in, dm_out, dv_in, dv_out, c_in, c_out, e_in, e_out, s_buf, b_in, p_out, p_in, ph, pl_,
         wt_out, wt_in, land, red, red_in, full, lsem, ssem, rsem, bsem):
    B = F.shape[1]
    R = V.shape[0]
    M = Y.shape[1]
    hb = M // 2
    nc = ns // 2
    mid = nc // 2
    qrows = B // nq
    ch = M // ns
    q = lax.axis_index("quad")
    s = lax.axis_index("slab")
    chip = s // 2
    core = s % 2
    buddy = chip * 2 + (1 - core)

    def home(slab):
        return nq // 2 - 1 + slab % 2

    target = home(s)

    top, last = slice(0, B - R), slice(B - R, B)
    loads = [
        pltpu.make_async_copy(src, dst, lsem.at[i])
        for i, (src, dst) in enumerate([
            (y_hbm.at[0], Y), (v_hbm.at[0], V),
            (f_hbm.at[0, 0, 0, last], F.at[0, last]), (f_hbm.at[0, 0, 1, last], F.at[1, last]),
            (f_hbm.at[0, 0, 0, top], F.at[0, top]), (f_hbm.at[0, 0, 1, top], F.at[1, top]),
            (on_hbm.at[0], ON)])
    ]
    for copy in loads:
        copy.start()

    barrier = pltpu.get_barrier_semaphore()
    others = ns * nq - 1

    def peer(i):
        to = lax.rem(q * ns + s + 1 + i, ns * nq)
        return {"quad": to // ns, "slab": lax.rem(to, ns)}

    @pl.loop(0, others)
    def _(i):
        pl.semaphore_signal(barrier, inc=1, device_id=peer(i), device_id_type=MESH)

    counts = [0, 0]

    def fresh(which):
        counts[which] += 1
        return counts[which] - 1

    def remote(src, dst, recv, **where):
        return pltpu.make_async_remote_copy(
            src_ref=src, dst_ref=dst, send_sem=ssem.at[fresh(0)], recv_sem=rsem.at[recv],
            device_id=where, device_id_type=MESH,
        )

    def arrival(dst, recv):
        return pltpu.make_async_remote_copy(
            src_ref=dst, dst_ref=dst, send_sem=ssem.at[0], recv_sem=rsem.at[recv],
            device_id={"slab": buddy}, device_id_type=MESH,
        )

    for copy in loads[:4]:
        copy.wait()
    y = Y[...]
    last_re = mm(F[0, last], y)
    last_im = mm(F[1, last], y)
    vs = split(V[...])
    vts = split(V[...].T)
    f21 = jnp.concatenate([F[0, last, :R], F[1, last, :R]], axis=1)
    a_cols = mm(vts[0], f21) + mm(vts[1], f21)
    s_last = split(jnp.concatenate([last_re, last_im], axis=1))
    b_cols = dot3(vts, s_last)
    abs_[core, :R] = jnp.concatenate([a_cols[:, :R].T, a_cols[:, R:].T], axis=1)
    abs_[core, R:] = jnp.concatenate([b_cols[:, :M].T, b_cols[:, M:].T], axis=1)

    pl.semaphore_wait(barrier, others)

    r_ab, r_cde = fresh(1), fresh(1)
    pair_ab = remote(abs_.at[core], abs_.at[core], r_ab, slab=buddy)
    pair_cde = remote(cde.at[core], cde.at[core], r_cde, slab=buddy)
    pair_ab.start()

    for copy in loads[4:6]:
        copy.wait()
    src_re = jnp.concatenate([mm(F[0, top], y), last_re], axis=0)
    src_im = jnp.concatenate([mm(F[1, top], y), last_im], axis=0)
    f_right = jnp.concatenate([F[0, :, last], F[1, :, last]], axis=0)
    p_flat = nt(vts[0], f_right) + nt(vts[1], f_right)
    p_out[...] = jnp.concatenate([p_flat[:, R:B], p_flat[:, B + R :]], axis=0)
    r_p = [fresh(1) for _ in range(1, nq)]
    r_b = [fresh(1) for _ in range(1, nq)]
    r_wt = [fresh(1) for _ in range(2 * nq)]
    away = lax.rem(q - target + nq, nq)
    slot = jnp.maximum(away - 1, 0)
    send_p = remote(p_out, p_in.at[slot], r_p[0] + slot, quad=target)
    send_b = remote(s_buf.at[R:], b_in.at[slot], r_b[0] + slot, quad=target)

    @pl.when(q != target)
    def _():
        send_p.start()

    cde[core, 0] = jnp.concatenate([p_flat[:, :R], p_flat[:, B : B + R]], axis=1)
    cde[core, 1] = jnp.concatenate(
        [F[0, :R, :R].astype(f32).T, F[1, :R, :R].astype(f32).T], axis=1
    )
    cde[core, 2] = jnp.concatenate([src_re[:R].T, src_im[:R].T], axis=1)
    pair_cde.start()

    rows = pl.ds(pl.multiple_of(core * hb, hb), hb)
    other_rows = pl.ds(pl.multiple_of((1 - core) * hb, hb), hb)

    def half(x):
        return jnp.where(core == 0, x[:hb], x[hb:])

    r_u, r_t, r_dm, r_dv, r_c, r_e = (fresh(1) for _ in range(6))
    left = jnp.maximum(s - 2, core)
    forward = remote(uout, uin, r_u, slab=jnp.minimum(s + 2, ns - 2 + core))
    r_cu = fresh(1)
    cross_u = remote(uout, ufull.at[rows], r_cu, slab=jnp.minimum(s + 2, ns - 2 + core) + 1 - 2 * core)
    back = [remote(tout, tmid, r_t, slab=2 * c + core) for c in range(mid)]
    send_dm = remote(dm_out, dm_in, r_dm, slab=left)
    send_dv = remote(dv_out, dv_in, r_dv, slab=left)
    send_c = remote(c_out, c_in, r_c, slab=left)
    send_e = remote(e_out, e_in, r_e, slab=left)
    inner_left = jnp.logical_and(chip > 0, chip < mid)

    arrival(abs_.at[1 - core], r_ab).wait_recv()
    ab_l = split(abs_[0])
    zero_map = jnp.zeros((R, 2 * R), f32)
    ab = dot3(ab_l, embed(abs_[1, :R])) + jnp.concatenate([zero_map, abs_[1, R:]], axis=0)

    @pl.when(chip == 0)
    def _():
        uin[...] = jnp.zeros_like(uin)
        ufull[...] = jnp.zeros_like(ufull)
        uout[...] = half(ab[R:])
        forward.start()
        cross_u.start()

    arrival(cde.at[1 - core], r_cde).wait_recv()
    cl, dl, el = cde[0, 0], cde[0, 1], cde[0, 2]
    cr, dr, er = cde[1, 0], cde[1, 1], cde[1, 2]
    e_dr = embed(dr)
    g = dot3(ab_l, e_dr) + jnp.concatenate([zero_map, er], axis=0)
    gc = times(jnp.concatenate([g, cr], axis=0), embed(cl))
    chip_d = gc[: R + M] + jnp.concatenate([dl, el], axis=0)
    chip_c = gc[R + M :]

    d_half = half(chip_d[R:])
    b_half = half(ab[R:])

    @pl.when(chip == nc - 1)
    def _():
        dm_out[...] = chip_d[:R]
        dv_out[...] = d_half
        send_dm.start()
        send_dv.start()

    @pl.when(jnp.logical_and(chip >= mid, chip < nc - 1))
    def _():
        @pl.when(chip > mid)
        def _():
            send_dm.wait_recv()
            z = times(jnp.concatenate([ab[:R], b_half], axis=0), embed(dm_in[...]))
            send_dv.wait_recv()
            z_b = z[R:] + dv_in[...]
            out = times(jnp.concatenate([z[:R], z_b], axis=0), embed(chip_c))
            dm_out[...] = out[:R] + chip_d[:R]
            dv_out[...] = out[R:] + d_half
            send_dm.start()
            send_dv.start()

    @pl.when(chip == mid - 1)
    def _():
        c_out[...] = chip_c

    @pl.when(chip < mid - 1)
    def _():
        send_c.wait_recv()

        @pl.when(chip > 0)
        def _():
            c_out[...] = times(c_in[...], embed(chip_c))

    @pl.when(inner_left)
    def _():
        send_c.start()

    e_out_map = embed(ab[:R])
    e_d = embed(chip_d[:R])
    e_c = embed(chip_c)

    @pl.when(chip > 0)
    def _():
        forward.wait_recv()

    u_in = uin[...]
    us = split(u_in)

    @pl.when(chip == nc - 1)
    def _():
        t_buf[...] = jnp.zeros_like(t_buf)

    @pl.when(jnp.logical_and(chip > 0, chip < nc - 1))
    def _():
        u_out = dot3(us, e_out_map) + b_half
        uout[...] = u_out
        forward.start()
        cross_u.start()

        @pl.when(chip >= mid)
        def _():
            const = dot3(us, e_d) + d_half

            @pl.when(chip == mid)
            def _():
                send_dm.wait_recv()
                send_dv.wait_recv()

            t_in = times(u_out, embed(dm_in[...])) + dv_in[...]
            t_buf[...] = t_in

            @pl.when(chip == mid)
            def _():
                tout[...] = times(t_in, e_c) + const
                for copy in back:
                    copy.start()

    ufull[rows, :] = u_in

    @pl.when(inner_left)
    def _():
        const = dot3(us, e_d) + d_half

        @pl.when(chip == mid - 1)
        def _():
            e_out[...] = const

        @pl.when(chip < mid - 1)
        def _():
            send_e.wait_recv()
            e_out[...] = times(e_in[...], e_c) + const

        send_e.start()

    @pl.when(chip == 0)
    def _():
        if mid > 1:
            send_e.wait_recv()

    wr, wi = w_ref[0, 0], w_ref[0, 1]

    def weighted(x):
        re, im = x[:, :R], x[:, R:]
        return wr * re - wi * im, -(wr * im + wi * re)

    @pl.when(chip > 0)
    def _():
        arrival(ufull.at[other_rows], r_cu).wait_recv()

    u_chip = ufull[...]
    e_al = embed(abs_[0, :R])
    e_cr = embed(cr)
    u_left = times(u_chip, e_al) + abs_[0, R:]
    u_own = jnp.where(core == 0, u_chip, u_left)
    wu = split(jnp.concatenate(weighted(u_own), axis=1))
    f_left = jnp.concatenate([F[0, R:, :R], F[1, R:, :R]], axis=1)
    s_buf[R:, :] = wr * src_re[R:] - wi * src_im[R:] + (nt(f_left, wu[0]) + nt(f_left, wu[1]))

    @pl.when(q != target)
    def _():
        send_b.start()

    t_const = times(dot3(us, e_al) + half(abs_[0, R:]), e_dr) + half(er)
    first_const = dot3(us, e_d) + d_half
    e_both = tuple(jnp.concatenate([a, b], axis=1) for a, b in zip(e_cr, e_c))
    loads[6].wait()

    @pl.when(q == target)
    def _():
        on = split(0.5 * ON[...])
        onh[...] = on[0]
        onl[...] = on[1]

    @pl.when(chip == mid - 1)
    def _():
        back[0].wait_recv()
        t_buf[...] = tmid[...]

    @pl.when(chip < mid - 1)
    def _():
        e_cin = embed(c_in[...])
        back[0].wait_recv()
        t_buf[...] = times(tmid[...], e_cin) + e_in[...]

    t_in = t_buf[...]
    t_both = times(t_in, e_both)
    w_left = weighted(t_both[:, : 2 * R] + t_const)
    w_first = weighted(t_both[:, 2 * R :] + first_const)
    wt_out[1] = jnp.concatenate([*weighted(t_in), w_left[0]], axis=1)
    wt_out[0] = jnp.concatenate([*w_left, w_first[0]], axis=1)
    to_home = []
    for k in (1, 0):
        at = nq // 2 - 1 + k
        hop = lax.rem(q - at + nq, nq)
        mine = jnp.logical_and(q == at, core == k)
        copy = remote(wt_out.at[k], wt_in.at[hop, rows], r_wt[0] + 2 * hop + core,
                      quad=at, slab=jnp.where(mine, buddy, chip * 2 + k))
        to_home.append((mine, copy))

        @pl.when(mine)
        def _():
            wt_in[0, rows] = wt_out[k]

        @pl.when(jnp.logical_not(mine))
        def _():
            copy.start()

    r_sub = fresh(1)
    r_full = [fresh(1) for _ in range(ns)]
    shares = [
        remote(s_buf.at[slice(p * qrows, (p + 1) * qrows)], land, r_sub, quad=p)
        for p in range(nq)
    ]
    r_red = [fresh(1) for _ in range(1, ns)]
    scatter = []
    for d in range(1, ns):
        to = lax.rem(s + d, ns)
        scatter.append(remote(red.at[to], red_in.at[d - 1], r_red[d - 1], quad=home(to), slab=to))

    def whole(i):
        return pltpu.make_async_remote_copy(
            src_ref=full.at[s], dst_ref=full.at[s], send_sem=bsem.at[i],
            recv_sem=rsem.at[r_full[0] + s], device_id=peer(i), device_id_type=MESH,
        )

    @pl.when(q == target)
    def _():
        total = s_buf[R:, :]
        for d in range(1, nq):
            arrival(b_in.at[d - 1], r_b[d - 1]).wait_recv()
            total += b_in[d - 1]
        total = total.T
        for d in range(nq):
            if d > 0:
                arrival(p_in.at[d - 1], r_p[d - 1]).wait_recv()
            piece = split(p_out[...] if d == 0 else p_in[d - 1])
            ph[d * 2 * R : (d + 1) * 2 * R] = piece[0]
            pl_[d * 2 * R : (d + 1) * 2 * R] = piece[1]
        for d in range(nq):
            for k in (0, 1):
                if d > 0:
                    arrival(wt_in.at[d, k * hb : (k + 1) * hb], r_wt[2 * d + k]).wait_recv()
                else:
                    @pl.when(core != k)
                    def _():
                        arrival(wt_in.at[0, k * hb : (k + 1) * hb], r_wt[k]).wait_recv()
        zh, zl = split(jnp.concatenate([wt_in[d, :, : 2 * R] for d in range(nq)], axis=1))
        total += mm(zh, ph[...]) + (mm(zl, ph[...]) + mm(zh, pl_[...]))
        first = wt_in[0, :, 2 * R :]
        for d in range(1, nq):
            first += wt_in[d, :, 2 * R :]
        flipped = jnp.concatenate([first, total], axis=1)
        fs = split(flipped)
        half_h = dot3(fs, (onh[...], onl[...]))
        total = flipped.T
        s_buf[...] = total
        for p in range(nq):
            @pl.when(q == p)
            def _():
                land[...] = s_buf[p * qrows : (p + 1) * qrows]

            @pl.when(q != p)
            def _():
                shares[p].start()
        ts = split(total)
        following = wt_in[0, :, :R]
        for d in range(1, nq):
            following += wt_in[d, :, :R]
        upper = dot3(split(following), vts)
        weighted_rows = split(jnp.concatenate([half_h[:, top], half_h[:, last] + upper], axis=1))
        both = tuple(jnp.concatenate([a, b], axis=0) for a, b in zip(fs, weighted_rows))
        products = dot3(both, ts)
        gram, x = products[:M], products[M:]
        proj = x + x.T

        at_row = lax.broadcasted_iota(jnp.int32, (M, M), 0)
        at_col = lax.broadcasted_iota(jnp.int32, (M, M), 1)
        tile = jnp.where(at_row <= at_col, gram, proj)
        diag = jnp.sum(jnp.where(at_row == at_col, proj, 0.0), axis=0, keepdims=True)
        diag = jnp.broadcast_to(diag, (8, M))
        for i in range(ns):
            red[i, :ch] = tile[i * ch : (i + 1) * ch]
            red[i, ch : ch + 8] = diag
        for copy in scatter:
            copy.start()
        part = red[s]
        for d in range(1, ns):
            scatter[d - 1].wait_recv()
            part += red_in[d - 1]
        full[s] = part

        @pl.loop(0, others)
        def _(i):
            whole(i).start()

    @pl.when(q != target)
    def _():
        shares[0].wait_recv()

    sub_ref[0] = land[...]
    for i in range(ns):
        @pl.when(jnp.logical_or(q != target, s != i))
        def _():
            arrival(full.at[i], r_full[i]).wait_recv()
    scale = 1.0 / (ns * B)
    for i in range(ns):
        tile_ref[i * ch : (i + 1) * ch, :] = full[i, :ch] * scale
    tile_ref[M : M + 8, :] = full[0, ch : ch + 8] * scale

    for copy in [pair_ab, pair_cde]:
        copy.wait_send()

    @pl.when(chip < nc - 1)
    def _():
        forward.wait_send()
        cross_u.wait_send()

    @pl.when(chip > mid)
    def _():
        send_dm.wait_send()
        send_dv.wait_send()

    @pl.when(inner_left)
    def _():
        send_c.wait_send()
        send_e.wait_send()

    @pl.when(chip == mid)
    def _():
        for copy in back:
            copy.wait_send()

    for mine, copy in to_home:
        @pl.when(jnp.logical_not(mine))
        def _():
            copy.wait_send()

    @pl.when(q != target)
    def _():
        send_p.wait_send()
        send_b.wait_send()

    @pl.when(q == target)
    def _():
        for copy in scatter:
            copy.wait_send()

        @pl.loop(0, others)
        def _(i):
            whole(i).wait_send()

        for p in range(nq):
            @pl.when(q != p)
            def _():
                shares[p].wait_send()


def unpack(sub_ref, tile_ref, out_ref, corr_ref, proj_ref):
    M = corr_ref.shape[0]
    out_ref[...] = sub_ref[...]
    tile = tile_ref[:M]
    diag = tile_ref[M : M + 1]
    at_row = lax.broadcasted_iota(jnp.int32, (M, M), 0)
    at_col = lax.broadcasted_iota(jnp.int32, (M, M), 1)
    flipped = tile.T
    corr_ref[...] = jnp.where(at_row <= at_col, tile, flipped)
    low = jnp.where(at_row > at_col, tile, flipped)
    proj_ref[...] = jnp.where(at_row == at_col, jnp.broadcast_to(diag, (M, M)), low)


def per_device(nq, ns, factors, onsite, coupling, vectors, quad_weight):
    B = factors.shape[3]
    R = coupling.shape[1]
    M = vectors.shape[2]
    hb, ch, qrows = M // 2, M // ns, B // nq
    sends = 12 + ns // 4 + nq + (ns - 1)
    recvs = 10 + 2 * (nq - 1) + 2 * nq + (ns - 1) + ns
    vm = pltpu.VMEM
    in_hbm = pl.BlockSpec(memory_space=pltpu.HBM)
    here = pl.BlockSpec(memory_space=pltpu.VMEM)
    wide = vm((M, 2 * R), f32)
    thin = vm((hb, 2 * R), f32)
    sub, tile = pl.pallas_call(
        functools.partial(body, nq, ns),
        out_shape=(
            jax.ShapeDtypeStruct((1, qrows, M), f32),
            jax.ShapeDtypeStruct((M + 8, M), f32),
        ),
        in_specs=[in_hbm] * 4 + [pl.BlockSpec(memory_space=pltpu.SMEM)],
        out_specs=(here, here),
        scratch_shapes=[
            vm((2, B, B), bf16), vm((B, B), f32), vm((R, R), f32), vm((B, M), bf16),
            vm((B, B), bf16), vm((B, B), bf16),
            vm((2, R + M, 2 * R), f32), vm((2, 3, R, 2 * R), f32),
            thin, thin, thin, thin, wide, thin,
            wide, wide, thin, thin, wide, wide, thin, thin,
            vm((B, M), f32), vm((nq - 1, B - R, M), f32),
            vm((2 * R, B - R), f32), vm((nq - 1, 2 * R, B - R), f32),
            vm((2 * nq * R, B - R), bf16), vm((2 * nq * R, B - R), bf16),
            vm((2, hb, 3 * R), f32), vm((nq, M, 3 * R), f32), vm((qrows, M), f32),
            vm((ns, ch + 8, M), f32), vm((ns - 1, ch + 8, M), f32), vm((ns, ch + 8, M), f32),
            pltpu.SemaphoreType.DMA((7,)),
            pltpu.SemaphoreType.DMA((sends,)),
            pltpu.SemaphoreType.DMA((recvs,)),
            pltpu.SemaphoreType.DMA((ns * nq,)),
        ],
        compiler_params=pltpu.CompilerParams(
            collective_id=0, has_side_effects=True, vmem_limit_bytes=VMEM_BYTES
        ),
    )(factors, onsite, coupling, vectors, quad_weight)
    return pl.pallas_call(
        unpack,
        out_shape=(
            jax.ShapeDtypeStruct((1, qrows, M), f32),
            jax.ShapeDtypeStruct((M, M), f32),
            jax.ShapeDtypeStruct((M, M), f32),
        ),
        in_specs=[here, here],
        out_specs=(here, here, here),
        compiler_params=pltpu.CompilerParams(vmem_limit_bytes=VMEM_BYTES),
    )(sub, tile)


def solution(mesh):
    placed = (
        P("quad", "slab", None, None, None),
        P("slab", None, None),
        P("slab", None, None),
        P("slab", None, None),
        P("quad", None),
    )
    return jax.shard_map(
        functools.partial(per_device, mesh.shape["quad"], mesh.shape["slab"]),
        mesh=mesh,
        in_specs=placed,
        out_specs=(P("slab", "quad", None), P(), P()),
        check_vma=False,
    )
```
